32 devices in a mesh: wide: 8 (over y, x, core), narrow: 4 (over z).
Axes of the slice: x: 2, y: 2, z: 4, core: 2. Of those that a mesh axis runs over, the one named last changes fastest.
Arguments:
- hidden_in: bfloat16 [2, 32, 512, 768], P(None, ('wide', 'narrow')), may hold values from -6 to 6
- cotangent: bfloat16 [2, 32, 512, 768], P(None, ('wide', 'narrow')), may hold values from -6 to 6
- seq_lengths: int32 [2, 32], P(None, ('wide', 'narrow')), may hold values from 64 to 512, as said below
- query_weight: bfloat16 [768, 768], P(('wide', 'narrow')), may hold values from -0.21875 to 0.21875
- query_bias: bfloat16 [768], P(('wide', 'narrow')), may hold values from -3 to 3
- key_weight: bfloat16 [768, 768], P(('wide', 'narrow')), may hold values from -0.21875 to 0.21875
- key_bias: bfloat16 [768], P(('wide', 'narrow')), may hold values from -3 to 3
- value_weight: bfloat16 [768, 768], P(('wide', 'narrow')), may hold values from -0.21875 to 0.21875
- value_bias: bfloat16 [768], P(('wide', 'narrow')), may hold values from -3 to 3
- out_weight: bfloat16 [768, 768], P(('wide', 'narrow')), may hold values from -0.875 to 0.875
- out_bias: bfloat16 [768], P(('wide', 'narrow')), may hold values from -3 to 3
- first_gain: bfloat16 [768], P(('wide', 'narrow')), may hold values from 0.5 to 1.5
- first_shift: bfloat16 [768], P(('wide', 'narrow')), may hold values from -3 to 3
- up_weight: bfloat16 [768, 3072], P(('wide', 'narrow')), may hold values from -0.21875 to 0.21875
- up_bias: bfloat16 [3072], P(('wide', 'narrow')), may hold values from -3 to 3
- down_weight: bfloat16 [3072, 768], P(('wide', 'narrow')), may hold values from -0.109375 to 0.109375
- down_bias: bfloat16 [768], P(('wide', 'narrow')), may hold values from -3 to 3
- second_gain: bfloat16 [768], P(('wide', 'narrow')), may hold values from 0.5 to 1.5
- second_shift: bfloat16 [768], P(('wide', 'narrow')), may hold values from -3 to 3
- rel_table: bfloat16 [512, 768], P(None, ('wide', 'narrow')), may hold values from -6 to 6
Outputs:
- hidden_out: bfloat16 [2, 32, 512, 768], P(None, ('wide', 'narrow'))
- grad_hidden_in: float32 [2, 32, 512, 768], P(None, ('wide', 'narrow'))
- grad_query_weight: float32 [768, 768], P(('wide', 'narrow'))
- grad_query_bias: float32 [768], P(('wide', 'narrow'))
- grad_key_weight: float32 [768, 768], P(('wide', 'narrow'))
- grad_key_bias: float32 [768], P(('wide', 'narrow'))
- grad_value_weight: float32 [768, 768], P(('wide', 'narrow'))
- grad_value_bias: float32 [768], P(('wide', 'narrow'))
- grad_out_weight: float32 [768, 768], P(('wide', 'narrow'))
- grad_out_bias: float32 [768], P(('wide', 'narrow'))
- grad_first_gain: float32 [768], P(('wide', 'narrow'))
- grad_first_shift: float32 [768], P(('wide', 'narrow'))
- grad_up_weight: float32 [768, 3072], P(('wide', 'narrow'))
- grad_up_bias: float32 [3072], P(('wide', 'narrow'))
- grad_down_weight: float32 [3072, 768], P(('wide', 'narrow'))
- grad_down_bias: float32 [768], P(('wide', 'narrow'))
- grad_second_gain: float32 [768], P(('wide', 'narrow'))
- grad_second_shift: float32 [768], P(('wide', 'narrow'))
- grad_rel_table: float32 [512, 768], P(None, ('wide', 'narrow'))
The draws below stay inside these ranges and needn't reach their ends.
Inputs may be any that keep to these rules, and one draw needn't show every extreme that they name: `seq_lengths`: each sequence's live length; key slots at or past it are padding.
All inputs are finite; a program needn't handle non-finite values.
Results may differ from the reference program's by a relative error of at most 0.04.
Values may be sent and summed in bfloat16 or wider, within the bound.
No kernel may reach another device: no remote copies, remote signals or barrier semaphores. Data moves between devices by JAX's collectives and lax.ppermute only.
A program may use at most 256 MiB of HBM per device.

```python
import math
import jax
import jax.numpy as jnp
from jax import lax

D = 768
HEADS = 12
HEAD = 64
FF = 3072
SPAN = 256
SEQ = 512
MICRO = 2
SEQS = 32


def draw_seq_lengths(key, part):
    base_key, power_key = jax.random.split(key)
    base_len = jax.random.randint(base_key, (MICRO, SEQS), SEQ // 8, SEQ // 4 + 1)
    power_exp = jax.random.randint(power_key, (MICRO, SEQS), 0, 4)
    return jnp.minimum(jnp.left_shift(base_len, power_exp), SEQ).astype(jnp.int32)


def block_levels(own_key, shape, cuts, least, largest):
    gain, own = 1.0, jax.random.fold_in(own_key, 6)
    for dim, parts in cuts:
        steps = jnp.exp(jax.random.uniform(jax.random.fold_in(own, dim), (parts,), jnp.float32, least / len(cuts), largest / len(cuts)))
        gain = gain * jnp.repeat(steps, shape[dim] // parts).reshape([-1 if axis == dim else 1 for axis in range(len(shape))])
    return gain


def scatter_about(own_key, shape, deviation, limit, cuts=(), kind=jnp.bfloat16):
    factor_of = block_levels(own_key, shape, cuts, -0.22, 0.18) if cuts else 1.0
    array = jax.random.normal(own_key, shape, jnp.float32) * deviation * factor_of
    return jnp.minimum(jnp.maximum(array, -limit), limit).astype(kind)


def setup_inputs(seed: int = 0) -> dict:
    seeds = jax.random.split(jax.random.key(seed), 21)
    hidden_in = scatter_about(seeds[0], (MICRO, SEQS, SEQ, D), 1.0, 6.0, ((1, 32),))
    cotangent = scatter_about(seeds[1], (MICRO, SEQS, SEQ, D), 1.0, 6.0, ((1, 32),))
    seq_lengths = draw_seq_lengths(jax.random.fold_in(seeds[20], 71), 0)
    query_weight = scatter_about(seeds[3], (D, D), D ** -0.5, 0.21875, ((0, 32),))
    query_bias = scatter_about(seeds[4], (D,), 0.5, 3.0, ((0, 32),))
    key_weight = scatter_about(seeds[5], (D, D), D ** -0.5, 0.21875, ((0, 32),))
    key_bias = scatter_about(seeds[6], (D,), 0.5, 3.0, ((0, 32),))
    value_weight = scatter_about(seeds[7], (D, D), D ** -0.5, 0.21875, ((0, 32),))
    value_bias = scatter_about(seeds[8], (D,), 0.5, 3.0, ((0, 32),))
    out_weight = scatter_about(seeds[9], (D, D), (D // 16) ** -0.5, 0.875, ((0, 32),))
    out_bias = scatter_about(seeds[10], (D,), 0.5, 3.0, ((0, 32),))
    first_gain = jnp.clip(1.0 + 0.1 * jax.random.normal(seeds[11], (D,), jnp.float32), 0.5, 1.5).astype(jnp.bfloat16)
    first_shift = scatter_about(seeds[12], (D,), 0.5, 3.0, ((0, 32),))
    up_weight = scatter_about(seeds[13], (D, FF), D ** -0.5, 0.21875, ((0, 32),))
    up_bias = scatter_about(seeds[14], (FF,), 0.5, 3.0, ((0, 32),))
    down_weight = scatter_about(seeds[15], (FF, D), FF ** -0.5, 0.109375, ((0, 32),))
    down_bias = scatter_about(seeds[16], (D,), 0.5, 3.0, ((0, 32),))
    second_gain = jnp.clip(1.0 + 0.1 * jax.random.normal(seeds[17], (D,), jnp.float32), 0.5, 1.5).astype(jnp.bfloat16)
    second_shift = scatter_about(seeds[18], (D,), 0.5, 3.0, ((0, 32),))
    rel_table = scatter_about(seeds[19], (2 * SPAN, D), 1.0, 6.0, ((1, 32),))
    return dict(hidden_in=hidden_in, cotangent=cotangent, seq_lengths=seq_lengths, query_weight=query_weight, query_bias=query_bias, key_weight=key_weight, key_bias=key_bias, value_weight=value_weight, value_bias=value_bias, out_weight=out_weight, out_bias=out_bias, first_gain=first_gain, first_shift=first_shift, up_weight=up_weight, up_bias=up_bias, down_weight=down_weight, down_bias=down_bias, second_gain=second_gain, second_shift=second_shift, rel_table=rel_table)


@jax.custom_vjp
def low(v):
    return lax.optimization_barrier(v.astype(jnp.bfloat16)).astype(jnp.float32)

@jax.custom_vjp
def low_back(v):
    return v

def low_keep(v):
    return (low(v), None)

def low_pass(kept, grad):
    return (grad,)

def back_keep(v):
    return (v, None)

def back_low(kept, grad):
    return (low(grad),)
low.defvjp(low_keep, low_pass)
low_back.defvjp(back_keep, back_low)
norm_epsilon = 1e-06
highest_precision = lax.Precision.HIGHEST
group_seqs = 8

def matmul(left, right):
    return jnp.matmul(left, right, precision=highest_precision)

def layer_norm(inputs, norm_gain, norm_shift):
    row_mean = lax.optimization_barrier(jnp.mean(inputs, axis=-1, keepdims=True))
    centered = inputs - row_mean
    variance = lax.optimization_barrier(jnp.mean(centered * centered, axis=-1, keepdims=True))
    return centered * lax.rsqrt(variance + norm_epsilon) * norm_gain + norm_shift

def offsets_table():
    places = jnp.arange(SEQ, dtype=jnp.int32)
    return jnp.clip(places[:, None] - places[None, :] + SPAN, 0, 2 * SPAN - 1).astype(jnp.int32)

def attend_one(queries, keys_in, values_in, length, rel_table, query_weight, query_bias, key_weight, key_bias):
    pos_key = low(low_back(matmul(rel_table, key_weight) + key_bias)).reshape(2 * SPAN, HEADS, HEAD)
    pos_query = low(low_back(matmul(rel_table, query_weight) + query_bias)).reshape(2 * SPAN, HEADS, HEAD)
    offsets = offsets_table()
    key_valid = jnp.arange(SEQ, dtype=jnp.int32) < length
    head_queries = queries.reshape(SEQ, HEADS, HEAD)
    head_keys = keys_in.reshape(SEQ, HEADS, HEAD)
    head_values = values_in.reshape(SEQ, HEADS, HEAD)
    content = jnp.einsum('ihe,jhe->hij', head_queries, head_keys, precision=highest_precision)
    query_to_pos = low_back(jnp.einsum('ihe,mhe->him', head_queries, pos_key, precision=highest_precision))
    key_to_pos = low_back(jnp.einsum('jhe,mhe->hjm', head_keys, pos_query, precision=highest_precision))
    index_query = jnp.broadcast_to(offsets[None], (HEADS, SEQ, SEQ))
    index_key = jnp.broadcast_to(offsets.T[None], (HEADS, SEQ, SEQ))
    content_pos = jnp.take_along_axis(query_to_pos, index_query, axis=2)
    pos_content = jnp.transpose(jnp.take_along_axis(key_to_pos, index_key, axis=2), (0, 2, 1))
    raw_scores = low_back(content + content_pos + pos_content)
    scores = jnp.where(key_valid[None, None, :], raw_scores * (1.0 / math.sqrt(3 * HEAD)), -1000000000.0)
    row_max = lax.optimization_barrier(jnp.max(scores, axis=2, keepdims=True))
    exp_scores = jnp.exp(scores - row_max)
    attn_probs = exp_scores / lax.optimization_barrier(jnp.sum(exp_scores, axis=2, keepdims=True))
    context = jnp.einsum('hij,jhe->ihe', low(attn_probs), head_values, precision=highest_precision)
    return low(low_back(context.reshape(SEQ, HEADS * HEAD)))

def block(params, inputs, lengths):
    query_weight, query_bias, key_weight, key_bias, value_weight, value_bias, out_weight, out_bias, first_gain, first_shift, up_weight, up_bias, down_weight, down_bias, second_gain, second_shift, rel_table = params
    queries = low(low_back(matmul(inputs, query_weight) + query_bias))
    keys_in = low(low_back(matmul(inputs, key_weight) + key_bias))
    values_in = low(low_back(matmul(inputs, value_weight) + value_bias))
    attend_saved = jax.checkpoint(attend_one)

    def per_sequence(seq_item):
        return attend_saved(seq_item[0], seq_item[1], seq_item[2], seq_item[3], rel_table, query_weight, query_bias, key_weight, key_bias)
    context = lax.map(per_sequence, (queries, keys_in, values_in, lengths))
    branch = low_back(matmul(context, out_weight) + out_bias)
    hidden = layer_norm(inputs + branch, first_gain, first_shift)
    upward = low_back(matmul(low(hidden), up_weight) + up_bias)
    activated = jax.nn.gelu(upward, approximate=False)
    feed_out = low_back(matmul(low(activated), down_weight) + down_bias)
    return layer_norm(hidden + feed_out, second_gain, second_shift)

def reference(hidden_in, cotangent, seq_lengths, query_weight, query_bias, key_weight, key_bias, value_weight, value_bias, out_weight, out_bias, first_gain, first_shift, up_weight, up_bias, down_weight, down_bias, second_gain, second_shift, rel_table):
    params = tuple((weight.astype(jnp.float32) for weight in (query_weight, query_bias, key_weight, key_bias, value_weight, value_bias, out_weight, out_bias, first_gain, first_shift, up_weight, up_bias, down_weight, down_bias, second_gain, second_shift, rel_table)))
    group_count = MICRO * SEQS // group_seqs
    inputs_all = hidden_in.astype(jnp.float32).reshape(group_count, group_seqs, SEQ, D)
    cot_all = cotangent.astype(jnp.float32).reshape(group_count, group_seqs, SEQ, D)
    lengths_all = seq_lengths.astype(jnp.int32).reshape(group_count, group_seqs)

    def one_group(totals, group_item):
        inputs, cot_group, lengths = group_item
        outputs, pullback = jax.vjp(lambda weights, activations: block(weights, activations, lengths), params, inputs)
        weight_grads, input_grad = pullback(cot_group)
        totals = tuple((total + grad for total, grad in zip(totals, weight_grads)))
        return (totals, (outputs.astype(jnp.bfloat16), input_grad))
    zero_grads = tuple((jnp.zeros_like(weight) for weight in params))
    totals, (outputs, input_grads) = lax.scan(one_group, zero_grads, (inputs_all, cot_all, lengths_all))
    return (outputs.reshape(MICRO, SEQS, SEQ, D), input_grads.reshape(MICRO, SEQS, SEQ, D), totals[0], totals[1], totals[2], totals[3], totals[4], totals[5], totals[6], totals[7], totals[8], totals[9], totals[10], totals[11], totals[12], totals[13], totals[14], totals[15], totals[16])
```

```python
import functools
import math

import jax
import jax.numpy as jnp
from jax import lax
from jax.experimental import pallas as pl
from jax.experimental.pallas import tpu as pltpu
from jax.sharding import PartitionSpec as P

D = 768
HEADS = 12
HEAD = 64
SEQ = 512
MICRO = 2
PAIR = 2 * HEAD
PAIRS = HEADS // 2
CHUNK = 128
VECTORS = 256
SCALE = 1.0 / math.sqrt(3 * HEAD)
AXES = ("wide", "narrow")
norm_epsilon = 1e-06
bf16 = jnp.bfloat16
f32 = jnp.float32


def dot_nt(left, right):
    return lax.dot_general(left, right, (((1,), (1,)), ((), ())), preferred_element_type=f32)


def dot_nn(left, right):
    return lax.dot_general(left, right, (((1,), (0,)), ((), ())), preferred_element_type=f32)


def dot_tn(left, right):
    return lax.dot_general(left, right, (((0,), (0,)), ((), ())), preferred_element_type=f32)


def reverse_rows(flip, block):
    half = SEQ // 2
    return jnp.concatenate(
        [dot_nn(flip, block[half:]).astype(bf16), dot_nn(flip, block[:half]).astype(bf16)], axis=0
    )


def flip_matrix():
    half = SEQ // 2
    rows = lax.broadcasted_iota(jnp.int32, (half, half), 0)
    cols = lax.broadcasted_iota(jnp.int32, (half, half), 1)
    return jnp.where(rows + cols == half - 1, 1.0, 0.0).astype(bf16)


def skew(rows, base):
    return pltpu.roll(rows, base % SEQ, 1, stride=1, stride_axis=0)


def attend_kernel(len_ref, q_ref, k_ref, v_ref, pq_ref, pk_ref, ctx_ref, probs_ref, back_ref):
    length = len_ref[pl.program_id(1)]
    flip = flip_matrix()
    lane_pair = lax.broadcasted_iota(jnp.int32, (1, PAIR), 1)
    rows = lax.broadcasted_iota(jnp.int32, (CHUNK, SEQ), 0)
    cols = lax.broadcasted_iota(jnp.int32, (CHUNK, SEQ), 1)
    eye = jnp.where(
        lax.broadcasted_iota(jnp.int32, (CHUNK, CHUNK), 0)
        == lax.broadcasted_iota(jnp.int32, (CHUNK, CHUNK), 1),
        1.0,
        0.0,
    ).astype(bf16)
    key_valid = cols[:1] < length
    q_all, k_all, v_all = q_ref[...], k_ref[...], v_ref[...]
    pq_all = pq_ref[...]
    pk_flipped = reverse_rows(flip, pk_ref[...])
    for head in range(2):
        mine = (lane_pair >= head * HEAD) & (lane_pair < (head + 1) * HEAD)
        q_head = jnp.where(mine, q_all, jnp.zeros_like(q_all))
        k_head = jnp.where(mine, k_all, jnp.zeros_like(k_all))
        for c in range(SEQ // CHUNK):
            part = slice(c * CHUNK, (c + 1) * CHUNK)
            table = dot_nt(k_head[part], pq_all).astype(bf16)
            moved = skew(table, c * CHUNK + 256)
            place = cols - rows - c * CHUNK + 256
            moved = jnp.where(place < 0, table[:, :1], moved)
            moved = jnp.where(place > SEQ - 1, table[:, SEQ - 1 :], moved)
            back_ref[part, :] = moved
        for c in range(SEQ // CHUNK):
            part = slice(c * CHUNK, (c + 1) * CHUNK)
            raw = dot_nt(
                jnp.concatenate([q_head[part], eye], axis=1),
                jnp.concatenate([k_all, back_ref[:, part]], axis=1),
            )
            table = dot_nt(q_head[part], pk_flipped).astype(bf16)
            moved = skew(table, c * CHUNK - 255)
            place = cols - rows - c * CHUNK + 255
            moved = jnp.where(place < 0, table[:, :1], moved)
            moved = jnp.where(place > SEQ - 1, table[:, SEQ - 1 :], moved)
            scores = jnp.where(key_valid, (raw + moved.astype(f32)) * SCALE, -1000000000.0)
            row_max = jnp.max(scores, axis=1, keepdims=True)
            exp_scores = jnp.exp(scores - row_max)
            row_total = jnp.sum(exp_scores, axis=1, keepdims=True)
            probs = (exp_scores * (1.0 / row_total)).astype(bf16)
            context = dot_nn(probs, v_all).astype(bf16)
            if head == 0:
                ctx_ref[part, :] = context
            else:
                ctx_ref[part, :] = jnp.where(mine, context, ctx_ref[part, :])
            half = SEQ // 2
            probs_ref[0, head, part, :half] = dot_nn(probs[:, half:], flip).astype(bf16)
            probs_ref[0, head, part, half:] = dot_nn(probs[:, :half], flip).astype(bf16)


def attend(lengths, qkv, pos):
    qkv_block = lambda which: pl.BlockSpec((SEQ, PAIR), lambda p, s, n: (s, which * PAIRS + p))
    pos_block = lambda which: pl.BlockSpec((SEQ, PAIR), lambda p, s, n: (0, which * PAIRS + p))
    return pl.pallas_call(
        attend_kernel,
        grid_spec=pltpu.PrefetchScalarGridSpec(
            num_scalar_prefetch=1,
            grid=(PAIRS, MICRO),
            in_specs=[qkv_block(0), qkv_block(1), qkv_block(2), pos_block(0), pos_block(1)],
            out_specs=[
                pl.BlockSpec((SEQ, PAIR), lambda p, s, n: (s, p)),
                pl.BlockSpec((1, 2, SEQ, SEQ), lambda p, s, n: (s, p, 0, 0)),
            ],
            scratch_shapes=[pltpu.VMEM((SEQ, SEQ), bf16)],
        ),
        out_shape=[
            jax.ShapeDtypeStruct((MICRO * SEQ, D), bf16),
            jax.ShapeDtypeStruct((MICRO, HEADS, SEQ, SEQ), bf16),
        ],
        compiler_params=pltpu.CompilerParams(vmem_limit_bytes=40 * 2**20),
        cost_estimate=pl.CostEstimate(
            flops=24 * 8 * 2 * SEQ * SEQ * PAIR,
            bytes_accessed=20 * 2**20,
            transcendentals=24 * SEQ * SEQ,
        ),
        name="attend",
    )(lengths, qkv, qkv, qkv, pos, pos)


def fold_edges(moved, c, rows, cols):
    first = c * CHUNK
    place = rows + first
    inside = (cols >= place - 255) & (cols <= place + 256)
    kept = jnp.where(inside, moved, jnp.zeros_like(moved))
    outside = jnp.where(inside, jnp.zeros_like(moved), moved)
    half = SEQ // 2
    region = outside[:, half:] if first < half else outside[:, :half]
    edge_sum = jnp.sum(region.astype(f32), axis=1, keepdims=True)
    edge = 0 if first < half else SEQ - 1
    return jnp.where(cols == edge, kept.astype(f32) + edge_sum, kept.astype(f32)).astype(bf16)


def attend_back_kernel(
    q_ref, k_ref, v_ref, pq_ref, pk_ref, gc_ref, probs_ref,
    gq_ref, gk_ref, gv_ref, gpq_ref, gpk_ref,
    raw_ref, moved_ref, turned_ref, turned_moved_ref,
):
    flip = flip_matrix()
    lane_pair = lax.broadcasted_iota(jnp.int32, (1, PAIR), 1)
    rows = lax.broadcasted_iota(jnp.int32, (CHUNK, SEQ), 0)
    cols = lax.broadcasted_iota(jnp.int32, (CHUNK, SEQ), 1)
    q_all = q_ref[...]
    pq_all, pk_all = pq_ref[...], pk_ref[...]
    gc_all = gc_ref[...]
    k_flipped = reverse_rows(flip, k_ref[...])
    v_flipped = reverse_rows(flip, v_ref[...])
    both = lambda: jnp.zeros((SEQ, PAIR), bf16)
    gk_pair = gv_pair = gpq_pair = gpk_pair = None
    for head in range(2):
        mine = (lane_pair >= head * HEAD) & (lane_pair < (head + 1) * HEAD)
        gc_head = jnp.where(mine, gc_all, jnp.zeros_like(gc_all))
        for c in range(SEQ // CHUNK):
            part = slice(c * CHUNK, (c + 1) * CHUNK)
            probs = probs_ref[0, head, part, :].astype(f32)
            grad_probs = dot_nt(gc_head[part], v_flipped)
            inner = jnp.sum(probs * grad_probs, axis=1, keepdims=True)
            grad_raw = (probs * (grad_probs - inner) * SCALE).astype(bf16)
            raw_ref[part, :] = grad_raw
            moved_ref[part, :] = fold_edges(skew(grad_raw, c * CHUNK - 255), c, rows, cols)
            gq = (dot_nn(grad_raw, k_flipped) + dot_nn(moved_ref[part, :], pk_all)).astype(bf16)
            if head == 0:
                gq_ref[part, :] = gq
            else:
                gq_ref[part, :] = jnp.where(mine, gq, gq_ref[part, :])
        gk_parts = []
        for c in range(SEQ // CHUNK):
            part = slice(c * CHUNK, (c + 1) * CHUNK)
            turned = raw_ref[:, part].T
            turned_moved = fold_edges(skew(turned, c * CHUNK - 255), c, rows, cols)
            turned_moved_ref[part, :] = turned_moved
            gk_parts.append(
                (dot_nn(turned, q_all) + dot_nn(turned_moved, pq_all)).astype(bf16)
            )
        gk = jnp.concatenate(gk_parts, axis=0)
        gv = dot_tn(gc_all, probs_ref[0, head]).T.astype(bf16)
        gpk = dot_tn(q_all, moved_ref[...]).T
        gpq = dot_tn(k_flipped, turned_moved_ref[...]).T
        if head == 0:
            gk_pair, gv_pair, gpk_pair, gpq_pair = gk, gv, gpk, gpq
        else:
            gk_pair = jnp.where(mine, gk, gk_pair)
            gv_pair = jnp.where(mine, gv, gv_pair)
            gpk_pair = jnp.where(mine, gpk, gpk_pair)
            gpq_pair = jnp.where(mine, gpq, gpq_pair)
    gk_ref[...] = reverse_rows(flip, gk_pair)
    gv_ref[...] = reverse_rows(flip, gv_pair)

    @pl.when(pl.program_id(1) == 0)
    def first():
        gpk_ref[...] = gpk_pair
        gpq_ref[...] = gpq_pair

    @pl.when(pl.program_id(1) != 0)
    def later():
        gpk_ref[...] += gpk_pair
        gpq_ref[...] += gpq_pair


def attend_back(qkv, pos, grad_context, probs):
    qkv_block = lambda which: pl.BlockSpec((SEQ, PAIR), lambda p, s: (s, which * PAIRS + p))
    pos_block = lambda which: pl.BlockSpec((SEQ, PAIR), lambda p, s: (0, which * PAIRS + p))
    token_block = pl.BlockSpec((SEQ, PAIR), lambda p, s: (s, p))
    table_block = pl.BlockSpec((SEQ, PAIR), lambda p, s: (0, p))
    token_shape = jax.ShapeDtypeStruct((MICRO * SEQ, D), bf16)
    table_shape = jax.ShapeDtypeStruct((SEQ, D), f32)
    return pl.pallas_call(
        attend_back_kernel,
        grid=(PAIRS, MICRO),
        in_specs=[
            qkv_block(0), qkv_block(1), qkv_block(2), pos_block(0), pos_block(1), token_block,
            pl.BlockSpec((1, 2, SEQ, SEQ), lambda p, s: (s, p, 0, 0)),
        ],
        out_specs=[token_block, token_block, token_block, table_block, table_block],
        out_shape=[token_shape, token_shape, token_shape, table_shape, table_shape],
        scratch_shapes=[pltpu.VMEM((SEQ, SEQ), bf16)] * 4,
        compiler_params=pltpu.CompilerParams(vmem_limit_bytes=40 * 2**20),
        cost_estimate=pl.CostEstimate(
            flops=24 * 16 * 2 * SEQ * SEQ * PAIR, bytes_accessed=24 * 2**20, transcendentals=0
        ),
        name="attend_back",
    )(qkv, qkv, qkv, pos, pos, grad_context, probs)


def normalise(v):
    row_mean = jnp.mean(v, axis=-1, keepdims=True)
    centered = v - row_mean
    variance = jnp.mean(centered * centered, axis=-1, keepdims=True)
    rstd = lax.rsqrt(variance + norm_epsilon)
    return centered * rstd, rstd


def norm_back(normed, rstd, gain, grad):
    e = grad * gain
    grad_in = rstd * (
        e
        - jnp.mean(e, axis=-1, keepdims=True)
        - normed * jnp.mean(e * normed, axis=-1, keepdims=True)
    )
    return grad_in, jnp.sum(grad * normed, axis=0), jnp.sum(grad, axis=0)


def narrow_shifts(block, shift):
    size = lax.axis_size("narrow")
    return lax.ppermute(block, "narrow", [(i, (i + shift) % size) for i in range(size)])


def gather_rows(shard):
    size = lax.axis_size("narrow")
    me = lax.axis_index("narrow")
    rows, cols = shard.shape
    together = jnp.zeros((size * rows, cols), shard.dtype)
    for shift in range(size):
        block = narrow_shifts(shard, shift) if shift else shard
        owner = lax.rem(me - shift + size, size)
        together = lax.dynamic_update_slice(together, block, (owner * rows, 0))
    return lax.all_gather(together, "wide", axis=0, tiled=True)


def scatter_wide(full):
    return lax.psum_scatter(full, "wide", scatter_dimension=0, tiled=True)


def scatter_narrow(part):
    size = lax.axis_size("narrow")
    me = lax.axis_index("narrow")
    rows = part.shape[0] // size
    total = None
    for shift in range(size):
        target = lax.rem(me + shift, size)
        block = lax.dynamic_slice_in_dim(part, target * rows, rows, 0)
        block = (narrow_shifts(block, shift) if shift else block).astype(f32)
        total = block if total is None else total + block
    return total


def body(
    hidden_in, cotangent, seq_lengths,
    query_weight, query_bias, key_weight, key_bias, value_weight, value_bias,
    out_weight, out_bias, first_gain, first_shift, up_weight, up_bias,
    down_weight, down_bias, second_gain, second_shift, rel_table,
):
    tokens = MICRO * SEQ
    x = hidden_in.reshape(tokens, D)
    cot = cotangent.reshape(tokens, D).astype(f32)
    lengths = seq_lengths.reshape(MICRO)
    share = query_weight.shape[0]
    vectors = [
        query_bias, key_bias, value_bias, out_bias, first_gain, first_shift,
        down_bias, second_gain, second_shift,
    ]
    vectors = jnp.concatenate([jnp.stack(vectors), up_bias.reshape(4, share)], axis=0)
    vectors = jnp.pad(vectors, ((0, VECTORS - vectors.shape[0]), (0, 0)))
    first_pack = gather_rows(
        jnp.concatenate(
            [
                query_weight, key_weight, value_weight,
                jnp.concatenate([rel_table, vectors], axis=0).T,
            ],
            axis=1,
        )
    )
    second_pack = gather_rows(jnp.concatenate([out_weight, up_weight], axis=1))
    down_full = gather_rows(down_weight)
    qkv_weight = first_pack[:, : 3 * D]
    rel_turned = first_pack[:, 3 * D : 3 * D + SEQ]
    out_full = second_pack[:, :D]
    up_full = second_pack[:, D:]
    vector_rows = first_pack[:, 3 * D + SEQ :].T.astype(f32)
    qkv_bias = vector_rows[:3].reshape(3 * D)
    out_b, gain_1, shift_1, down_b, gain_2, shift_2 = (vector_rows[i] for i in range(3, 9))
    up_b = jnp.transpose(vector_rows[9:13].reshape(4, D // share, share), (1, 0, 2)).reshape(4 * D)

    qkv = (dot_nn(x, qkv_weight) + qkv_bias).astype(bf16)
    pos = (dot_tn(rel_turned, qkv_weight[:, : 2 * D]) + qkv_bias[: 2 * D]).astype(bf16)
    context, probs = attend(lengths, qkv, pos)

    first_in = x.astype(f32) + dot_nn(context, out_full) + out_b
    normed_1, rstd_1 = normalise(first_in)
    hidden = normed_1 * gain_1 + shift_1
    hidden_low = hidden.astype(bf16)
    upward = dot_nn(hidden_low, up_full) + up_b
    cdf = 0.5 * (1.0 + lax.erf(upward * math.sqrt(0.5)))
    activated_low = (upward * cdf).astype(bf16)
    slope = (cdf + upward * jnp.exp(-0.5 * upward * upward) * (1 / math.sqrt(2 * math.pi))).astype(
        bf16
    )
    second_in = hidden + dot_nn(activated_low, down_full) + down_b
    normed_2, rstd_2 = normalise(second_in)
    hidden_out = (normed_2 * gain_2 + shift_2).astype(bf16)

    grad_second, grad_gain_2, grad_shift_2 = norm_back(normed_2, rstd_2, gain_2, cot)
    grad_feed = grad_second.astype(bf16)
    grad_down_bias = jnp.sum(grad_feed.astype(f32), axis=0)
    grad_down = dot_tn(activated_low, grad_feed).astype(bf16)
    grad_up = (dot_nt(grad_feed, down_full) * slope.astype(f32)).astype(bf16)
    grad_up_bias = jnp.sum(grad_up.astype(f32), axis=0)
    grad_up_weight = dot_tn(hidden_low, grad_up).astype(bf16)
    grad_hidden = grad_second + dot_nt(grad_up, up_full)
    grad_first, grad_gain_1, grad_shift_1 = norm_back(normed_1, rstd_1, gain_1, grad_hidden)
    grad_branch = grad_first.astype(bf16)
    grad_out_bias = jnp.sum(grad_branch.astype(f32), axis=0)
    grad_out = dot_tn(context, grad_branch).astype(bf16)
    grad_context = dot_nt(grad_branch, out_full).astype(bf16)

    grad_second_pack = jnp.concatenate([grad_out, grad_up_weight], axis=1)
    down_part = scatter_wide(grad_down)
    grad_context, grad_second_pack, down_part = lax.optimization_barrier(
        (grad_context, grad_second_pack, down_part)
    )
    second_part = scatter_wide(grad_second_pack)

    gq, gk, gv, gpq, gpk = attend_back(qkv, pos, grad_context, probs)
    gpos = jnp.concatenate([gpq, gpk], axis=1).astype(bf16)
    gqkv = jnp.concatenate([gq, gk, gv], axis=1)
    grad_inputs = grad_first + dot_nt(gqkv, qkv_weight)
    grad_qkv = dot_tn(x, gqkv)
    grad_pos_weight = dot_nn(rel_turned, gpos)
    grad_qkv = jnp.concatenate(
        [grad_qkv[:, : 2 * D] + grad_pos_weight, grad_qkv[:, 2 * D :]], axis=1
    )
    qkv_bias_grad = jnp.sum(gqkv.astype(f32), axis=0)
    pos_bias_grad = jnp.sum(gpos.astype(f32), axis=0)
    grad_rel_turned = dot_nt(qkv_weight[:, : 2 * D], gpos)
    vector_grads = [
        qkv_bias_grad[:D] + pos_bias_grad[:D],
        qkv_bias_grad[D : 2 * D] + pos_bias_grad[D:],
        qkv_bias_grad[2 * D :],
        grad_out_bias, grad_gain_1, grad_shift_1, grad_down_bias, grad_gain_2, grad_shift_2,
    ]
    grad_up_bias = jnp.transpose(grad_up_bias.reshape(D // share, 4, share), (1, 0, 2))
    vector_grads = jnp.concatenate(
        [
            jnp.stack(vector_grads),
            grad_up_bias.reshape(4, D),
            jnp.zeros((VECTORS - 13, D), f32),
        ],
        axis=0,
    )
    vector_grads = lax.optimization_barrier(vector_grads.T.astype(bf16))
    last_pack = jnp.concatenate(
        [grad_qkv.astype(bf16), grad_rel_turned.astype(bf16), vector_grads], axis=1
    )
    last_pack, second_part = lax.optimization_barrier((last_pack, second_part))
    last_sum = scatter_narrow(scatter_wide(last_pack))
    down_sum = scatter_narrow(down_part)
    second_sum = scatter_narrow(second_part)
    turned = last_sum[:, 3 * D :].T
    vec = lambda i: turned[SEQ + i]
    return (
        hidden_out.reshape(hidden_in.shape),
        grad_inputs.reshape(hidden_in.shape),
        last_sum[:, :D], vec(0),
        last_sum[:, D : 2 * D], vec(1),
        last_sum[:, 2 * D : 3 * D], vec(2),
        second_sum[:, :D], vec(3), vec(4), vec(5),
        second_sum[:, D:],
        turned[SEQ + 9 : SEQ + 13].reshape(4 * share),
        down_sum, vec(6), vec(7), vec(8),
        turned[:SEQ],
    )


def solution(mesh):
    tokens = P(None, AXES, None, None)
    rows = P(AXES, None)
    vector = P(AXES)
    weights = (
        rows, vector, rows, vector, rows, vector, rows, vector, vector, vector,
        rows, vector, rows, vector, vector, vector, P(None, AXES),
    )
    return jax.shard_map(
        body,
        mesh=mesh,
        in_specs=(tokens, tokens, P(None, AXES)) + weights,
        out_specs=(tokens, tokens) + weights,
        check_vma=False,
    )
```

```python
import functools
import math

import jax
import jax.numpy as jnp
from jax import lax
from jax.experimental import pallas as pl
from jax.experimental.pallas import tpu as pltpu
from jax.sharding import PartitionSpec as P

D = 768
HEADS = 12
HEAD = 64
SEQ = 512
MICRO = 2
PAIR = 2 * HEAD
PAIRS = HEADS // 2
CHUNK = 128
ROWS = 32
DELAYS = (0, 1)
LOG2E = 1.4426950408889634
VECTORS = 256
SCALE = 1.0 / math.sqrt(3 * HEAD)
AXES = ("wide", "narrow")
norm_epsilon = 1e-06
bf16 = jnp.bfloat16
f32 = jnp.float32


def dot_nt(left, right):
    return lax.dot_general(left, right, (((1,), (1,)), ((), ())), preferred_element_type=f32)


def dot_nn(left, right):
    return lax.dot_general(left, right, (((1,), (0,)), ((), ())), preferred_element_type=f32)


def dot_tn(left, right):
    return lax.dot_general(left, right, (((0,), (0,)), ((), ())), preferred_element_type=f32)


def reverse_rows(flip, block):
    half = SEQ // 2
    return jnp.concatenate(
        [dot_nn(flip, block[half:]).astype(bf16), dot_nn(flip, block[:half]).astype(bf16)], axis=0
    )


def flip_matrix():
    half = SEQ // 2
    rows = lax.broadcasted_iota(jnp.int32, (half, half), 0)
    cols = lax.broadcasted_iota(jnp.int32, (half, half), 1)
    return jnp.where(rows + cols == half - 1, 1.0, 0.0).astype(bf16)


def skew(rows, base):
    return pltpu.roll(rows, base % SEQ, 1, stride=1, stride_axis=0)


def lane_tiles(block):
    return [block[:, t * CHUNK : (t + 1) * CHUNK] for t in range(SEQ // CHUNK)]


def clip_edges(moved, table, c, below):
    tiles = lane_tiles(moved)
    left = jnp.broadcast_to(table[:, :1], (CHUNK, CHUNK))
    right = jnp.broadcast_to(table[:, SEQ - 1 :], (CHUNK, CHUNK))
    if c == 0:
        tiles[2], tiles[3] = jnp.where(below, tiles[2], right), right
    elif c == 1:
        tiles[3] = jnp.where(below, tiles[3], right)
    elif c == 2:
        tiles[0] = jnp.where(below, left, tiles[0])
    else:
        tiles[0], tiles[1] = left, jnp.where(below, left, tiles[1])
    return jnp.concatenate(tiles, axis=1)


def fold_edges(moved, c, below):
    tiles = lane_tiles(moved)
    part = (2, 3, 0, 1)[c]
    zero = jnp.zeros_like(tiles[part])
    upper = c < 2
    if upper:
        outside, tiles[part] = jnp.where(below, zero, tiles[part]), jnp.where(below, tiles[part], zero)
    else:
        outside, tiles[part] = jnp.where(below, tiles[part], zero), jnp.where(below, zero, tiles[part])
    outside = [outside]
    if c in (0, 3):
        whole = 3 if c == 0 else 0
        outside.append(tiles[whole])
        tiles[whole] = zero
    edge, lane = (0, 0) if upper else (3, CHUNK - 1)
    outside = jnp.concatenate(outside, axis=1)
    lanes = lax.broadcasted_iota(jnp.int32, (outside.shape[1], CHUNK), 1)
    to_lane = jnp.where(lanes == lane, 1.0, 0.0).astype(bf16)
    tiles[edge] = tiles[edge] + dot_nn(outside, to_lane).astype(bf16)
    return jnp.concatenate(tiles, axis=1)


def weave(first, second):
    waiting = {0: [], 1: []}

    def emit(which, piece):
        store = piece() if piece is not None else None
        if store is not None:
            waiting[which].append(store)
        keep = DELAYS[which] if piece is not None else 0
        while len(waiting[which]) > keep:
            waiting[which].pop(0)()

    total = max(len(first), len(second))
    done = [0, 0]
    for step in range(1, total + 1):
        for which, pieces in ((1, second), (0, first)):
            while done[which] * total < step * len(pieces):
                emit(which, pieces[done[which]])
                done[which] += 1
    for which in (1, 0):
        emit(which, None)


def storing(ref, where, value):
    def store():
        ref[where] = value

    return store


def attend_kernel(
    len_ref, q_ref, k_ref, v_ref, pq_ref, pk_ref, ctx_ref, wide_ref, probs_ref, scale_ref,
    kp_a, kp_b, qp_a, qp_b, raw_a, raw_b, back_a, back_b, low_a, low_b,
):
    kp, qp, raw, back, low = (kp_a, kp_b), (qp_a, qp_b), (raw_a, raw_b), (back_a, back_b), (low_a, low_b)
    flip = flip_matrix()
    half = SEQ // 2
    lane_pair = lax.broadcasted_iota(jnp.int32, (1, PAIR), 1)
    rows = lax.broadcasted_iota(jnp.int32, (CHUNK, CHUNK), 0)
    cols = lax.broadcasted_iota(jnp.int32, (CHUNK, CHUNK), 1)
    strictly_below, below = cols < rows, cols <= rows
    places = lax.broadcasted_iota(jnp.int32, (1, SEQ), 1)
    pq_all = pq_ref[...]
    pk_flipped = reverse_rows(flip, pk_ref[...])
    units = [(seq, head) for seq in range(MICRO) for head in range(2)]
    heads = [
        (lane_pair >= head * HEAD) & (lane_pair < (head + 1) * HEAD) for head in range(2)
    ]
    hidden_keys = [jnp.where(places < len_ref[seq], 0.0, -1e30) for seq in range(MICRO)]

    def products(u):
        seq, head = units[u]
        slot = u % 2
        tokens = slice(seq * SEQ, (seq + 1) * SEQ)
        pieces = []
        for part in (slice(0, half), slice(half, SEQ)):
            def key_places(part=part):
                k_all = k_ref[tokens, :]
                k_head = jnp.where(heads[head], k_all, jnp.zeros_like(k_all))
                return storing(kp[slot], (slice(None), part), dot_nt(k_head, pq_all[part]).astype(bf16))

            def query_places(part=part):
                q_all = q_ref[tokens, :]
                q_head = jnp.where(heads[head], q_all, jnp.zeros_like(q_all))
                return storing(qp[slot], (slice(None), part), dot_nt(q_head, pk_flipped[part]).astype(bf16))

            def content(part=part):
                q_all = q_ref[tokens, :]
                q_head = jnp.where(heads[head], q_all, jnp.zeros_like(q_all))
                keys = slice(seq * SEQ + part.start, seq * SEQ + part.stop)
                return storing(raw[slot], (slice(None), part), dot_nt(q_head, k_ref[keys, :]))

            pieces += [key_places, query_places, content]
        return pieces

    def softmax(u):
        seq, head = units[u]
        slot = u % 2
        pieces = []
        for c in range(SEQ // CHUNK):
            def turn(c=c):
                part = slice(c * CHUNK, (c + 1) * CHUNK)
                table = kp[slot][part, :]
                moved = clip_edges(skew(table, c * CHUNK + 256), table, c, strictly_below)
                return storing(back[slot], (slice(None), part), moved.T)

            pieces.append(turn)
        for c in range(SEQ // CHUNK):
            def shift(c=c):
                part = slice(c * CHUNK, (c + 1) * CHUNK)
                table = qp[slot][part, :]
                return storing(
                    qp[slot], (part, slice(None)),
                    clip_edges(skew(table, c * CHUNK - 255), table, c, below),
                )

            pieces.append(shift)
        pieces.append(None)

        def normal(here):
            scores = (
                raw[slot][here, :]
                + (qp[slot][here, :].astype(f32) + back[slot][here, :].astype(f32))
                + hidden_keys[seq]
            )
            row_max = jnp.max(scores, axis=1, keepdims=True)
            exp_scores = jnp.exp2((scores - row_max) * (SCALE * LOG2E))
            return storing(low[slot], (here, slice(None)), exp_scores.astype(bf16))

        for start in range(0, SEQ, ROWS):
            pieces.append(functools.partial(normal, slice(start, start + ROWS)))
        return pieces

    def results(u):
        seq, head = units[u]
        slot = u % 2
        tokens = slice(seq * SEQ, (seq + 1) * SEQ)

        def context():
            v_all = v_ref[tokens, :]
            both = dot_nn(low[slot][...], jnp.concatenate([v_all, jnp.ones_like(v_all)], axis=1))
            scale = 1.0 / both[:, PAIR:]
            scale_ref[seq, head] = scale
            ctx = both[:, :PAIR] * scale
            if head == 1:
                ctx = jnp.where(heads[head], ctx, wide_ref[tokens, :])
                ctx_ref[tokens, :] = ctx.astype(bf16)
            wide_ref[tokens, :] = ctx

        def left():
            probs_ref[seq, head, :, :half] = dot_nn(low[slot][:, half:], flip).astype(bf16)

        def right():
            probs_ref[seq, head, :, half:] = dot_nn(low[slot][:, :half], flip).astype(bf16)

        return [context, left, right]

    count = len(units)
    for step in range(count + 2):
        matrix = products(step) if step < count else []
        if step >= 2:
            matrix = results(step - 2) + matrix
        vector = softmax(step - 1) if 1 <= step <= count else []
        weave(matrix, vector)


def attend(lengths, qkv, pos):
    qkv_block = lambda which: pl.BlockSpec((MICRO * SEQ, PAIR), lambda p, n: (0, which * PAIRS + p))
    pos_block = lambda which: pl.BlockSpec((SEQ, PAIR), lambda p, n: (0, which * PAIRS + p))
    square = lambda kind: [pltpu.VMEM((SEQ, SEQ), kind)] * 2
    return pl.pallas_call(
        attend_kernel,
        grid_spec=pltpu.PrefetchScalarGridSpec(
            num_scalar_prefetch=1,
            grid=(PAIRS,),
            in_specs=[qkv_block(0), qkv_block(1), qkv_block(2), pos_block(0), pos_block(1)],
            out_specs=[
                pl.BlockSpec((MICRO * SEQ, PAIR), lambda p, n: (0, p)),
                pl.BlockSpec((MICRO * SEQ, PAIR), lambda p, n: (0, p)),
                pl.BlockSpec((MICRO, 2, SEQ, SEQ), lambda p, n: (0, p, 0, 0)),
                pl.BlockSpec((MICRO, 2, SEQ, CHUNK), lambda p, n: (0, p, 0, 0)),
            ],
            scratch_shapes=square(bf16) + square(bf16) + square(f32) + square(bf16) + square(bf16),
        ),
        out_shape=[
            jax.ShapeDtypeStruct((MICRO * SEQ, D), bf16),
            jax.ShapeDtypeStruct((MICRO * SEQ, D), f32),
            jax.ShapeDtypeStruct((MICRO, HEADS, SEQ, SEQ), bf16),
            jax.ShapeDtypeStruct((MICRO, HEADS, SEQ, CHUNK), f32),
        ],
        compiler_params=pltpu.CompilerParams(vmem_limit_bytes=40 * 2**20),
        cost_estimate=pl.CostEstimate(
            flops=24 * 8 * 2 * SEQ * SEQ * PAIR,
            bytes_accessed=20 * 2**20,
            transcendentals=24 * SEQ * SEQ,
        ),
        name="attend",
    )(lengths, qkv, qkv, qkv, pos, pos)


def attend_back_kernel(
    q_ref, k_ref, v_ref, pq_ref, pk_ref, gc_ref, ctx_ref, probs_ref, scale_ref,
    gq_ref, gk_ref, gv_ref, gpq_ref, gpk_ref,
    raw_a, raw_b, grad_a, grad_b, moved_a, moved_b, turned_a, turned_b,
    inner_a, inner_b, q_t, k_t, gc_t, pq_t, pk_t, k_rev, v_rev, gq_t, gk_t, gv_t,
):
    raw, grad, moved, turned = (raw_a, raw_b), (grad_a, grad_b), (moved_a, moved_b), (turned_a, turned_b)
    inner = (inner_a, inner_b)
    flip = flip_matrix()
    half = SEQ // 2
    lane_pair = lax.broadcasted_iota(jnp.int32, (1, PAIR), 1)
    rows = lax.broadcasted_iota(jnp.int32, (CHUNK, CHUNK), 0)
    cols = lax.broadcasted_iota(jnp.int32, (CHUNK, CHUNK), 1)
    below = cols <= rows
    units = [(seq, head) for seq in range(MICRO) for head in range(2)]
    heads = [
        (lane_pair >= head * HEAD) & (lane_pair < (head + 1) * HEAD) for head in range(2)
    ]
    tokens = [slice(seq * SEQ, (seq + 1) * SEQ) for seq in range(MICRO)]
    pq_t[...] = pq_ref[...].T
    pk_t[...] = pk_ref[...].T

    def prepare(seq):
        v_rev[seq] = reverse_rows(flip, v_ref[tokens[seq], :])
        k_flipped = reverse_rows(flip, k_ref[tokens[seq], :])
        k_t[seq] = k_flipped.T
        q_t[seq] = q_ref[tokens[seq], :].T
        scale = jnp.where(heads[0], scale_ref[seq, 0], scale_ref[seq, 1])
        gc_t[seq] = (gc_ref[tokens[seq], :].astype(f32) * scale).astype(bf16).T

    def grads(u):
        seq, head = units[u]
        slot = u % 2
        pieces = []

        def start():
            if head == 0:
                prepare(seq)
            product = gc_ref[tokens[seq], :].astype(f32) * ctx_ref[tokens[seq], :]
            product = jnp.where(heads[head], product, 0.0)
            inner[slot][...] = jnp.broadcast_to(
                jnp.sum(product, axis=1, keepdims=True), (SEQ, CHUNK)
            )

        pieces.append(start)
        for part in (slice(0, half), slice(half, SEQ)):
            def values(part=part):
                gc_all = gc_ref[tokens[seq], :]
                gc_head = jnp.where(heads[head], gc_all, jnp.zeros_like(gc_all))
                return storing(raw[slot], (slice(None), part), dot_nt(gc_head, v_rev[seq, part, :]))

            pieces.append(values)
        pieces.append(None)
        for c in range(SEQ // CHUNK):
            for r in range(0, CHUNK, ROWS):
                def softmax(here=slice(c * CHUNK + r, c * CHUNK + r + ROWS)):
                    low, scale = inner[slot][here, :], scale_ref[seq, head, here, :]
                    tiles = [
                        (
                            probs_ref[seq, head, here, t : t + CHUNK].astype(f32)
                            * ((raw[slot][here, t : t + CHUNK] - low) * scale)
                        ).astype(bf16)
                        for t in range(0, SEQ, CHUNK)
                    ]
                    return storing(grad[slot], (here, slice(None)), jnp.concatenate(tiles, axis=1))

                pieces.append(softmax)
        pieces.append(None)

        def shift(c):
            part = slice(c * CHUNK, (c + 1) * CHUNK)
            table = fold_edges(skew(grad[slot][part, :], c * CHUNK - 255), c, below)
            return storing(moved[slot], (part, slice(None)), table)

        def turn(c):
            part = slice(c * CHUNK, (c + 1) * CHUNK)
            table = fold_edges(skew(grad[slot][:, part].T, c * CHUNK - 255), c, below)
            return storing(turned[slot], (part, slice(None)), table)

        for c in range(SEQ // CHUNK):
            pieces += [functools.partial(turn, c), functools.partial(shift, c)]
        return pieces

    def results(u):
        seq, head = units[u]
        slot = u % 2
        mine = slice(head * HEAD, (head + 1) * HEAD)

        def values():
            gv_t[seq, mine, :] = dot_nn(gc_t[seq, mine, :], probs_ref[seq, head]).astype(bf16)

        def keys():
            total = dot_nn(q_t[seq, mine, :], grad[slot][...])
            total = total + dot_nt(pq_t[mine, :], turned[slot][...])
            gk_t[seq, mine, :] = (total * SCALE).astype(bf16)

        def queries():
            total = dot_nt(k_t[seq, mine, :], grad[slot][...])
            total = total + dot_nt(pk_t[mine, :], moved[slot][...])
            gq_t[seq, mine, :] = (total * SCALE).astype(bf16)

        def key_places():
            total = dot_nn(q_t[seq, mine, :], moved[slot][...]) * SCALE
            gpk_ref[mine, :] = total if seq == 0 else gpk_ref[mine, :] + total

        def query_places():
            total = dot_nn(k_t[seq, mine, :], turned[slot][...]) * SCALE
            gpq_ref[mine, :] = total if seq == 0 else gpq_ref[mine, :] + total

        def finish():
            gq_ref[tokens[seq], :] = gq_t[seq].T
            for kept, out in ((gk_t, gk_ref), (gv_t, gv_ref)):
                out[tokens[seq], :] = jnp.concatenate(
                    [
                        dot_nn(kept[seq, :, half:], flip).astype(bf16),
                        dot_nn(kept[seq, :, :half], flip).astype(bf16),
                    ],
                    axis=1,
                ).T

        pieces = [values, keys, queries, key_places, query_places]
        return pieces + [finish] if head == 1 else pieces

    count = len(units)
    for step in range(count + 1):
        matrix = results(step - 1) if step >= 1 else []
        vector = grads(step) if step < count else []
        weave(matrix, vector)


def attend_back(qkv, pos, grad_context, context_wide, probs, scale):
    qkv_block = lambda which: pl.BlockSpec((MICRO * SEQ, PAIR), lambda p: (0, which * PAIRS + p))
    pos_block = lambda which: pl.BlockSpec((SEQ, PAIR), lambda p: (0, which * PAIRS + p))
    token_block = pl.BlockSpec((MICRO * SEQ, PAIR), lambda p: (0, p))
    table_block = pl.BlockSpec((PAIR, SEQ), lambda p: (p, 0))
    token_shape = jax.ShapeDtypeStruct((MICRO * SEQ, D), bf16)
    table_shape = jax.ShapeDtypeStruct((D, SEQ), f32)
    square = lambda kind: [pltpu.VMEM((SEQ, SEQ), kind)] * 2
    wide = pltpu.VMEM((MICRO, PAIR, SEQ), bf16)
    tall = pltpu.VMEM((MICRO, SEQ, PAIR), bf16)
    return pl.pallas_call(
        attend_back_kernel,
        grid=(PAIRS,),
        in_specs=[
            qkv_block(0), qkv_block(1), qkv_block(2), pos_block(0), pos_block(1),
            token_block, token_block,
            pl.BlockSpec((MICRO, 2, SEQ, SEQ), lambda p: (0, p, 0, 0)),
            pl.BlockSpec((MICRO, 2, SEQ, CHUNK), lambda p: (0, p, 0, 0)),
        ],
        out_specs=[token_block, token_block, token_block, table_block, table_block],
        out_shape=[token_shape, token_shape, token_shape, table_shape, table_shape],
        scratch_shapes=square(f32) + square(bf16) * 3
        + [pltpu.VMEM((SEQ, CHUNK), f32)] * 2
        + [wide, wide, wide, pltpu.VMEM((PAIR, SEQ), bf16), pltpu.VMEM((PAIR, SEQ), bf16)]
        + [tall, tall, wide, wide, wide],
        compiler_params=pltpu.CompilerParams(vmem_limit_bytes=40 * 2**20),
        cost_estimate=pl.CostEstimate(
            flops=24 * 16 * 2 * SEQ * SEQ * PAIR, bytes_accessed=24 * 2**20, transcendentals=0
        ),
        name="attend_back",
    )(qkv, qkv, qkv, pos, pos, grad_context, context_wide, probs, scale)


def weigh_kernel(
    x_ref, gq_ref, gk_ref, gv_ref, rel_ref, gpq_ref, gpk_ref, wq_ref, wk_ref, vec_ref,
    first_ref, second_ref, x_turned, rel_sum, rows_ref,
):
    step = pl.program_id(0)
    width = gq_ref.shape[1]

    @pl.when(step == 0)
    def begin():
        x_turned[...] = x_ref[...].T
        rel_sum[...] = jnp.zeros_like(rel_sum)
        rows_ref[...] = jnp.zeros_like(rows_ref)
        rows_ref[8:24, :] = vec_ref[...]

    token_ones = jnp.ones((8, MICRO * SEQ), bf16)
    place_ones = jnp.ones((8, SEQ), bf16)
    here = pl.ds(pl.multiple_of(step * width, width), width)
    row = lax.broadcasted_iota(jnp.int32, (8, width), 0)
    biases = jnp.zeros((8, width), f32)
    tables = ((gq_ref, gpq_ref, wq_ref), (gk_ref, gpk_ref, wk_ref))
    for which, (grad_ref, table_ref, weight_ref) in enumerate(tables):
        grad = grad_ref[...]
        table = table_ref[...].astype(bf16)
        total = dot_nn(x_turned[...], grad) + dot_nt(rel_ref[...], table)
        first_ref[:, pl.ds(pl.multiple_of(which * D + step * width, width), width)] = total.astype(bf16)
        rel_sum[...] += dot_nn(weight_ref[...], table)
        bias = dot_nn(token_ones, grad) + dot_nt(place_ones, table)
        biases = jnp.where(row == which, bias, biases)
    grad = gv_ref[...]
    second_ref[:, here] = dot_nn(x_turned[...], grad).astype(bf16)
    rows_ref[:8, here] = jnp.where(row == 2, dot_nn(token_ones, grad), biases)

    @pl.when(step == pl.num_programs(0) - 1)
    def end():
        second_ref[:, D : D + SEQ] = rel_sum[...].astype(bf16)
        second_ref[:, D + SEQ :] = rows_ref[...].T.astype(bf16)


def weigh(x, gq, gk, gv, rel_turned, gpq, gpk, qkv_weight, vectors):
    steps = 3
    width = D // steps
    whole = lambda shape: pl.BlockSpec(shape, lambda p: (0, 0))
    columns = lambda rows, which=0: pl.BlockSpec((rows, width), lambda p: (0, which * steps + p))
    tokens = MICRO * SEQ
    return pl.pallas_call(
        weigh_kernel,
        grid=(steps,),
        in_specs=[
            whole((tokens, D)), columns(tokens), columns(tokens), columns(tokens),
            whole((D, SEQ)),
            pl.BlockSpec((width, SEQ), lambda p: (p, 0)), pl.BlockSpec((width, SEQ), lambda p: (p, 0)),
            columns(D), columns(D, 1), whole((16, D)),
        ],
        out_specs=[whole((D, 2 * D)), whole((D, D + SEQ + CHUNK))],
        out_shape=[
            jax.ShapeDtypeStruct((D, 2 * D), bf16),
            jax.ShapeDtypeStruct((D, D + SEQ + CHUNK), bf16),
        ],
        scratch_shapes=[
            pltpu.VMEM((D, tokens), bf16), pltpu.VMEM((D, SEQ), f32), pltpu.VMEM((CHUNK, D), f32),
        ],
        compiler_params=pltpu.CompilerParams(vmem_limit_bytes=40 * 2**20),
        cost_estimate=pl.CostEstimate(
            flops=2 * D * D * (3 * tokens + 4 * SEQ), bytes_accessed=20 * 2**20, transcendentals=0
        ),
        name="weigh",
    )(x, gq, gk, gv, rel_turned, gpq, gpk, qkv_weight, qkv_weight, vectors)


def normalise(v):
    row_mean = jnp.mean(v, axis=-1, keepdims=True)
    centered = v - row_mean
    variance = jnp.mean(centered * centered, axis=-1, keepdims=True)
    rstd = lax.rsqrt(variance + norm_epsilon)
    return centered * rstd, rstd


def norm_back(normed, rstd, gain, grad):
    e = grad * gain
    grad_in = rstd * (
        e
        - jnp.mean(e, axis=-1, keepdims=True)
        - normed * jnp.mean(e * normed, axis=-1, keepdims=True)
    )
    return grad_in, jnp.sum(grad * normed, axis=0), jnp.sum(grad, axis=0)


def narrow_shifts(block, shift):
    size = lax.axis_size("narrow")
    return lax.ppermute(block, "narrow", [(i, (i + shift) % size) for i in range(size)])


def gather_rows(shard):
    size = lax.axis_size("narrow")
    me = lax.axis_index("narrow")
    rows, cols = shard.shape
    together = jnp.zeros((size * rows, cols), shard.dtype)
    for shift in range(size):
        block = narrow_shifts(shard, shift) if shift else shard
        owner = lax.rem(me - shift + size, size)
        together = lax.dynamic_update_slice(together, block, (owner * rows, 0))
    return lax.all_gather(together, "wide", axis=0, tiled=True)


def scatter_wide(full):
    return lax.psum_scatter(full, "wide", scatter_dimension=0, tiled=True)


def scatter_narrow_start(part):
    size = lax.axis_size("narrow")
    me = lax.axis_index("narrow")
    rows = part.shape[-2] // size
    pieces = []
    for shift in range(size):
        target = lax.rem(me + shift, size)
        block = lax.dynamic_slice_in_dim(part, target * rows, rows, part.ndim - 2)
        pieces.append(narrow_shifts(block, shift) if shift else block)
    return pieces


def scatter_narrow(part):
    return sum(piece.astype(f32) for piece in scatter_narrow_start(part))


def swap(block, bit):
    size = lax.axis_size("wide")
    return lax.ppermute(block, "wide", [(i, i ^ (1 << bit)) for i in range(size)])


def my_bit(bit):
    return lax.rem(lax.axis_index("wide") // (1 << bit), 2)


def wide_bits():
    return (lax.axis_size("wide") - 1).bit_length()


def split_bits(full):
    bits = wide_bits()
    return full.reshape((2,) * bits + (full.shape[0] >> bits, full.shape[1]))


def halve(part, bit, left):
    axis, mine = left.index(bit), my_bit(bit)
    keep = lax.dynamic_index_in_dim(part, mine, axis, keepdims=False)
    send = lax.dynamic_index_in_dim(part, 1 - mine, axis, keepdims=False)
    left.remove(bit)
    return (keep.astype(f32) + swap(send, bit).astype(f32)).astype(bf16)


def all_bits():
    return list(range(wide_bits()))[::-1]


def body(
    hidden_in, cotangent, seq_lengths,
    query_weight, query_bias, key_weight, key_bias, value_weight, value_bias,
    out_weight, out_bias, first_gain, first_shift, up_weight, up_bias,
    down_weight, down_bias, second_gain, second_shift, rel_table,
):
    tokens = MICRO * SEQ
    x = hidden_in.reshape(tokens, D)
    cot = cotangent.reshape(tokens, D).astype(f32)
    lengths = seq_lengths.reshape(MICRO)
    share = query_weight.shape[0]
    vectors = [
        query_bias, key_bias, value_bias, out_bias, first_gain, first_shift,
        down_bias, second_gain, second_shift,
    ]
    vectors = jnp.concatenate([jnp.stack(vectors), up_bias.reshape(4, share)], axis=0)
    vectors = jnp.pad(vectors, ((0, VECTORS - vectors.shape[0]), (0, 0)))
    first_pack = gather_rows(
        jnp.concatenate(
            [
                query_weight, key_weight, value_weight,
                jnp.concatenate([rel_table, vectors], axis=0).T,
            ],
            axis=1,
        )
    )
    second_pack = gather_rows(jnp.concatenate([out_weight, up_weight], axis=1))
    down_full = gather_rows(down_weight)
    qkv_weight = first_pack[:, : 3 * D]
    rel_turned = first_pack[:, 3 * D : 3 * D + SEQ]
    out_full = second_pack[:, :D]
    up_full = second_pack[:, D:]
    vector_rows = first_pack[:, 3 * D + SEQ :].T.astype(f32)
    qkv_bias = vector_rows[:3].reshape(3 * D)
    out_b, gain_1, shift_1, down_b, gain_2, shift_2 = (vector_rows[i] for i in range(3, 9))
    up_b = jnp.transpose(vector_rows[9:13].reshape(4, D // share, share), (1, 0, 2)).reshape(4 * D)

    qkv = (dot_nn(x, qkv_weight) + qkv_bias).astype(bf16)
    pos = (dot_tn(rel_turned, qkv_weight[:, : 2 * D]) + qkv_bias[: 2 * D]).astype(bf16)
    context, context_wide, probs, probs_scale = attend(lengths, qkv, pos)

    first_in = x.astype(f32) + dot_nn(context, out_full) + out_b
    normed_1, rstd_1 = normalise(first_in)
    hidden = normed_1 * gain_1 + shift_1
    hidden_low = hidden.astype(bf16)
    upward = dot_nn(hidden_low, up_full) + up_b
    cdf = 0.5 * (1.0 + lax.erf(upward * math.sqrt(0.5)))
    activated_low = (upward * cdf).astype(bf16)
    slope = (cdf + upward * jnp.exp(-0.5 * upward * upward) * (1 / math.sqrt(2 * math.pi))).astype(
        bf16
    )
    second_in = hidden + dot_nn(activated_low, down_full) + down_b
    normed_2, rstd_2 = normalise(second_in)
    hidden_out = (normed_2 * gain_2 + shift_2).astype(bf16)

    grad_second, grad_gain_2, grad_shift_2 = norm_back(normed_2, rstd_2, gain_2, cot)
    grad_feed = grad_second.astype(bf16)
    grad_down_bias = jnp.sum(grad_feed.astype(f32), axis=0)
    grad_down = dot_tn(activated_low, grad_feed).astype(bf16)
    grad_up = (dot_nt(grad_feed, down_full) * slope.astype(f32)).astype(bf16)
    grad_up_bias = jnp.sum(grad_up.astype(f32), axis=0)
    grad_up_weight = dot_tn(hidden_low, grad_up).astype(bf16)
    grad_hidden = grad_second + dot_nt(grad_up, up_full)
    grad_first, grad_gain_1, grad_shift_1 = norm_back(normed_1, rstd_1, gain_1, grad_hidden)
    grad_branch = grad_first.astype(bf16)
    grad_out_bias = jnp.sum(grad_branch.astype(f32), axis=0)
    grad_out = dot_tn(context, grad_branch).astype(bf16)
    grad_context = dot_nt(grad_branch, out_full).astype(bf16)

    grad_second_pack = jnp.concatenate([grad_out, grad_up_weight], axis=1)
    down_part = scatter_wide(grad_down)
    grad_context, grad_second_pack, down_part = lax.optimization_barrier(
        (grad_context, grad_second_pack, down_part)
    )
    down_pieces = scatter_narrow_start(down_part)
    second_part = scatter_wide(grad_second_pack)

    gq, gk, gv, gpq, gpk = attend_back(
        qkv, pos, grad_context, context_wide, probs, probs_scale
    )
    grad_up_bias = jnp.transpose(grad_up_bias.reshape(D // share, 4, share), (1, 0, 2))
    vector_grads = jnp.concatenate(
        [
            jnp.stack(
                [
                    grad_out_bias, grad_gain_1, grad_shift_1,
                    grad_down_bias, grad_gain_2, grad_shift_2,
                ]
            ),
            grad_up_bias.reshape(4, D),
            jnp.zeros((6, D), f32),
        ],
        axis=0,
    )
    gq, down_pieces = lax.optimization_barrier((gq, down_pieces))
    down_sum = sum(piece.astype(f32) for piece in down_pieces)
    first_half, second_half = weigh(
        x, gq, gk, gv, rel_turned, gpq, gpk, qkv_weight, vector_grads
    )
    upper = all_bits()[:-1]
    halves = [
        [split_bits(first_half), all_bits(), [0] + upper],
        [split_bits(second_half), all_bits(), [0] + upper[::-1]],
    ]

    def halve_both():
        for entry in halves:
            entry[0] = halve(entry[0], entry[2].pop(0), entry[1])

    def together(*others):
        kept = lax.optimization_barrier((halves[0][0], halves[1][0]) + others)
        halves[0][0], halves[1][0] = kept[:2]
        return kept[2:]

    halve_both()
    gq, gk, gv, second_part = together(gq, gk, gv, second_part)
    second_pieces = scatter_narrow_start(second_part)
    grad_inputs = grad_first + dot_nt(jnp.concatenate([gq, gk, gv], axis=1), qkv_weight)
    halve_both()
    grad_inputs, *second_pieces = together(grad_inputs, *second_pieces)
    second_sum = sum(piece.astype(f32) for piece in second_pieces)
    while halves[0][2]:
        halve_both()
    last_sum = scatter_narrow(jnp.concatenate([halves[0][0], halves[1][0]], axis=1))
    turned = last_sum[:, 3 * D :].T
    vec = lambda i: turned[SEQ + i]
    return (
        hidden_out.reshape(hidden_in.shape),
        grad_inputs.reshape(hidden_in.shape),
        last_sum[:, :D], vec(0),
        last_sum[:, D : 2 * D], vec(1),
        last_sum[:, 2 * D : 3 * D], vec(2),
        second_sum[:, :D], vec(8), vec(9), vec(10),
        second_sum[:, D:],
        turned[SEQ + 14 : SEQ + 18].reshape(4 * share),
        down_sum, vec(11), vec(12), vec(13),
        turned[:SEQ],
    )


def solution(mesh):
    tokens = P(None, AXES, None, None)
    rows = P(AXES, None)
    vector = P(AXES)
    weights = (
        rows, vector, rows, vector, rows, vector, rows, vector, vector, vector,
        rows, vector, rows, vector, vector, vector, P(None, AXES),
    )
    return jax.shard_map(
        body,
        mesh=mesh,
        in_specs=(tokens, tokens, P(None, AXES)) + weights,
        out_specs=(tokens, tokens) + weights,
        check_vma=False,
    )
```

```python
import functools
import math

import jax
import jax.numpy as jnp
from jax import lax
from jax.experimental import pallas as pl
from jax.experimental.pallas import tpu as pltpu
from jax.sharding import PartitionSpec as P

D = 768
HEADS = 12
HEAD = 64
SEQ = 512
MICRO = 2
PAIR = 2 * HEAD
PAIRS = HEADS // 2
CHUNK = 128
ROWS = 32
DELAYS = (0, 1)
LOG2E = 1.4426950408889634
VECTORS = 128
EARLY = 2
SCALE = 1.0 / math.sqrt(3 * HEAD)
AXES = ("wide", "narrow")
norm_epsilon = 1e-06
bf16 = jnp.bfloat16
f32 = jnp.float32


def dot_nt(left, right):
    return lax.dot_general(left, right, (((1,), (1,)), ((), ())), preferred_element_type=f32)


def dot_nn(left, right):
    return lax.dot_general(left, right, (((1,), (0,)), ((), ())), preferred_element_type=f32)


def dot_tn(left, right):
    return lax.dot_general(left, right, (((0,), (0,)), ((), ())), preferred_element_type=f32)


def reverse_rows(flip, block):
    half = SEQ // 2
    return jnp.concatenate(
        [dot_nn(flip, block[half:]).astype(bf16), dot_nn(flip, block[:half]).astype(bf16)], axis=0
    )


def flip_matrix():
    half = SEQ // 2
    rows = lax.broadcasted_iota(jnp.int32, (half, half), 0)
    cols = lax.broadcasted_iota(jnp.int32, (half, half), 1)
    return jnp.where(rows + cols == half - 1, 1.0, 0.0).astype(bf16)


def skew(rows, base):
    return pltpu.roll(rows, base % SEQ, 1, stride=1, stride_axis=0)


def lane_tiles(block):
    return [block[:, t * CHUNK : (t + 1) * CHUNK] for t in range(SEQ // CHUNK)]


def clip_edges(moved, table, c, below):
    tiles = lane_tiles(moved)
    left = jnp.broadcast_to(table[:, :1], (CHUNK, CHUNK))
    right = jnp.broadcast_to(table[:, SEQ - 1 :], (CHUNK, CHUNK))
    if c == 0:
        tiles[2], tiles[3] = jnp.where(below, tiles[2], right), right
    elif c == 1:
        tiles[3] = jnp.where(below, tiles[3], right)
    elif c == 2:
        tiles[0] = jnp.where(below, left, tiles[0])
    else:
        tiles[0], tiles[1] = left, jnp.where(below, left, tiles[1])
    return jnp.concatenate(tiles, axis=1)


def fold_edges(moved, c, below):
    tiles = lane_tiles(moved)
    part = (2, 3, 0, 1)[c]
    zero = jnp.zeros_like(tiles[part])
    upper = c < 2
    if upper:
        outside, tiles[part] = jnp.where(below, zero, tiles[part]), jnp.where(below, tiles[part], zero)
    else:
        outside, tiles[part] = jnp.where(below, tiles[part], zero), jnp.where(below, zero, tiles[part])
    outside = [outside]
    if c in (0, 3):
        whole = 3 if c == 0 else 0
        outside.append(tiles[whole])
        tiles[whole] = zero
    edge, lane = (0, 0) if upper else (3, CHUNK - 1)
    outside = jnp.concatenate(outside, axis=1)
    lanes = lax.broadcasted_iota(jnp.int32, (outside.shape[1], CHUNK), 1)
    to_lane = jnp.where(lanes == lane, 1.0, 0.0).astype(bf16)
    tiles[edge] = tiles[edge] + dot_nn(outside, to_lane).astype(bf16)
    return jnp.concatenate(tiles, axis=1)


def weave(first, second):
    waiting = {0: [], 1: []}

    def emit(which, piece):
        store = piece() if piece is not None else None
        if store is not None:
            waiting[which].append(store)
        keep = DELAYS[which] if piece is not None else 0
        while len(waiting[which]) > keep:
            waiting[which].pop(0)()

    total = max(len(first), len(second))
    done = [0, 0]
    for step in range(1, total + 1):
        for which, pieces in ((1, second), (0, first)):
            while done[which] * total < step * len(pieces):
                emit(which, pieces[done[which]])
                done[which] += 1
    for which in (1, 0):
        emit(which, None)


def storing(ref, where, value):
    def store():
        ref[where] = value

    return store


def attend_kernel(
    len_ref, q_ref, k_ref, v_ref, pq_ref, pk_ref, ctx_ref, wide_ref, probs_ref, scale_ref,
    kp_a, kp_b, qp_a, qp_b, raw_a, raw_b, back_a, back_b, low_a, low_b,
):
    kp, qp, raw, back, low = (kp_a, kp_b), (qp_a, qp_b), (raw_a, raw_b), (back_a, back_b), (low_a, low_b)
    flip = flip_matrix()
    half = SEQ // 2
    lane_pair = lax.broadcasted_iota(jnp.int32, (1, PAIR), 1)
    rows = lax.broadcasted_iota(jnp.int32, (CHUNK, CHUNK), 0)
    cols = lax.broadcasted_iota(jnp.int32, (CHUNK, CHUNK), 1)
    strictly_below, below = cols < rows, cols <= rows
    places = lax.broadcasted_iota(jnp.int32, (1, SEQ), 1)
    pq_all = pq_ref[...]
    pk_flipped = reverse_rows(flip, pk_ref[...])
    units = [(seq, head) for seq in range(MICRO) for head in range(2)]
    heads = [
        (lane_pair >= head * HEAD) & (lane_pair < (head + 1) * HEAD) for head in range(2)
    ]
    hidden_keys = [jnp.where(places < len_ref[seq], 0.0, -1e30) for seq in range(MICRO)]

    def products(u):
        seq, head = units[u]
        slot = u % 2
        tokens = slice(seq * SEQ, (seq + 1) * SEQ)
        pieces = []
        for part in (slice(0, half), slice(half, SEQ)):
            def key_places(part=part):
                k_all = k_ref[tokens, :]
                k_head = jnp.where(heads[head], k_all, jnp.zeros_like(k_all))
                return storing(kp[slot], (slice(None), part), dot_nt(k_head, pq_all[part]).astype(bf16))

            def query_places(part=part):
                q_all = q_ref[tokens, :]
                q_head = jnp.where(heads[head], q_all, jnp.zeros_like(q_all))
                return storing(qp[slot], (slice(None), part), dot_nt(q_head, pk_flipped[part]).astype(bf16))

            def content(part=part):
                q_all = q_ref[tokens, :]
                q_head = jnp.where(heads[head], q_all, jnp.zeros_like(q_all))
                keys = slice(seq * SEQ + part.start, seq * SEQ + part.stop)
                return storing(raw[slot], (slice(None), part), dot_nt(q_head, k_ref[keys, :]))

            pieces += [key_places, query_places, content]
        return pieces

    def softmax(u):
        seq, head = units[u]
        slot = u % 2
        pieces = []
        for c in range(SEQ // CHUNK):
            def turn(c=c):
                part = slice(c * CHUNK, (c + 1) * CHUNK)
                table = kp[slot][part, :]
                moved = clip_edges(skew(table, c * CHUNK + 256), table, c, strictly_below)
                return storing(back[slot], (slice(None), part), moved.T)

            pieces.append(turn)
        for c in range(SEQ // CHUNK):
            def shift(c=c):
                part = slice(c * CHUNK, (c + 1) * CHUNK)
                table = qp[slot][part, :]
                return storing(
                    qp[slot], (part, slice(None)),
                    clip_edges(skew(table, c * CHUNK - 255), table, c, below),
                )

            pieces.append(shift)
        pieces.append(None)

        def normal(here):
            scores = (
                raw[slot][here, :]
                + (qp[slot][here, :].astype(f32) + back[slot][here, :].astype(f32))
                + hidden_keys[seq]
            )
            row_max = jnp.max(scores, axis=1, keepdims=True)
            exp_scores = jnp.exp2((scores - row_max) * (SCALE * LOG2E))
            return storing(low[slot], (here, slice(None)), exp_scores.astype(bf16))

        for start in range(0, SEQ, ROWS):
            pieces.append(functools.partial(normal, slice(start, start + ROWS)))
        return pieces

    def results(u):
        seq, head = units[u]
        slot = u % 2
        tokens = slice(seq * SEQ, (seq + 1) * SEQ)

        def context():
            v_all = v_ref[tokens, :]
            both = dot_nn(low[slot][...], jnp.concatenate([v_all, jnp.ones_like(v_all)], axis=1))
            scale = 1.0 / both[:, PAIR:]
            scale_ref[seq, head] = scale
            ctx = both[:, :PAIR] * scale
            if head == 1:
                ctx = jnp.where(heads[head], ctx, wide_ref[tokens, :])
                ctx_ref[tokens, :] = ctx.astype(bf16)
            wide_ref[tokens, :] = ctx

        def left():
            probs_ref[seq, head, :, :half] = dot_nn(low[slot][:, half:], flip).astype(bf16)

        def right():
            probs_ref[seq, head, :, half:] = dot_nn(low[slot][:, :half], flip).astype(bf16)

        return [context, left, right]

    count = len(units)
    for step in range(count + 2):
        matrix = products(step) if step < count else []
        if step >= 2:
            matrix = results(step - 2) + matrix
        vector = softmax(step - 1) if 1 <= step <= count else []
        weave(matrix, vector)


def attend(lengths, qkv, pos):
    qkv_block = lambda which: pl.BlockSpec((MICRO * SEQ, PAIR), lambda p, n: (0, which * PAIRS + p))
    pos_block = lambda which: pl.BlockSpec((SEQ, PAIR), lambda p, n: (0, which * PAIRS + p))
    square = lambda kind: [pltpu.VMEM((SEQ, SEQ), kind)] * 2
    return pl.pallas_call(
        attend_kernel,
        grid_spec=pltpu.PrefetchScalarGridSpec(
            num_scalar_prefetch=1,
            grid=(PAIRS,),
            in_specs=[qkv_block(0), qkv_block(1), qkv_block(2), pos_block(0), pos_block(1)],
            out_specs=[
                pl.BlockSpec((MICRO * SEQ, PAIR), lambda p, n: (0, p)),
                pl.BlockSpec((MICRO * SEQ, PAIR), lambda p, n: (0, p)),
                pl.BlockSpec((MICRO, 2, SEQ, SEQ), lambda p, n: (0, p, 0, 0)),
                pl.BlockSpec((MICRO, 2, SEQ, CHUNK), lambda p, n: (0, p, 0, 0)),
            ],
            scratch_shapes=square(bf16) + square(bf16) + square(f32) + square(bf16) + square(bf16),
        ),
        out_shape=[
            jax.ShapeDtypeStruct((MICRO * SEQ, D), bf16),
            jax.ShapeDtypeStruct((MICRO * SEQ, D), f32),
            jax.ShapeDtypeStruct((MICRO, HEADS, SEQ, SEQ), bf16),
            jax.ShapeDtypeStruct((MICRO, HEADS, SEQ, CHUNK), f32),
        ],
        compiler_params=pltpu.CompilerParams(vmem_limit_bytes=40 * 2**20),
        cost_estimate=pl.CostEstimate(
            flops=24 * 8 * 2 * SEQ * SEQ * PAIR,
            bytes_accessed=20 * 2**20,
            transcendentals=24 * SEQ * SEQ,
        ),
        name="attend",
    )(lengths, qkv, qkv, qkv, pos, pos)


def attend_back_kernel(
    earlier, q_ref, k_ref, v_ref, pq_ref, pk_ref, gc_ref, ctx_ref, probs_ref, scale_ref, *refs
):
    (
    gq_ref, gk_ref, gv_ref, gpq_ref, gpk_ref,
    raw_a, raw_b, grad_a, grad_b, moved_a, moved_b, turned_a, turned_b,
    inner_a, inner_b, q_t, k_t, gc_t, pq_t, pk_t, k_rev, v_rev, gq_t, gk_t, gv_t,
    ) = refs[earlier:]
    raw, grad, moved, turned = (raw_a, raw_b), (grad_a, grad_b), (moved_a, moved_b), (turned_a, turned_b)
    inner = (inner_a, inner_b)
    flip = flip_matrix()
    half = SEQ // 2
    lane_pair = lax.broadcasted_iota(jnp.int32, (1, PAIR), 1)
    rows = lax.broadcasted_iota(jnp.int32, (CHUNK, CHUNK), 0)
    cols = lax.broadcasted_iota(jnp.int32, (CHUNK, CHUNK), 1)
    below = cols <= rows
    units = [(seq, head) for seq in range(MICRO) for head in range(2)]
    heads = [
        (lane_pair >= head * HEAD) & (lane_pair < (head + 1) * HEAD) for head in range(2)
    ]
    tokens = [slice(seq * SEQ, (seq + 1) * SEQ) for seq in range(MICRO)]
    pq_t[...] = pq_ref[...].T
    pk_t[...] = pk_ref[...].T

    def prepare(seq):
        v_rev[seq] = reverse_rows(flip, v_ref[tokens[seq], :])
        k_flipped = reverse_rows(flip, k_ref[tokens[seq], :])
        k_t[seq] = k_flipped.T
        q_t[seq] = q_ref[tokens[seq], :].T
        scale = jnp.where(heads[0], scale_ref[seq, 0], scale_ref[seq, 1])
        gc_t[seq] = (gc_ref[tokens[seq], :].astype(f32) * scale).astype(bf16).T

    def grads(u):
        seq, head = units[u]
        slot = u % 2
        pieces = []

        def start():
            if head == 0:
                prepare(seq)
            product = gc_ref[tokens[seq], :].astype(f32) * ctx_ref[tokens[seq], :]
            product = jnp.where(heads[head], product, 0.0)
            inner[slot][...] = jnp.broadcast_to(
                jnp.sum(product, axis=1, keepdims=True), (SEQ, CHUNK)
            )

        pieces.append(start)
        for part in (slice(0, half), slice(half, SEQ)):
            def values(part=part):
                gc_all = gc_ref[tokens[seq], :]
                gc_head = jnp.where(heads[head], gc_all, jnp.zeros_like(gc_all))
                return storing(raw[slot], (slice(None), part), dot_nt(gc_head, v_rev[seq, part, :]))

            pieces.append(values)
        pieces.append(None)
        for c in range(SEQ // CHUNK):
            for r in range(0, CHUNK, ROWS):
                def softmax(here=slice(c * CHUNK + r, c * CHUNK + r + ROWS)):
                    low, scale = inner[slot][here, :], scale_ref[seq, head, here, :]
                    tiles = [
                        (
                            probs_ref[seq, head, here, t : t + CHUNK].astype(f32)
                            * ((raw[slot][here, t : t + CHUNK] - low) * scale)
                        ).astype(bf16)
                        for t in range(0, SEQ, CHUNK)
                    ]
                    return storing(grad[slot], (here, slice(None)), jnp.concatenate(tiles, axis=1))

                pieces.append(softmax)
        pieces.append(None)

        def shift(c):
            part = slice(c * CHUNK, (c + 1) * CHUNK)
            table = fold_edges(skew(grad[slot][part, :], c * CHUNK - 255), c, below)
            return storing(moved[slot], (part, slice(None)), table)

        def turn(c):
            part = slice(c * CHUNK, (c + 1) * CHUNK)
            table = fold_edges(skew(grad[slot][:, part].T, c * CHUNK - 255), c, below)
            return storing(turned[slot], (part, slice(None)), table)

        for c in range(SEQ // CHUNK):
            pieces += [functools.partial(turn, c), functools.partial(shift, c)]
        return pieces

    def results(u):
        seq, head = units[u]
        slot = u % 2
        mine = slice(head * HEAD, (head + 1) * HEAD)

        def values():
            gv_t[seq, mine, :] = dot_nn(gc_t[seq, mine, :], probs_ref[seq, head]).astype(bf16)

        def keys():
            total = dot_nn(q_t[seq, mine, :], grad[slot][...])
            total = total + dot_nt(pq_t[mine, :], turned[slot][...])
            gk_t[seq, mine, :] = (total * SCALE).astype(bf16)

        def queries():
            total = dot_nt(k_t[seq, mine, :], grad[slot][...])
            total = total + dot_nt(pk_t[mine, :], moved[slot][...])
            gq_t[seq, mine, :] = (total * SCALE).astype(bf16)

        def key_places():
            total = dot_nn(q_t[seq, mine, :], moved[slot][...]) * SCALE
            gpk_ref[mine, :] = total if seq == 0 else gpk_ref[mine, :] + total

        def query_places():
            total = dot_nn(k_t[seq, mine, :], turned[slot][...]) * SCALE
            gpq_ref[mine, :] = total if seq == 0 else gpq_ref[mine, :] + total

        def finish():
            gq_ref[tokens[seq], :] = gq_t[seq].T
            for kept, out in ((gk_t, gk_ref), (gv_t, gv_ref)):
                out[tokens[seq], :] = jnp.concatenate(
                    [
                        dot_nn(kept[seq, :, half:], flip).astype(bf16),
                        dot_nn(kept[seq, :, :half], flip).astype(bf16),
                    ],
                    axis=1,
                ).T

        pieces = [values, keys, queries, key_places, query_places]
        return pieces + [finish] if head == 1 else pieces

    count = len(units)
    for step in range(count + 1):
        matrix = results(step - 1) if step >= 1 else []
        vector = grads(step) if step < count else []
        weave(matrix, vector)


def attend_back(first, count, earlier, qkv, pos, grad_context, context_wide, probs, scale):
    qkv_block = lambda which: pl.BlockSpec((MICRO * SEQ, PAIR), lambda p: (0, which * PAIRS + first + p))
    pos_block = lambda which: pl.BlockSpec((SEQ, PAIR), lambda p: (0, which * PAIRS + first + p))
    token_block = pl.BlockSpec((MICRO * SEQ, PAIR), lambda p: (0, first + p))
    table_block = pl.BlockSpec((PAIR, SEQ), lambda p: (first + p, 0))
    token_shape = jax.ShapeDtypeStruct((MICRO * SEQ, D), bf16)
    table_shape = jax.ShapeDtypeStruct((D, SEQ), f32)
    square = lambda kind: [pltpu.VMEM((SEQ, SEQ), kind)] * 2
    wide = pltpu.VMEM((MICRO, PAIR, SEQ), bf16)
    tall = pltpu.VMEM((MICRO, SEQ, PAIR), bf16)
    return pl.pallas_call(
        functools.partial(attend_back_kernel, len(earlier)),
        grid=(count,),
        input_output_aliases={9 + i: i for i in range(len(earlier))},
        in_specs=[
            qkv_block(0), qkv_block(1), qkv_block(2), pos_block(0), pos_block(1),
            token_block, token_block,
            pl.BlockSpec((MICRO, 2, SEQ, SEQ), lambda p: (0, first + p, 0, 0)),
            pl.BlockSpec((MICRO, 2, SEQ, CHUNK), lambda p: (0, first + p, 0, 0)),
        ]
        + [pl.BlockSpec(memory_space=pl.ANY)] * len(earlier),
        out_specs=[token_block, token_block, token_block, table_block, table_block],
        out_shape=[token_shape, token_shape, token_shape, table_shape, table_shape],
        scratch_shapes=square(f32) + square(bf16) * 3
        + [pltpu.VMEM((SEQ, CHUNK), f32)] * 2
        + [wide, wide, wide, pltpu.VMEM((PAIR, SEQ), bf16), pltpu.VMEM((PAIR, SEQ), bf16)]
        + [tall, tall, wide, wide, wide],
        compiler_params=pltpu.CompilerParams(vmem_limit_bytes=56 * 2**20),
        cost_estimate=pl.CostEstimate(
            flops=count * 4 * 16 * 2 * SEQ * SEQ * PAIR, bytes_accessed=count * 4 * 2**20, transcendentals=0
        ),
        name="attend_back",
    )(qkv, qkv, qkv, pos, pos, grad_context, context_wide, probs, scale, *earlier)


def weigh_kernel(
    low_ref, x_ref, gq_ref, gk_ref, gv_ref, rel_ref, gpq_ref, gpk_ref, wq_ref, wk_ref,
    vec_ref, up_bias_ref,
    first_keep, first_send, second_keep, second_send, x_turned, rel_sum, rows_ref,
):
    step = pl.program_id(0)
    width = gq_ref.shape[1]
    count, rows = first_keep.shape[0], first_keep.shape[1]

    def put(keep, send, columns, value):
        value = value.astype(bf16).reshape(count, 2, rows, value.shape[1])
        lower, upper = value[:, 0], value[:, 1]
        is_upper = low_ref[0] == 1
        keep[:, :, columns] = jnp.where(is_upper, upper, lower)
        send[:, :, columns] = jnp.where(is_upper, lower, upper)

    def columns_at(start):
        return pl.ds(pl.multiple_of(start, width), width)

    @pl.when(step == 0)
    def begin():
        x_turned[...] = x_ref[...].T
        rel_sum[...] = jnp.zeros_like(rel_sum)
        rows_ref[...] = jnp.zeros_like(rows_ref)
        rows_ref[8:14, :] = vec_ref[...]
        rows_ref[14:18, :] = up_bias_ref[...]

    token_ones = jnp.ones((8, MICRO * SEQ), bf16)
    place_ones = jnp.ones((8, SEQ), bf16)
    row = lax.broadcasted_iota(jnp.int32, (8, width), 0)
    biases = jnp.zeros((8, width), f32)
    tables = ((gq_ref, gpq_ref, wq_ref), (gk_ref, gpk_ref, wk_ref))
    for which, (grad_ref, table_ref, weight_ref) in enumerate(tables):
        grad = grad_ref[...]
        table = table_ref[...].astype(bf16)
        total = dot_nn(x_turned[...], grad) + dot_nt(rel_ref[...], table)
        put(first_keep, first_send, columns_at(which * D + step * width), total)
        rel_sum[...] += dot_nn(weight_ref[...], table)
        bias = dot_nn(token_ones, grad) + dot_nt(place_ones, table)
        biases = jnp.where(row == which, bias, biases)
    grad = gv_ref[...]
    put(second_keep, second_send, columns_at(step * width), dot_nn(x_turned[...], grad))
    rows_ref[:8, columns_at(step * width)] = jnp.where(row == 2, dot_nn(token_ones, grad), biases)

    @pl.when(step == pl.num_programs(0) - 1)
    def end():
        put(second_keep, second_send, slice(D, D + SEQ), rel_sum[...])
        put(second_keep, second_send, slice(D + SEQ, D + SEQ + CHUNK), rows_ref[...].T)


def weigh(x, gq, gk, gv, gpq, gpk, first_pack, vectors):
    steps = 3
    width = D // steps
    whole = lambda shape: pl.BlockSpec(shape, lambda p, n: (0,) * len(shape))
    columns = lambda rows, skip=0: pl.BlockSpec((rows, width), lambda p, n: (0, skip // width + p))
    tokens = MICRO * SEQ
    size = lax.axis_size("wide")
    shapes = [(size // 2, D // size, cols) for cols in (2 * D, 2 * D, D + SEQ + CHUNK, D + SEQ + CHUNK)]
    return pl.pallas_call(
        weigh_kernel,
        grid_spec=pltpu.PrefetchScalarGridSpec(
            num_scalar_prefetch=1,
            grid=(steps,),
            in_specs=[
                whole((tokens, D)), columns(tokens), columns(tokens), columns(tokens),
                whole((D, SEQ)),
                pl.BlockSpec((width, SEQ), lambda p, n: (p, 0)),
                pl.BlockSpec((width, SEQ), lambda p, n: (p, 0)),
                columns(D, SEQ), columns(D, SEQ + D),
            ]
            + [whole((6, D)), whole((4, D))],
            out_specs=[whole(shape) for shape in shapes],
            scratch_shapes=[
                pltpu.VMEM((D, tokens), bf16), pltpu.VMEM((D, SEQ), f32), pltpu.VMEM((CHUNK, D), f32),
            ],
        ),
        out_shape=[jax.ShapeDtypeStruct(shape, bf16) for shape in shapes],
        compiler_params=pltpu.CompilerParams(vmem_limit_bytes=56 * 2**20),
        cost_estimate=pl.CostEstimate(
            flops=2 * D * D * (3 * tokens + 4 * SEQ), bytes_accessed=20 * 2**20, transcendentals=0
        ),
        name="weigh",
    )(my_bit(0).reshape(1), x, gq, gk, gv, first_pack, gpq, gpk, first_pack, first_pack, *vectors)


def feed_back_kernel(
    grad_ref, hidden_ref, slope_ref, down_ref, up_ref,
    grad_hidden_ref, grad_weight_ref, bias_ref, hidden_turned, grad_up,
):
    step = pl.program_id(0)

    @pl.when(step == 0)
    def begin():
        hidden_turned[...] = hidden_ref[...].T
        grad_hidden_ref[...] = jnp.zeros_like(grad_hidden_ref)

    for seq in range(MICRO):
        part = slice(seq * SEQ, (seq + 1) * SEQ)
        grad_act = dot_nt(grad_ref[part, :], down_ref[...])
        grad_up[part, :] = (grad_act * slope_ref[part, :].astype(f32)).astype(bf16)
    for seq in range(MICRO):
        part = slice(seq * SEQ, (seq + 1) * SEQ)
        grad_hidden_ref[part, :] += dot_nt(grad_up[part, :], up_ref[...])
    grad_weight_ref[...] = dot_nn(hidden_turned[...], grad_up[...]).astype(bf16)
    bias_ref[...] = dot_nn(jnp.ones((8, MICRO * SEQ), bf16), grad_up[...])


def feed_back(grad_feed, hidden_low, slope, down_full, second_pack):
    tokens = MICRO * SEQ
    blocks = slope.shape[1] // D
    whole = lambda shape: pl.BlockSpec(shape, lambda f: (0, 0))
    return pl.pallas_call(
        feed_back_kernel,
        grid=(blocks,),
        in_specs=[
            whole((tokens, D)), whole((tokens, D)),
            pl.BlockSpec((tokens, D), lambda f: (0, f)),
            pl.BlockSpec((D, D), lambda f: (f, 0)),
            pl.BlockSpec((D, D), lambda f: (0, 1 + f)),
        ],
        out_specs=[
            whole((tokens, D)),
            pl.BlockSpec((D, D), lambda f: (0, 1 + f)),
            pl.BlockSpec((8, D), lambda f: (0, f)),
        ],
        out_shape=[
            jax.ShapeDtypeStruct((tokens, D), f32),
            jax.ShapeDtypeStruct((D, (1 + blocks) * D), bf16),
            jax.ShapeDtypeStruct((8, blocks * D), f32),
        ],
        scratch_shapes=[pltpu.VMEM((D, tokens), bf16), pltpu.VMEM((tokens, D), bf16)],
        compiler_params=pltpu.CompilerParams(vmem_limit_bytes=56 * 2**20),
        cost_estimate=pl.CostEstimate(
            flops=6 * tokens * D * blocks * D, bytes_accessed=30 * 2**20, transcendentals=0
        ),
        name="feed_back",
    )(grad_feed, hidden_low, slope, down_full, second_pack)


def normalise(v):
    row_mean = jnp.mean(v, axis=-1, keepdims=True)
    centered = v - row_mean
    variance = jnp.mean(centered * centered, axis=-1, keepdims=True)
    rstd = lax.rsqrt(variance + norm_epsilon)
    return centered * rstd, rstd


def column_sums(values):
    return jnp.sum(values, axis=0)


def norm_back(normed, rstd, gain, grad):
    e = grad * gain
    grad_in = rstd * (
        e
        - jnp.mean(e, axis=-1, keepdims=True)
        - normed * jnp.mean(e * normed, axis=-1, keepdims=True)
    )
    return grad_in, column_sums(grad * normed), column_sums(grad)


def narrow_shifts(block, shift):
    size = lax.axis_size("narrow")
    return lax.ppermute(block, "narrow", [(i, (i + shift) % size) for i in range(size)])


def gather_rows(shard):
    size = lax.axis_size("narrow")
    me = lax.axis_index("narrow")
    rows, cols = shard.shape
    together = jnp.zeros((size * rows, cols), shard.dtype)
    for shift in range(size):
        block = narrow_shifts(shard, shift) if shift else shard
        owner = lax.rem(me - shift + size, size)
        together = lax.dynamic_update_slice(together, block, (owner * rows, 0))
    return lax.all_gather(together, "wide", axis=0, tiled=True)


def scatter_wide(full):
    return lax.psum_scatter(full, "wide", scatter_dimension=0, tiled=True)


def scatter_narrow_start(part):
    size = lax.axis_size("narrow")
    me = lax.axis_index("narrow")
    rows = part.shape[-2] // size
    pieces = []
    for shift in range(size):
        target = lax.rem(me + shift, size)
        block = lax.dynamic_slice_in_dim(part, target * rows, rows, part.ndim - 2)
        pieces.append(narrow_shifts(block, shift) if shift else block)
    return pieces


def scatter_narrow(part):
    return sum(piece.astype(f32) for piece in scatter_narrow_start(part))


def swap(block, bit):
    size = lax.axis_size("wide")
    return lax.ppermute(block, "wide", [(i, i ^ (1 << bit)) for i in range(size)])


def my_bit(bit):
    return lax.rem(lax.axis_index("wide") // (1 << bit), 2)


def wide_bits():
    return (lax.axis_size("wide") - 1).bit_length()


def split_bits(full):
    bits = wide_bits()
    return full.reshape((2,) * bits + (full.shape[0] >> bits, full.shape[1]))


def add_low(first, second):
    return (first.astype(f32) + second.astype(f32)).astype(bf16)


def two_halves(part, bit, left):
    axis, mine = left.index(bit), my_bit(bit)
    keep = lax.dynamic_index_in_dim(part, mine, axis, keepdims=False)
    send = lax.dynamic_index_in_dim(part, 1 - mine, axis, keepdims=False)
    left.remove(bit)
    return keep, send


def scatter_upper(part):
    size = lax.axis_size("wide")
    groups = [list(range(low, size, 2)) for low in range(2)]
    part = part.reshape(-1, part.shape[-1])
    return lax.psum_scatter(part, "wide", scatter_dimension=0, tiled=True, axis_index_groups=groups)


def halve(part, bit, left):
    keep, send = two_halves(part, bit, left)
    return add_low(keep, swap(send, bit))


def all_bits():
    return list(range(wide_bits()))[::-1]


def body(
    hidden_in, cotangent, seq_lengths,
    query_weight, query_bias, key_weight, key_bias, value_weight, value_bias,
    out_weight, out_bias, first_gain, first_shift, up_weight, up_bias,
    down_weight, down_bias, second_gain, second_shift, rel_table,
):
    tokens = MICRO * SEQ
    x = hidden_in.reshape(tokens, D)
    cot = cotangent.reshape(tokens, D).astype(f32)
    lengths = seq_lengths.reshape(MICRO)
    share = query_weight.shape[0]
    vectors = [
        query_bias, key_bias, value_bias, out_bias, first_gain, first_shift,
        down_bias, second_gain, second_shift,
    ]
    vectors += [up_bias[c * share : (c + 1) * share] for c in range(4)]
    places = lax.broadcasted_iota(jnp.int32, (VECTORS, share), 0)
    stacked = jnp.zeros((VECTORS, share), bf16)
    for place, vector in enumerate(vectors):
        stacked = jnp.where(places == place, vector[None, :], stacked)
    first_pack = gather_rows(
        jnp.concatenate(
            [rel_table.T, query_weight, key_weight, value_weight, stacked.T], axis=1
        )
    )
    second_pack = gather_rows(jnp.concatenate([out_weight, up_weight], axis=1))
    down_full = gather_rows(down_weight)
    qkv_weight = first_pack[:, SEQ : SEQ + 3 * D]
    rel_turned = first_pack[:, :SEQ]
    out_full = second_pack[:, :D]
    up_full = second_pack[:, D:]
    vector_rows = first_pack[:, SEQ + 3 * D :].T.astype(f32)
    qkv_bias = vector_rows[:3].reshape(3 * D)
    out_b, gain_1, shift_1, down_b, gain_2, shift_2 = (vector_rows[i] for i in range(3, 9))
    up_b = jnp.transpose(vector_rows[9:13].reshape(4, D // share, share), (1, 0, 2)).reshape(4 * D)

    qkv = (dot_nn(x, qkv_weight) + qkv_bias).astype(bf16)
    pos = (dot_tn(rel_turned, qkv_weight[:, : 2 * D]) + qkv_bias[: 2 * D]).astype(bf16)
    context, context_wide, probs, probs_scale = attend(lengths, qkv, pos)

    first_in = x.astype(f32) + dot_nn(context, out_full) + out_b
    normed_1, rstd_1 = normalise(first_in)
    hidden = normed_1 * gain_1 + shift_1
    hidden_low = hidden.astype(bf16)
    upward = dot_nn(hidden_low, up_full) + up_b
    cdf = 0.5 * (1.0 + lax.erf(upward * math.sqrt(0.5)))
    activated_low = (upward * cdf).astype(bf16)
    slope = (cdf + upward * jnp.exp(-0.5 * upward * upward) * (1 / math.sqrt(2 * math.pi))).astype(
        bf16
    )
    second_in = hidden + dot_nn(activated_low, down_full) + down_b
    normed_2, rstd_2 = normalise(second_in)
    hidden_out = (normed_2 * gain_2 + shift_2).astype(bf16)

    grad_second, grad_gain_2, grad_shift_2 = norm_back(normed_2, rstd_2, gain_2, cot)
    grad_feed = grad_second.astype(bf16)
    grad_down_bias = column_sums(grad_feed.astype(f32))
    grad_down = dot_tn(activated_low, grad_feed).astype(bf16)
    grad_hidden, grad_second_pack, grad_up_bias = feed_back(
        grad_feed, hidden_low, slope, down_full, second_pack
    )
    grad_up_bias = grad_up_bias[0]
    grad_hidden = grad_second + grad_hidden
    grad_first, grad_gain_1, grad_shift_1 = norm_back(normed_1, rstd_1, gain_1, grad_hidden)
    grad_branch = grad_first.astype(bf16)
    grad_out_bias = column_sums(grad_branch.astype(f32))
    grad_out = dot_tn(context, grad_branch).astype(bf16)
    grad_context = dot_nt(grad_branch, out_full).astype(bf16)

    grad_second_pack = lax.dynamic_update_slice(grad_second_pack, grad_out, (0, 0))
    down_part = scatter_wide(grad_down)
    keep, send = two_halves(split_bits(grad_second_pack), 0, all_bits())
    came = swap(send, 0)
    grad_context, keep, send = lax.optimization_barrier((grad_context, keep, send))
    inputs = (qkv, pos, grad_context, context_wide, probs, probs_scale)
    early = list(attend_back(0, EARLY, (), *inputs))
    early[0], keep, came, down_part = lax.optimization_barrier((early[0], keep, came, down_part))
    second_part = scatter_upper(add_low(keep, came))
    down_pieces = scatter_narrow_start(down_part)
    gq, gk, gv, gpq, gpk = attend_back(EARLY, PAIRS - EARLY, early, *inputs)
    grad_up_bias = jnp.transpose(grad_up_bias.reshape(D // share, 4, share), (1, 0, 2))
    vector_grads = jnp.concatenate(
        [grad_out_bias, grad_gain_1, grad_shift_1, grad_down_bias, grad_gain_2, grad_shift_2]
    )
    vector_grads = (vector_grads.reshape(6, D), grad_up_bias.reshape(4, D))
    gq, down_pieces = lax.optimization_barrier((gq, down_pieces))
    down_sum = sum(piece.astype(f32) for piece in down_pieces)
    first_keep, first_send, second_keep, second_send = weigh(
        x, gq, gk, gv, gpq, gpk, first_pack, vector_grads
    )
    upper = all_bits()[:-1]
    sides = lambda part: part.reshape((2,) * len(upper) + part.shape[1:])
    halves = [
        [sides(add_low(first_keep, swap(first_send, 0))), all_bits()[:-1], list(upper)],
        [sides(add_low(second_keep, swap(second_send, 0))), all_bits()[:-1], upper[::-1]],
    ]

    def halve_both():
        for entry in halves:
            entry[0] = halve(entry[0], entry[2].pop(0), entry[1])

    def together(*others):
        kept = lax.optimization_barrier((halves[0][0], halves[1][0]) + others)
        halves[0][0], halves[1][0] = kept[:2]
        return kept[2:]

    gq, gk, gv, second_part = together(gq, gk, gv, second_part)
    second_pieces = scatter_narrow_start(second_part)
    grad_inputs = grad_first + dot_nt(jnp.concatenate([gq, gk, gv], axis=1), qkv_weight)
    halve_both()
    grad_inputs, *second_pieces = together(grad_inputs, *second_pieces)
    second_sum = sum(piece.astype(f32) for piece in second_pieces)
    while halves[0][2]:
        halve_both()
    last_sum = scatter_narrow(jnp.concatenate([halves[0][0], halves[1][0]], axis=1))
    turned = last_sum[:, 3 * D :].T
    vec = lambda i: turned[SEQ + i]
    return (
        hidden_out.reshape(hidden_in.shape),
        grad_inputs.reshape(hidden_in.shape),
        last_sum[:, :D], vec(0),
        last_sum[:, D : 2 * D], vec(1),
        last_sum[:, 2 * D : 3 * D], vec(2),
        second_sum[:, :D], vec(8), vec(9), vec(10),
        second_sum[:, D:],
        turned[SEQ + 14 : SEQ + 18].reshape(4 * share),
        down_sum, vec(11), vec(12), vec(13),
        turned[:SEQ],
    )


def solution(mesh):
    tokens = P(None, AXES, None, None)
    rows = P(AXES, None)
    vector = P(AXES)
    weights = (
        rows, vector, rows, vector, rows, vector, rows, vector, vector, vector,
        rows, vector, rows, vector, vector, vector, P(None, AXES),
    )
    return jax.shard_map(
        body,
        mesh=mesh,
        in_specs=(tokens, tokens, P(None, AXES)) + weights,
        out_specs=(tokens, tokens) + weights,
        check_vma=False,
    )
```

```python
import functools
import math

import jax
import jax.numpy as jnp
from jax import lax
from jax.experimental import pallas as pl
from jax.experimental.pallas import tpu as pltpu
from jax.sharding import PartitionSpec as P

D = 768
HEADS = 12
HEAD = 64
SEQ = 512
MICRO = 2
PAIR = 2 * HEAD
PAIRS = HEADS // 2
CHUNK = 128
ROWS = 32
DELAYS = (0, 1)
LOG2E = 1.4426950408889634
VECTORS = 128
EARLY = 2
SCALE = 1.0 / math.sqrt(3 * HEAD)
AXES = ("wide", "narrow")
norm_epsilon = 1e-06
bf16 = jnp.bfloat16
f32 = jnp.float32


def dot_nt(left, right):
    return lax.dot_general(left, right, (((1,), (1,)), ((), ())), preferred_element_type=f32)


def dot_nn(left, right):
    return lax.dot_general(left, right, (((1,), (0,)), ((), ())), preferred_element_type=f32)


def dot_tn(left, right):
    return lax.dot_general(left, right, (((0,), (0,)), ((), ())), preferred_element_type=f32)


def reverse_rows(flip, block):
    half = SEQ // 2
    return jnp.concatenate(
        [dot_nn(flip, block[half:]).astype(bf16), dot_nn(flip, block[:half]).astype(bf16)], axis=0
    )


def flip_matrix():
    half = SEQ // 2
    rows = lax.broadcasted_iota(jnp.int32, (half, half), 0)
    cols = lax.broadcasted_iota(jnp.int32, (half, half), 1)
    return jnp.where(rows + cols == half - 1, 1.0, 0.0).astype(bf16)


def skew(rows, base):
    return pltpu.roll(rows, base % SEQ, 1, stride=1, stride_axis=0)


def lane_tiles(block):
    return [block[:, t * CHUNK : (t + 1) * CHUNK] for t in range(SEQ // CHUNK)]


def clip_edges(moved, table, c, below):
    tiles = lane_tiles(moved)
    left = jnp.broadcast_to(table[:, :1], (CHUNK, CHUNK))
    right = jnp.broadcast_to(table[:, SEQ - 1 :], (CHUNK, CHUNK))
    if c == 0:
        tiles[2], tiles[3] = jnp.where(below, tiles[2], right), right
    elif c == 1:
        tiles[3] = jnp.where(below, tiles[3], right)
    elif c == 2:
        tiles[0] = jnp.where(below, left, tiles[0])
    else:
        tiles[0], tiles[1] = left, jnp.where(below, left, tiles[1])
    return jnp.concatenate(tiles, axis=1)


def fold_edges(moved, c, below):
    tiles = lane_tiles(moved)
    part = (2, 3, 0, 1)[c]
    zero = jnp.zeros_like(tiles[part])
    upper = c < 2
    if upper:
        outside, tiles[part] = jnp.where(below, zero, tiles[part]), jnp.where(below, tiles[part], zero)
    else:
        outside, tiles[part] = jnp.where(below, tiles[part], zero), jnp.where(below, zero, tiles[part])
    outside = [outside]
    if c in (0, 3):
        whole = 3 if c == 0 else 0
        outside.append(tiles[whole])
        tiles[whole] = zero
    edge, lane = (0, 0) if upper else (3, CHUNK - 1)
    outside = jnp.concatenate(outside, axis=1)
    lanes = lax.broadcasted_iota(jnp.int32, (outside.shape[1], CHUNK), 1)
    to_lane = jnp.where(lanes == lane, 1.0, 0.0).astype(bf16)
    tiles[edge] = tiles[edge] + dot_nn(outside, to_lane).astype(bf16)
    return jnp.concatenate(tiles, axis=1)


def weave(first, second):
    waiting = {0: [], 1: []}

    def emit(which, piece):
        store = piece() if piece is not None else None
        if store is not None:
            waiting[which].append(store)
        keep = DELAYS[which] if piece is not None else 0
        while len(waiting[which]) > keep:
            waiting[which].pop(0)()

    total = max(len(first), len(second))
    done = [0, 0]
    for step in range(1, total + 1):
        for which, pieces in ((1, second), (0, first)):
            while done[which] * total < step * len(pieces):
                emit(which, pieces[done[which]])
                done[which] += 1
    for which in (1, 0):
        emit(which, None)


def storing(ref, where, value):
    def store():
        ref[where] = value

    return store


def attend_kernel(
    len_ref, q_ref, k_ref, v_ref, pq_ref, pk_ref, ctx_ref, wide_ref, probs_ref, scale_ref,
    kp_a, kp_b, qp_a, qp_b, raw_a, raw_b, back_a, back_b, low_a, low_b,
):
    kp, qp, raw, back, low = (kp_a, kp_b), (qp_a, qp_b), (raw_a, raw_b), (back_a, back_b), (low_a, low_b)
    flip = flip_matrix()
    half = SEQ // 2
    lane_pair = lax.broadcasted_iota(jnp.int32, (1, PAIR), 1)
    rows = lax.broadcasted_iota(jnp.int32, (CHUNK, CHUNK), 0)
    cols = lax.broadcasted_iota(jnp.int32, (CHUNK, CHUNK), 1)
    strictly_below, below = cols < rows, cols <= rows
    places = lax.broadcasted_iota(jnp.int32, (1, SEQ), 1)
    pq_all = pq_ref[...]
    pk_flipped = reverse_rows(flip, pk_ref[...])
    units = [(seq, head) for seq in range(MICRO) for head in range(2)]
    heads = [
        (lane_pair >= head * HEAD) & (lane_pair < (head + 1) * HEAD) for head in range(2)
    ]
    hidden_keys = [jnp.where(places < len_ref[seq], 0.0, -1e30) for seq in range(MICRO)]

    def products(u):
        seq, head = units[u]
        slot = u % 2
        tokens = slice(seq * SEQ, (seq + 1) * SEQ)
        pieces = []
        for part in (slice(0, half), slice(half, SEQ)):
            def key_places(part=part):
                k_all = k_ref[tokens, :]
                k_head = jnp.where(heads[head], k_all, jnp.zeros_like(k_all))
                return storing(kp[slot], (slice(None), part), dot_nt(k_head, pq_all[part]).astype(bf16))

            def query_places(part=part):
                q_all = q_ref[tokens, :]
                q_head = jnp.where(heads[head], q_all, jnp.zeros_like(q_all))
                return storing(qp[slot], (slice(None), part), dot_nt(q_head, pk_flipped[part]).astype(bf16))

            def content(part=part):
                q_all = q_ref[tokens, :]
                q_head = jnp.where(heads[head], q_all, jnp.zeros_like(q_all))
                keys = slice(seq * SEQ + part.start, seq * SEQ + part.stop)
                return storing(raw[slot], (slice(None), part), dot_nt(q_head, k_ref[keys, :]))

            pieces += [key_places, query_places, content]
        return pieces

    def softmax(u):
        seq, head = units[u]
        slot = u % 2
        pieces = []
        for c in range(SEQ // CHUNK):
            def turn(c=c):
                part = slice(c * CHUNK, (c + 1) * CHUNK)
                table = kp[slot][part, :]
                moved = clip_edges(skew(table, c * CHUNK + 256), table, c, strictly_below)
                return storing(back[slot], (slice(None), part), moved.T)

            pieces.append(turn)
        for c in range(SEQ // CHUNK):
            def shift(c=c):
                part = slice(c * CHUNK, (c + 1) * CHUNK)
                table = qp[slot][part, :]
                return storing(
                    qp[slot], (part, slice(None)),
                    clip_edges(skew(table, c * CHUNK - 255), table, c, below),
                )

            pieces.append(shift)
        pieces.append(None)

        def normal(here):
            scores = (
                raw[slot][here, :]
                + (qp[slot][here, :].astype(f32) + back[slot][here, :].astype(f32))
                + hidden_keys[seq]
            )
            row_max = jnp.max(scores, axis=1, keepdims=True)
            exp_scores = jnp.exp2((scores - row_max) * (SCALE * LOG2E))
            return storing(low[slot], (here, slice(None)), exp_scores.astype(bf16))

        for start in range(0, SEQ, ROWS):
            pieces.append(functools.partial(normal, slice(start, start + ROWS)))
        return pieces

    def results(u):
        seq, head = units[u]
        slot = u % 2
        tokens = slice(seq * SEQ, (seq + 1) * SEQ)

        def context():
            v_all = v_ref[tokens, :]
            both = dot_nn(low[slot][...], jnp.concatenate([v_all, jnp.ones_like(v_all)], axis=1))
            scale = 1.0 / both[:, PAIR:]
            scale_ref[seq, head] = scale
            ctx = both[:, :PAIR] * scale
            if head == 1:
                ctx = jnp.where(heads[head], ctx, wide_ref[tokens, :])
                ctx_ref[tokens, :] = ctx.astype(bf16)
            wide_ref[tokens, :] = ctx

        def left():
            probs_ref[seq, head, :, :half] = dot_nn(low[slot][:, half:], flip).astype(bf16)

        def right():
            probs_ref[seq, head, :, half:] = dot_nn(low[slot][:, :half], flip).astype(bf16)

        return [context, left, right]

    count = len(units)
    for step in range(count + 2):
        matrix = products(step) if step < count else []
        if step >= 2:
            matrix = results(step - 2) + matrix
        vector = softmax(step - 1) if 1 <= step <= count else []
        weave(matrix, vector)


def attend(lengths, qkv, pos):
    qkv_block = lambda which: pl.BlockSpec((MICRO * SEQ, PAIR), lambda p, n: (0, which * PAIRS + p))
    pos_block = lambda which: pl.BlockSpec((SEQ, PAIR), lambda p, n: (0, which * PAIRS + p))
    square = lambda kind: [pltpu.VMEM((SEQ, SEQ), kind)] * 2
    return pl.pallas_call(
        attend_kernel,
        grid_spec=pltpu.PrefetchScalarGridSpec(
            num_scalar_prefetch=1,
            grid=(PAIRS,),
            in_specs=[qkv_block(0), qkv_block(1), qkv_block(2), pos_block(0), pos_block(1)],
            out_specs=[
                pl.BlockSpec((MICRO * SEQ, PAIR), lambda p, n: (0, p)),
                pl.BlockSpec((MICRO * SEQ, PAIR), lambda p, n: (0, p)),
                pl.BlockSpec((MICRO, 2, SEQ, SEQ), lambda p, n: (0, p, 0, 0)),
                pl.BlockSpec((MICRO, 2, SEQ, CHUNK), lambda p, n: (0, p, 0, 0)),
            ],
            scratch_shapes=square(bf16) + square(bf16) + square(f32) + square(bf16) + square(bf16),
        ),
        out_shape=[
            jax.ShapeDtypeStruct((MICRO * SEQ, D), bf16),
            jax.ShapeDtypeStruct((MICRO * SEQ, D), f32),
            jax.ShapeDtypeStruct((MICRO, HEADS, SEQ, SEQ), bf16),
            jax.ShapeDtypeStruct((MICRO, HEADS, SEQ, CHUNK), f32),
        ],
        compiler_params=pltpu.CompilerParams(vmem_limit_bytes=40 * 2**20),
        cost_estimate=pl.CostEstimate(
            flops=24 * 8 * 2 * SEQ * SEQ * PAIR,
            bytes_accessed=20 * 2**20,
            transcendentals=24 * SEQ * SEQ,
        ),
        name="attend",
    )(lengths, qkv, qkv, qkv, pos, pos)


def attend_back_kernel(
    earlier, q_ref, k_ref, v_ref, pq_ref, pk_ref, gc_ref, ctx_ref, probs_ref, scale_ref, *refs
):
    (
    gq_ref, gk_ref, gv_ref, gpq_ref, gpk_ref,
    raw_a, raw_b, grad_a, grad_b, moved_a, moved_b, turned_a, turned_b,
    inner_a, inner_b, q_t, k_t, gc_t, pq_t, pk_t, k_rev, v_rev, gq_t, gk_t, gv_t,
    ) = refs[earlier:]
    raw, grad, moved, turned = (raw_a, raw_b), (grad_a, grad_b), (moved_a, moved_b), (turned_a, turned_b)
    inner = (inner_a, inner_b)
    flip = flip_matrix()
    half = SEQ // 2
    lane_pair = lax.broadcasted_iota(jnp.int32, (1, PAIR), 1)
    rows = lax.broadcasted_iota(jnp.int32, (CHUNK, CHUNK), 0)
    cols = lax.broadcasted_iota(jnp.int32, (CHUNK, CHUNK), 1)
    below = cols <= rows
    units = [(seq, head) for seq in range(MICRO) for head in range(2)]
    heads = [
        (lane_pair >= head * HEAD) & (lane_pair < (head + 1) * HEAD) for head in range(2)
    ]
    tokens = [slice(seq * SEQ, (seq + 1) * SEQ) for seq in range(MICRO)]
    pq_t[...] = pq_ref[...].T
    pk_t[...] = pk_ref[...].T

    def prepare(seq):
        v_rev[seq] = reverse_rows(flip, v_ref[tokens[seq], :])
        k_flipped = reverse_rows(flip, k_ref[tokens[seq], :])
        k_t[seq] = k_flipped.T
        q_t[seq] = q_ref[tokens[seq], :].T
        scale = jnp.where(heads[0], scale_ref[seq, 0], scale_ref[seq, 1])
        gc_t[seq] = (gc_ref[tokens[seq], :].astype(f32) * scale).astype(bf16).T

    def grads(u):
        seq, head = units[u]
        slot = u % 2
        pieces = []

        def start():
            if head == 0:
                prepare(seq)
            product = gc_ref[tokens[seq], :].astype(f32) * ctx_ref[tokens[seq], :]
            product = jnp.where(heads[head], product, 0.0)
            inner[slot][...] = jnp.broadcast_to(
                jnp.sum(product, axis=1, keepdims=True), (SEQ, CHUNK)
            )

        pieces.append(start)
        for part in (slice(0, half), slice(half, SEQ)):
            def values(part=part):
                gc_all = gc_ref[tokens[seq], :]
                gc_head = jnp.where(heads[head], gc_all, jnp.zeros_like(gc_all))
                return storing(raw[slot], (slice(None), part), dot_nt(gc_head, v_rev[seq, part, :]))

            pieces.append(values)
        pieces.append(None)
        for c in range(SEQ // CHUNK):
            for r in range(0, CHUNK, ROWS):
                def softmax(here=slice(c * CHUNK + r, c * CHUNK + r + ROWS)):
                    low, scale = inner[slot][here, :], scale_ref[seq, head, here, :]
                    tiles = [
                        (
                            probs_ref[seq, head, here, t : t + CHUNK].astype(f32)
                            * ((raw[slot][here, t : t + CHUNK] - low) * scale)
                        ).astype(bf16)
                        for t in range(0, SEQ, CHUNK)
                    ]
                    return storing(grad[slot], (here, slice(None)), jnp.concatenate(tiles, axis=1))

                pieces.append(softmax)
        pieces.append(None)

        def shift(c):
            part = slice(c * CHUNK, (c + 1) * CHUNK)
            table = fold_edges(skew(grad[slot][part, :], c * CHUNK - 255), c, below)
            return storing(moved[slot], (part, slice(None)), table)

        def turn(c):
            part = slice(c * CHUNK, (c + 1) * CHUNK)
            table = fold_edges(skew(grad[slot][:, part].T, c * CHUNK - 255), c, below)
            return storing(turned[slot], (part, slice(None)), table)

        for c in range(SEQ // CHUNK):
            pieces += [functools.partial(turn, c), functools.partial(shift, c)]
        return pieces

    def results(u):
        seq, head = units[u]
        slot = u % 2
        mine = slice(head * HEAD, (head + 1) * HEAD)

        def values():
            gv_t[seq, mine, :] = dot_nn(gc_t[seq, mine, :], probs_ref[seq, head]).astype(bf16)

        def keys():
            total = dot_nn(q_t[seq, mine, :], grad[slot][...])
            total = total + dot_nt(pq_t[mine, :], turned[slot][...])
            gk_t[seq, mine, :] = (total * SCALE).astype(bf16)

        def queries():
            total = dot_nt(k_t[seq, mine, :], grad[slot][...])
            total = total + dot_nt(pk_t[mine, :], moved[slot][...])
            gq_t[seq, mine, :] = (total * SCALE).astype(bf16)

        def key_places():
            total = dot_nn(q_t[seq, mine, :], moved[slot][...]) * SCALE
            gpk_ref[mine, :] = total if seq == 0 else gpk_ref[mine, :] + total

        def query_places():
            total = dot_nn(k_t[seq, mine, :], turned[slot][...]) * SCALE
            gpq_ref[mine, :] = total if seq == 0 else gpq_ref[mine, :] + total

        def finish():
            gq_ref[tokens[seq], :] = gq_t[seq].T
            for kept, out in ((gk_t, gk_ref), (gv_t, gv_ref)):
                out[tokens[seq], :] = jnp.concatenate(
                    [
                        dot_nn(kept[seq, :, half:], flip).astype(bf16),
                        dot_nn(kept[seq, :, :half], flip).astype(bf16),
                    ],
                    axis=1,
                ).T

        pieces = [values, keys, queries, key_places, query_places]
        return pieces + [finish] if head == 1 else pieces

    count = len(units)
    for step in range(count + 1):
        matrix = results(step - 1) if step >= 1 else []
        vector = grads(step) if step < count else []
        weave(matrix, vector)


def attend_back(first, count, earlier, qkv, pos, grad_context, context_wide, probs, scale):
    qkv_block = lambda which: pl.BlockSpec((MICRO * SEQ, PAIR), lambda p: (0, which * PAIRS + first + p))
    pos_block = lambda which: pl.BlockSpec((SEQ, PAIR), lambda p: (0, which * PAIRS + first + p))
    token_block = pl.BlockSpec((MICRO * SEQ, PAIR), lambda p: (0, first + p))
    table_block = pl.BlockSpec((PAIR, SEQ), lambda p: (first + p, 0))
    token_shape = jax.ShapeDtypeStruct((MICRO * SEQ, D), bf16)
    table_shape = jax.ShapeDtypeStruct((D, SEQ), f32)
    square = lambda kind: [pltpu.VMEM((SEQ, SEQ), kind)] * 2
    wide = pltpu.VMEM((MICRO, PAIR, SEQ), bf16)
    tall = pltpu.VMEM((MICRO, SEQ, PAIR), bf16)
    return pl.pallas_call(
        functools.partial(attend_back_kernel, len(earlier)),
        grid=(count,),
        input_output_aliases={9 + i: i for i in range(len(earlier))},
        in_specs=[
            qkv_block(0), qkv_block(1), qkv_block(2), pos_block(0), pos_block(1),
            token_block, token_block,
            pl.BlockSpec((MICRO, 2, SEQ, SEQ), lambda p: (0, first + p, 0, 0)),
            pl.BlockSpec((MICRO, 2, SEQ, CHUNK), lambda p: (0, first + p, 0, 0)),
        ]
        + [pl.BlockSpec(memory_space=pl.ANY)] * len(earlier),
        out_specs=[token_block, token_block, token_block, table_block, table_block],
        out_shape=[token_shape, token_shape, token_shape, table_shape, table_shape],
        scratch_shapes=square(f32) + square(bf16) * 3
        + [pltpu.VMEM((SEQ, CHUNK), f32)] * 2
        + [wide, wide, wide, pltpu.VMEM((PAIR, SEQ), bf16), pltpu.VMEM((PAIR, SEQ), bf16)]
        + [tall, tall, wide, wide, wide],
        compiler_params=pltpu.CompilerParams(vmem_limit_bytes=56 * 2**20),
        cost_estimate=pl.CostEstimate(
            flops=count * 4 * 16 * 2 * SEQ * SEQ * PAIR, bytes_accessed=count * 4 * 2**20, transcendentals=0
        ),
        name="attend_back",
    )(qkv, qkv, qkv, pos, pos, grad_context, context_wide, probs, scale, *earlier)


def weigh_kernel(
    low_ref, x_ref, gq_ref, gk_ref, gv_ref, rel_ref, gpq_ref, gpk_ref, wq_ref, wk_ref,
    vec_ref, up_bias_ref,
    first_keep, first_send, second_keep, second_send, x_turned, rel_sum, rows_ref,
):
    step = pl.program_id(0)
    width = gq_ref.shape[1]
    count, rows = first_keep.shape[0], first_keep.shape[1]

    def put(keep, send, columns, value):
        value = value.astype(bf16).reshape(count, 2, rows, value.shape[1])
        lower, upper = value[:, 0], value[:, 1]
        is_upper = low_ref[0] == 1
        keep[:, :, columns] = jnp.where(is_upper, upper, lower)
        send[:, :, columns] = jnp.where(is_upper, lower, upper)

    def columns_at(start):
        return pl.ds(pl.multiple_of(start, width), width)

    @pl.when(step == 0)
    def begin():
        x_turned[...] = x_ref[...].T
        rel_sum[...] = jnp.zeros_like(rel_sum)
        rows_ref[...] = jnp.zeros_like(rows_ref)
        rows_ref[8:14, :] = vec_ref[...]
        rows_ref[14:18, :] = up_bias_ref[...]

    token_ones = jnp.ones((8, MICRO * SEQ), bf16)
    place_ones = jnp.ones((8, SEQ), bf16)
    row = lax.broadcasted_iota(jnp.int32, (8, width), 0)
    biases = jnp.zeros((8, width), f32)
    tables = ((gq_ref, gpq_ref, wq_ref), (gk_ref, gpk_ref, wk_ref))
    for which, (grad_ref, table_ref, weight_ref) in enumerate(tables):
        grad = grad_ref[...]
        table = table_ref[...].astype(bf16)
        total = dot_nn(x_turned[...], grad) + dot_nt(rel_ref[...], table)
        put(first_keep, first_send, columns_at(which * D + step * width), total)
        rel_sum[...] += dot_nn(weight_ref[...], table)
        bias = dot_nn(token_ones, grad) + dot_nt(place_ones, table)
        biases = jnp.where(row == which, bias, biases)
    grad = gv_ref[...]
    put(second_keep, second_send, columns_at(step * width), dot_nn(x_turned[...], grad))
    rows_ref[:8, columns_at(step * width)] = jnp.where(row == 2, dot_nn(token_ones, grad), biases)

    @pl.when(step == pl.num_programs(0) - 1)
    def end():
        put(second_keep, second_send, slice(D, D + SEQ), rel_sum[...])
        put(second_keep, second_send, slice(D + SEQ, D + SEQ + CHUNK), rows_ref[...].T)


def weigh(x, gq, gk, gv, gpq, gpk, first_pack, vectors):
    steps = 3
    width = D // steps
    whole = lambda shape: pl.BlockSpec(shape, lambda p, n: (0,) * len(shape))
    columns = lambda rows, skip=0: pl.BlockSpec((rows, width), lambda p, n: (0, skip // width + p))
    tokens = MICRO * SEQ
    size = lax.axis_size("wide")
    shapes = [(size // 2, D // size, cols) for cols in (2 * D, 2 * D, D + SEQ + CHUNK, D + SEQ + CHUNK)]
    return pl.pallas_call(
        weigh_kernel,
        grid_spec=pltpu.PrefetchScalarGridSpec(
            num_scalar_prefetch=1,
            grid=(steps,),
            in_specs=[
                whole((tokens, D)), columns(tokens), columns(tokens), columns(tokens),
                whole((D, SEQ)),
                pl.BlockSpec((width, SEQ), lambda p, n: (p, 0)),
                pl.BlockSpec((width, SEQ), lambda p, n: (p, 0)),
                columns(D, SEQ), columns(D, SEQ + D),
            ]
            + [whole((6, D)), whole((4, D))],
            out_specs=[whole(shape) for shape in shapes],
            scratch_shapes=[
                pltpu.VMEM((D, tokens), bf16), pltpu.VMEM((D, SEQ), f32), pltpu.VMEM((CHUNK, D), f32),
            ],
        ),
        out_shape=[jax.ShapeDtypeStruct(shape, bf16) for shape in shapes],
        compiler_params=pltpu.CompilerParams(vmem_limit_bytes=56 * 2**20),
        cost_estimate=pl.CostEstimate(
            flops=2 * D * D * (3 * tokens + 4 * SEQ), bytes_accessed=20 * 2**20, transcendentals=0
        ),
        name="weigh",
    )(my_bit(0).reshape(1), x, gq, gk, gv, first_pack, gpq, gpk, first_pack, first_pack, *vectors)


def feed_back_kernel(
    grad_ref, hidden_ref, slope_ref, down_ref, up_ref,
    grad_hidden_ref, grad_weight_ref, bias_ref, hidden_turned, grad_up,
):
    step = pl.program_id(0)

    @pl.when(step == 0)
    def begin():
        hidden_turned[...] = hidden_ref[...].T
        grad_hidden_ref[...] = jnp.zeros_like(grad_hidden_ref)

    for seq in range(MICRO):
        part = slice(seq * SEQ, (seq + 1) * SEQ)
        grad_act = dot_nt(grad_ref[part, :], down_ref[...])
        grad_up[part, :] = (grad_act * slope_ref[part, :].astype(f32)).astype(bf16)
    for seq in range(MICRO):
        part = slice(seq * SEQ, (seq + 1) * SEQ)
        grad_hidden_ref[part, :] += dot_nt(grad_up[part, :], up_ref[...])
    grad_weight_ref[...] = dot_nn(hidden_turned[...], grad_up[...]).astype(bf16)
    bias_ref[...] = dot_nn(jnp.ones((8, MICRO * SEQ), bf16), grad_up[...])


def feed_back(grad_feed, hidden_low, slope, down_full, second_pack):
    tokens = MICRO * SEQ
    blocks = slope.shape[1] // D
    whole = lambda shape: pl.BlockSpec(shape, lambda f: (0, 0))
    return pl.pallas_call(
        feed_back_kernel,
        grid=(blocks,),
        in_specs=[
            whole((tokens, D)), whole((tokens, D)),
            pl.BlockSpec((tokens, D), lambda f: (0, f)),
            pl.BlockSpec((D, D), lambda f: (f, 0)),
            pl.BlockSpec((D, D), lambda f: (0, 1 + f)),
        ],
        out_specs=[
            whole((tokens, D)),
            pl.BlockSpec((D, D), lambda f: (0, 1 + f)),
            pl.BlockSpec((8, D), lambda f: (0, f)),
        ],
        out_shape=[
            jax.ShapeDtypeStruct((tokens, D), f32),
            jax.ShapeDtypeStruct((D, (1 + blocks) * D), bf16),
            jax.ShapeDtypeStruct((8, blocks * D), f32),
        ],
        scratch_shapes=[pltpu.VMEM((D, tokens), bf16), pltpu.VMEM((tokens, D), bf16)],
        compiler_params=pltpu.CompilerParams(vmem_limit_bytes=56 * 2**20),
        cost_estimate=pl.CostEstimate(
            flops=6 * tokens * D * blocks * D, bytes_accessed=30 * 2**20, transcendentals=0
        ),
        name="feed_back",
    )(grad_feed, hidden_low, slope, down_full, second_pack)


def normalise(v):
    row_mean = jnp.mean(v, axis=-1, keepdims=True)
    centered = v - row_mean
    variance = jnp.mean(centered * centered, axis=-1, keepdims=True)
    rstd = lax.rsqrt(variance + norm_epsilon)
    return centered * rstd, rstd


def column_sums(values):
    return jnp.sum(values, axis=0)


def norm_back(normed, rstd, gain, grad):
    e = grad * gain
    grad_in = rstd * (
        e
        - jnp.mean(e, axis=-1, keepdims=True)
        - normed * jnp.mean(e * normed, axis=-1, keepdims=True)
    )
    return grad_in, column_sums(grad * normed), column_sums(grad)


def narrow_shifts(block, shift):
    size = lax.axis_size("narrow")
    return lax.ppermute(block, "narrow", [(i, (i + shift) % size) for i in range(size)])


def gather_rows(shard):
    size = lax.axis_size("narrow")
    me = lax.axis_index("narrow")
    rows, cols = shard.shape
    together = jnp.zeros((size * rows, cols), shard.dtype)
    for shift in range(size):
        block = narrow_shifts(shard, shift) if shift else shard
        owner = lax.rem(me - shift + size, size)
        together = lax.dynamic_update_slice(together, block, (owner * rows, 0))
    return lax.all_gather(together, "wide", axis=0, tiled=True)


def scatter_wide(full):
    return lax.psum_scatter(full, "wide", scatter_dimension=0, tiled=True)


def scatter_narrow_start(part):
    size = lax.axis_size("narrow")
    me = lax.axis_index("narrow")
    rows = part.shape[-2] // size
    pieces = []
    for shift in range(size):
        target = lax.rem(me + shift, size)
        block = lax.dynamic_slice_in_dim(part, target * rows, rows, part.ndim - 2)
        pieces.append(narrow_shifts(block, shift) if shift else block)
    return pieces


def scatter_narrow(part):
    return sum(piece.astype(f32) for piece in scatter_narrow_start(part))


def swap(block, bit):
    size = lax.axis_size("wide")
    return lax.ppermute(block, "wide", [(i, i ^ (1 << bit)) for i in range(size)])


def my_bit(bit):
    return lax.rem(lax.axis_index("wide") // (1 << bit), 2)


def wide_bits():
    return (lax.axis_size("wide") - 1).bit_length()


def split_bits(full):
    bits = wide_bits()
    return full.reshape((2,) * bits + (full.shape[0] >> bits, full.shape[1]))


def add_low(first, second):
    return (first.astype(f32) + second.astype(f32)).astype(bf16)


def two_halves(part, bit, left):
    axis, mine = left.index(bit), my_bit(bit)
    keep = lax.dynamic_index_in_dim(part, mine, axis, keepdims=False)
    send = lax.dynamic_index_in_dim(part, 1 - mine, axis, keepdims=False)
    left.remove(bit)
    return keep, send


def scatter_upper(part):
    size = lax.axis_size("wide")
    groups = [list(range(low, size, 2)) for low in range(2)]
    part = part.reshape(-1, part.shape[-1])
    return lax.psum_scatter(part, "wide", scatter_dimension=0, tiled=True, axis_index_groups=groups)


def halve(part, bit, left):
    keep, send = two_halves(part, bit, left)
    return add_low(keep, swap(send, bit))


def all_bits():
    return list(range(wide_bits()))[::-1]


def body(
    hidden_in, cotangent, seq_lengths,
    query_weight, query_bias, key_weight, key_bias, value_weight, value_bias,
    out_weight, out_bias, first_gain, first_shift, up_weight, up_bias,
    down_weight, down_bias, second_gain, second_shift, rel_table,
):
    tokens = MICRO * SEQ
    x = hidden_in.reshape(tokens, D)
    cot = cotangent.reshape(tokens, D).astype(f32)
    lengths = seq_lengths.reshape(MICRO)
    share = query_weight.shape[0]
    vectors = [
        query_bias, key_bias, value_bias, out_bias, first_gain, first_shift,
        down_bias, second_gain, second_shift,
    ]
    vectors += [up_bias[c * share : (c + 1) * share] for c in range(4)]
    places = lax.broadcasted_iota(jnp.int32, (VECTORS, share), 0)
    stacked = jnp.zeros((VECTORS, share), bf16)
    for place, vector in enumerate(vectors):
        stacked = jnp.where(places == place, vector[None, :], stacked)
    first_pack = gather_rows(
        jnp.concatenate(
            [rel_table.T, query_weight, key_weight, value_weight, stacked.T], axis=1
        )
    )
    second_pack = gather_rows(jnp.concatenate([out_weight, up_weight], axis=1))
    down_full = gather_rows(down_weight)
    qkv_weight = first_pack[:, SEQ : SEQ + 3 * D]
    rel_turned = first_pack[:, :SEQ]
    out_full = second_pack[:, :D]
    up_full = second_pack[:, D:]
    vector_rows = first_pack[:, SEQ + 3 * D :].T.astype(f32)
    qkv_bias = vector_rows[:3].reshape(3 * D)
    out_b, gain_1, shift_1, down_b, gain_2, shift_2 = (vector_rows[i] for i in range(3, 9))
    up_b = jnp.transpose(vector_rows[9:13].reshape(4, D // share, share), (1, 0, 2)).reshape(4 * D)

    qkv = (dot_nn(x, qkv_weight) + qkv_bias).astype(bf16)
    pos = (dot_tn(rel_turned, qkv_weight[:, : 2 * D]) + qkv_bias[: 2 * D]).astype(bf16)
    context, context_wide, probs, probs_scale = attend(lengths, qkv, pos)

    first_in = x.astype(f32) + dot_nn(context, out_full) + out_b
    normed_1, rstd_1 = normalise(first_in)
    hidden = normed_1 * gain_1 + shift_1
    hidden_low = hidden.astype(bf16)
    upward = dot_nn(hidden_low, up_full) + up_b
    cdf = 0.5 * (1.0 + lax.erf(upward * math.sqrt(0.5)))
    activated_low = (upward * cdf).astype(bf16)
    slope = (cdf + upward * jnp.exp(-0.5 * upward * upward) * (1 / math.sqrt(2 * math.pi))).astype(
        bf16
    )
    second_in = hidden + dot_nn(activated_low, down_full) + down_b
    normed_2, rstd_2 = normalise(second_in)
    hidden_out = (normed_2 * gain_2 + shift_2).astype(bf16)

    grad_second, grad_gain_2, grad_shift_2 = norm_back(normed_2, rstd_2, gain_2, cot)
    grad_feed = grad_second.astype(bf16)
    grad_down_bias = column_sums(grad_feed.astype(f32))
    grad_down = dot_tn(activated_low, grad_feed).astype(bf16)
    grad_hidden, grad_second_pack, grad_up_bias = feed_back(
        grad_feed, hidden_low, slope, down_full, second_pack
    )
    grad_up_bias = grad_up_bias[0]
    grad_hidden = grad_second + grad_hidden
    grad_first, grad_gain_1, grad_shift_1 = norm_back(normed_1, rstd_1, gain_1, grad_hidden)
    grad_branch = grad_first.astype(bf16)
    grad_out_bias = column_sums(grad_branch.astype(f32))
    grad_out = dot_tn(context, grad_branch).astype(bf16)
    grad_context = dot_nt(grad_branch, out_full).astype(bf16)

    grad_second_pack = lax.dynamic_update_slice(grad_second_pack, grad_out, (0, 0))
    down_part = scatter_wide(grad_down)
    keep, send = two_halves(split_bits(grad_second_pack), 0, all_bits())
    came = swap(send, 0)
    grad_context, keep, send = lax.optimization_barrier((grad_context, keep, send))
    inputs = (qkv, pos, grad_context, context_wide, probs, probs_scale)
    early = list(attend_back(0, EARLY, (), *inputs))
    early[0], keep, came, down_part = lax.optimization_barrier((early[0], keep, came, down_part))
    second_part = scatter_upper(add_low(keep, came))
    down_pieces = scatter_narrow_start(down_part)
    gq, gk, gv, gpq, gpk = attend_back(EARLY, PAIRS - EARLY, early, *inputs)
    grad_up_bias = jnp.transpose(grad_up_bias.reshape(D // share, 4, share), (1, 0, 2))
    vector_grads = jnp.concatenate(
        [grad_out_bias, grad_gain_1, grad_shift_1, grad_down_bias, grad_gain_2, grad_shift_2]
    )
    vector_grads = (vector_grads.reshape(6, D), grad_up_bias.reshape(4, D))
    gq, down_pieces = lax.optimization_barrier((gq, down_pieces))
    down_sum = sum(piece.astype(f32) for piece in down_pieces)
    first_keep, first_send, second_keep, second_send = weigh(
        x, gq, gk, gv, gpq, gpk, first_pack, vector_grads
    )
    first_keep, second_part = lax.optimization_barrier((first_keep, second_part))
    second_pieces = scatter_narrow_start(second_part)
    upper = all_bits()[:-1]
    sides = lambda part: part.reshape((2,) * len(upper) + part.shape[1:])
    halves = [
        [sides(add_low(first_keep, swap(first_send, 0))), all_bits()[:-1], list(upper)],
        [sides(add_low(second_keep, swap(second_send, 0))), all_bits()[:-1], upper[::-1]],
    ]

    def halve_both():
        for entry in halves:
            entry[0] = halve(entry[0], entry[2].pop(0), entry[1])

    def together(*others):
        kept = lax.optimization_barrier((halves[0][0], halves[1][0]) + others)
        halves[0][0], halves[1][0] = kept[:2]
        return kept[2:]

    gq, gk, gv = together(gq, gk, gv)
    grad_inputs = grad_first + dot_nt(jnp.concatenate([gq, gk, gv], axis=1), qkv_weight)
    halve_both()
    grad_inputs, *second_pieces = together(grad_inputs, *second_pieces)
    second_sum = sum(piece.astype(f32) for piece in second_pieces)
    while halves[0][2]:
        halve_both()
    last_sum = scatter_narrow(jnp.concatenate([halves[0][0], halves[1][0]], axis=1))
    turned = last_sum[:, 3 * D :].T
    vec = lambda i: turned[SEQ + i]
    return (
        hidden_out.reshape(hidden_in.shape),
        grad_inputs.reshape(hidden_in.shape),
        last_sum[:, :D], vec(0),
        last_sum[:, D : 2 * D], vec(1),
        last_sum[:, 2 * D : 3 * D], vec(2),
        second_sum[:, :D], vec(8), vec(9), vec(10),
        second_sum[:, D:],
        turned[SEQ + 14 : SEQ + 18].reshape(4 * share),
        down_sum, vec(11), vec(12), vec(13),
        turned[:SEQ],
    )


def solution(mesh):
    tokens = P(None, AXES, None, None)
    rows = P(AXES, None)
    vector = P(AXES)
    weights = (
        rows, vector, rows, vector, rows, vector, rows, vector, vector, vector,
        rows, vector, rows, vector, vector, vector, P(None, AXES),
    )
    return jax.shard_map(
        body,
        mesh=mesh,
        in_specs=(tokens, tokens, P(None, AXES)) + weights,
        out_specs=(tokens, tokens) + weights,
        check_vma=False,
    )
```

```python
import functools
import math

import jax
import jax.numpy as jnp
from jax import lax
from jax.experimental import pallas as pl
from jax.experimental.pallas import tpu as pltpu
from jax.sharding import PartitionSpec as P

D = 768
HEADS = 12
HEAD = 64
SEQ = 512
MICRO = 2
PAIR = 2 * HEAD
PAIRS = HEADS // 2
CHUNK = 128
ROWS = 32
DELAYS = (0, 1)
LOG2E = 1.4426950408889634
VECTORS = 128
EARLY = 3
SCALE = 1.0 / math.sqrt(3 * HEAD)
AXES = ("wide", "narrow")
norm_epsilon = 1e-06
bf16 = jnp.bfloat16
f32 = jnp.float32


def dot_nt(left, right):
    return lax.dot_general(left, right, (((1,), (1,)), ((), ())), preferred_element_type=f32)


def dot_nn(left, right):
    return lax.dot_general(left, right, (((1,), (0,)), ((), ())), preferred_element_type=f32)


def dot_tn(left, right):
    return lax.dot_general(left, right, (((0,), (0,)), ((), ())), preferred_element_type=f32)


def reverse_rows(flip, block):
    half = SEQ // 2
    return jnp.concatenate(
        [dot_nn(flip, block[half:]).astype(bf16), dot_nn(flip, block[:half]).astype(bf16)], axis=0
    )


def flip_matrix():
    half = SEQ // 2
    rows = lax.broadcasted_iota(jnp.int32, (half, half), 0)
    cols = lax.broadcasted_iota(jnp.int32, (half, half), 1)
    return jnp.where(rows + cols == half - 1, 1.0, 0.0).astype(bf16)


def skew(rows, base):
    return pltpu.roll(rows, base % SEQ, 1, stride=1, stride_axis=0)


def lane_tiles(block):
    return [block[:, t * CHUNK : (t + 1) * CHUNK] for t in range(SEQ // CHUNK)]


def clip_edges(moved, table, c, below):
    tiles = lane_tiles(moved)
    left = jnp.broadcast_to(table[:, :1], (CHUNK, CHUNK))
    right = jnp.broadcast_to(table[:, SEQ - 1 :], (CHUNK, CHUNK))
    if c == 0:
        tiles[2], tiles[3] = jnp.where(below, tiles[2], right), right
    elif c == 1:
        tiles[3] = jnp.where(below, tiles[3], right)
    elif c == 2:
        tiles[0] = jnp.where(below, left, tiles[0])
    else:
        tiles[0], tiles[1] = left, jnp.where(below, left, tiles[1])
    return jnp.concatenate(tiles, axis=1)


def fold_edges(moved, c, below):
    tiles = lane_tiles(moved)
    part = (2, 3, 0, 1)[c]
    zero = jnp.zeros_like(tiles[part])
    upper = c < 2
    if upper:
        outside, tiles[part] = jnp.where(below, zero, tiles[part]), jnp.where(below, tiles[part], zero)
    else:
        outside, tiles[part] = jnp.where(below, tiles[part], zero), jnp.where(below, zero, tiles[part])
    outside = [outside]
    if c in (0, 3):
        whole = 3 if c == 0 else 0
        outside.append(tiles[whole])
        tiles[whole] = zero
    edge, lane = (0, 0) if upper else (3, CHUNK - 1)
    outside = jnp.concatenate(outside, axis=1)
    lanes = lax.broadcasted_iota(jnp.int32, (outside.shape[1], CHUNK), 1)
    to_lane = jnp.where(lanes == lane, 1.0, 0.0).astype(bf16)
    tiles[edge] = tiles[edge] + dot_nn(outside, to_lane).astype(bf16)
    return jnp.concatenate(tiles, axis=1)


def weave(first, second):
    waiting = {0: [], 1: []}

    def emit(which, piece):
        store = piece() if piece is not None else None
        if store is not None:
            waiting[which].append(store)
        keep = DELAYS[which] if piece is not None else 0
        while len(waiting[which]) > keep:
            waiting[which].pop(0)()

    total = max(len(first), len(second))
    done = [0, 0]
    for step in range(1, total + 1):
        for which, pieces in ((1, second), (0, first)):
            while done[which] * total < step * len(pieces):
                emit(which, pieces[done[which]])
                done[which] += 1
    for which in (1, 0):
        emit(which, None)


def storing(ref, where, value):
    def store():
        ref[where] = value

    return store


def attend_kernel(
    len_ref, q_ref, k_ref, v_ref, pq_ref, pk_ref, ctx_ref, wide_ref, probs_ref, scale_ref,
    kp_a, kp_b, qp_a, qp_b, raw_a, raw_b, back_a, back_b, low_a, low_b,
):
    kp, qp, raw, back, low = (kp_a, kp_b), (qp_a, qp_b), (raw_a, raw_b), (back_a, back_b), (low_a, low_b)
    flip = flip_matrix()
    half = SEQ // 2
    lane_pair = lax.broadcasted_iota(jnp.int32, (1, PAIR), 1)
    rows = lax.broadcasted_iota(jnp.int32, (CHUNK, CHUNK), 0)
    cols = lax.broadcasted_iota(jnp.int32, (CHUNK, CHUNK), 1)
    strictly_below, below = cols < rows, cols <= rows
    places = lax.broadcasted_iota(jnp.int32, (1, SEQ), 1)
    pq_all = pq_ref[...]
    pk_flipped = reverse_rows(flip, pk_ref[...])
    units = [(seq, head) for seq in range(MICRO) for head in range(2)]
    heads = [
        (lane_pair >= head * HEAD) & (lane_pair < (head + 1) * HEAD) for head in range(2)
    ]
    hidden_keys = [jnp.where(places < len_ref[seq], 0.0, -1e30) for seq in range(MICRO)]

    def products(u):
        seq, head = units[u]
        slot = u % 2
        tokens = slice(seq * SEQ, (seq + 1) * SEQ)
        pieces = []
        for part in (slice(0, half), slice(half, SEQ)):
            def key_places(part=part):
                k_all = k_ref[tokens, :]
                k_head = jnp.where(heads[head], k_all, jnp.zeros_like(k_all))
                return storing(kp[slot], (slice(None), part), dot_nt(k_head, pq_all[part]).astype(bf16))

            def query_places(part=part):
                q_all = q_ref[tokens, :]
                q_head = jnp.where(heads[head], q_all, jnp.zeros_like(q_all))
                return storing(qp[slot], (slice(None), part), dot_nt(q_head, pk_flipped[part]).astype(bf16))

            def content(part=part):
                q_all = q_ref[tokens, :]
                q_head = jnp.where(heads[head], q_all, jnp.zeros_like(q_all))
                keys = slice(seq * SEQ + part.start, seq * SEQ + part.stop)
                return storing(raw[slot], (slice(None), part), dot_nt(q_head, k_ref[keys, :]))

            pieces += [key_places, query_places, content]
        return pieces

    def softmax(u):
        seq, head = units[u]
        slot = u % 2
        pieces = []
        for c in range(SEQ // CHUNK):
            def turn(c=c):
                part = slice(c * CHUNK, (c + 1) * CHUNK)
                table = kp[slot][part, :]
                moved = clip_edges(skew(table, c * CHUNK + 256), table, c, strictly_below)
                return storing(back[slot], (slice(None), part), moved.T)

            pieces.append(turn)
        for c in range(SEQ // CHUNK):
            def shift(c=c):
                part = slice(c * CHUNK, (c + 1) * CHUNK)
                table = qp[slot][part, :]
                return storing(
                    qp[slot], (part, slice(None)),
                    clip_edges(skew(table, c * CHUNK - 255), table, c, below),
                )

            pieces.append(shift)
        pieces.append(None)

        def normal(here):
            scores = (
                raw[slot][here, :]
                + (qp[slot][here, :].astype(f32) + back[slot][here, :].astype(f32))
                + hidden_keys[seq]
            )
            row_max = jnp.max(scores, axis=1, keepdims=True)
            exp_scores = jnp.exp2((scores - row_max) * (SCALE * LOG2E))
            return storing(low[slot], (here, slice(None)), exp_scores.astype(bf16))

        for start in range(0, SEQ, ROWS):
            pieces.append(functools.partial(normal, slice(start, start + ROWS)))
        return pieces

    def results(u):
        seq, head = units[u]
        slot = u % 2
        tokens = slice(seq * SEQ, (seq + 1) * SEQ)

        def context():
            v_all = v_ref[tokens, :]
            both = dot_nn(low[slot][...], jnp.concatenate([v_all, jnp.ones_like(v_all)], axis=1))
            scale = 1.0 / both[:, PAIR:]
            scale_ref[seq, head] = scale
            ctx = both[:, :PAIR] * scale
            if head == 1:
                ctx = jnp.where(heads[head], ctx, wide_ref[tokens, :])
                ctx_ref[tokens, :] = ctx.astype(bf16)
            wide_ref[tokens, :] = ctx

        def left():
            probs_ref[seq, head, :, :half] = dot_nn(low[slot][:, half:], flip).astype(bf16)

        def right():
            probs_ref[seq, head, :, half:] = dot_nn(low[slot][:, :half], flip).astype(bf16)

        return [context, left, right]

    count = len(units)
    for step in range(count + 2):
        matrix = products(step) if step < count else []
        if step >= 2:
            matrix = results(step - 2) + matrix
        vector = softmax(step - 1) if 1 <= step <= count else []
        weave(matrix, vector)


def attend(lengths, qkv, pos):
    qkv_block = lambda which: pl.BlockSpec((MICRO * SEQ, PAIR), lambda p, n: (0, which * PAIRS + p))
    pos_block = lambda which: pl.BlockSpec((SEQ, PAIR), lambda p, n: (0, which * PAIRS + p))
    square = lambda kind: [pltpu.VMEM((SEQ, SEQ), kind)] * 2
    return pl.pallas_call(
        attend_kernel,
        grid_spec=pltpu.PrefetchScalarGridSpec(
            num_scalar_prefetch=1,
            grid=(PAIRS,),
            in_specs=[qkv_block(0), qkv_block(1), qkv_block(2), pos_block(0), pos_block(1)],
            out_specs=[
                pl.BlockSpec((MICRO * SEQ, PAIR), lambda p, n: (0, p)),
                pl.BlockSpec((MICRO * SEQ, PAIR), lambda p, n: (0, p)),
                pl.BlockSpec((MICRO, 2, SEQ, SEQ), lambda p, n: (0, p, 0, 0)),
                pl.BlockSpec((MICRO, 2, SEQ, CHUNK), lambda p, n: (0, p, 0, 0)),
            ],
            scratch_shapes=square(bf16) + square(bf16) + square(f32) + square(bf16) + square(bf16),
        ),
        out_shape=[
            jax.ShapeDtypeStruct((MICRO * SEQ, D), bf16),
            jax.ShapeDtypeStruct((MICRO * SEQ, D), f32),
            jax.ShapeDtypeStruct((MICRO, HEADS, SEQ, SEQ), bf16),
            jax.ShapeDtypeStruct((MICRO, HEADS, SEQ, CHUNK), f32),
        ],
        compiler_params=pltpu.CompilerParams(vmem_limit_bytes=40 * 2**20),
        cost_estimate=pl.CostEstimate(
            flops=24 * 8 * 2 * SEQ * SEQ * PAIR,
            bytes_accessed=20 * 2**20,
            transcendentals=24 * SEQ * SEQ,
        ),
        name="attend",
    )(lengths, qkv, qkv, qkv, pos, pos)


def attend_back_kernel(
    earlier, q_ref, k_ref, v_ref, pq_ref, pk_ref, gc_ref, ctx_ref, probs_ref, scale_ref, *refs
):
    (
    gq_ref, gk_ref, gv_ref, gpq_ref, gpk_ref,
    raw_a, raw_b, grad_a, grad_b, moved_a, moved_b, turned_a, turned_b,
    inner_a, inner_b, q_t, k_t, gc_t, pq_t, pk_t, k_rev, v_rev, gq_t, gk_t, gv_t,
    ) = refs[earlier:]
    raw, grad, moved, turned = (raw_a, raw_b), (grad_a, grad_b), (moved_a, moved_b), (turned_a, turned_b)
    inner = (inner_a, inner_b)
    flip = flip_matrix()
    half = SEQ // 2
    lane_pair = lax.broadcasted_iota(jnp.int32, (1, PAIR), 1)
    rows = lax.broadcasted_iota(jnp.int32, (CHUNK, CHUNK), 0)
    cols = lax.broadcasted_iota(jnp.int32, (CHUNK, CHUNK), 1)
    below = cols <= rows
    units = [(seq, head) for seq in range(MICRO) for head in range(2)]
    heads = [
        (lane_pair >= head * HEAD) & (lane_pair < (head + 1) * HEAD) for head in range(2)
    ]
    tokens = [slice(seq * SEQ, (seq + 1) * SEQ) for seq in range(MICRO)]
    pq_t[...] = pq_ref[...].T
    pk_t[...] = pk_ref[...].T

    def prepare(seq):
        v_rev[seq] = reverse_rows(flip, v_ref[tokens[seq], :])
        k_flipped = reverse_rows(flip, k_ref[tokens[seq], :])
        k_t[seq] = k_flipped.T
        q_t[seq] = q_ref[tokens[seq], :].T
        scale = jnp.where(heads[0], scale_ref[seq, 0], scale_ref[seq, 1])
        gc_t[seq] = (gc_ref[tokens[seq], :].astype(f32) * scale).astype(bf16).T

    def grads(u):
        seq, head = units[u]
        slot = u % 2
        pieces = []

        def start():
            if head == 0:
                prepare(seq)
            product = gc_ref[tokens[seq], :].astype(f32) * ctx_ref[tokens[seq], :]
            product = jnp.where(heads[head], product, 0.0)
            inner[slot][...] = jnp.broadcast_to(
                jnp.sum(product, axis=1, keepdims=True), (SEQ, CHUNK)
            )

        pieces.append(start)
        for part in (slice(0, half), slice(half, SEQ)):
            def values(part=part):
                gc_all = gc_ref[tokens[seq], :]
                gc_head = jnp.where(heads[head], gc_all, jnp.zeros_like(gc_all))
                return storing(raw[slot], (slice(None), part), dot_nt(gc_head, v_rev[seq, part, :]))

            pieces.append(values)
        pieces.append(None)
        for c in range(SEQ // CHUNK):
            for r in range(0, CHUNK, ROWS):
                def softmax(here=slice(c * CHUNK + r, c * CHUNK + r + ROWS)):
                    low, scale = inner[slot][here, :], scale_ref[seq, head, here, :]
                    tiles = [
                        (
                            probs_ref[seq, head, here, t : t + CHUNK].astype(f32)
                            * ((raw[slot][here, t : t + CHUNK] - low) * scale)
                        ).astype(bf16)
                        for t in range(0, SEQ, CHUNK)
                    ]
                    return storing(grad[slot], (here, slice(None)), jnp.concatenate(tiles, axis=1))

                pieces.append(softmax)
        pieces.append(None)

        def shift(c):
            part = slice(c * CHUNK, (c + 1) * CHUNK)
            table = fold_edges(skew(grad[slot][part, :], c * CHUNK - 255), c, below)
            return storing(moved[slot], (part, slice(None)), table)

        def turn(c):
            part = slice(c * CHUNK, (c + 1) * CHUNK)
            table = fold_edges(skew(grad[slot][:, part].T, c * CHUNK - 255), c, below)
            return storing(turned[slot], (part, slice(None)), table)

        for c in range(SEQ // CHUNK):
            pieces += [functools.partial(turn, c), functools.partial(shift, c)]
        return pieces

    def results(u):
        seq, head = units[u]
        slot = u % 2
        mine = slice(head * HEAD, (head + 1) * HEAD)

        def values():
            gv_t[seq, mine, :] = dot_nn(gc_t[seq, mine, :], probs_ref[seq, head]).astype(bf16)

        def keys():
            total = dot_nn(q_t[seq, mine, :], grad[slot][...])
            total = total + dot_nt(pq_t[mine, :], turned[slot][...])
            gk_t[seq, mine, :] = (total * SCALE).astype(bf16)

        def queries():
            total = dot_nt(k_t[seq, mine, :], grad[slot][...])
            total = total + dot_nt(pk_t[mine, :], moved[slot][...])
            gq_t[seq, mine, :] = (total * SCALE).astype(bf16)

        def key_places():
            total = dot_nn(q_t[seq, mine, :], moved[slot][...]) * SCALE
            gpk_ref[mine, :] = total if seq == 0 else gpk_ref[mine, :] + total

        def query_places():
            total = dot_nn(k_t[seq, mine, :], turned[slot][...]) * SCALE
            gpq_ref[mine, :] = total if seq == 0 else gpq_ref[mine, :] + total

        def finish():
            gq_ref[tokens[seq], :] = gq_t[seq].T
            for kept, out in ((gk_t, gk_ref), (gv_t, gv_ref)):
                out[tokens[seq], :] = jnp.concatenate(
                    [
                        dot_nn(kept[seq, :, half:], flip).astype(bf16),
                        dot_nn(kept[seq, :, :half], flip).astype(bf16),
                    ],
                    axis=1,
                ).T

        pieces = [values, keys, queries, key_places, query_places]
        return pieces + [finish] if head == 1 else pieces

    count = len(units)
    for step in range(count + 1):
        matrix = results(step - 1) if step >= 1 else []
        vector = grads(step) if step < count else []
        weave(matrix, vector)


def attend_back(first, count, earlier, qkv, pos, grad_context, context_wide, probs, scale):
    qkv_block = lambda which: pl.BlockSpec((MICRO * SEQ, PAIR), lambda p: (0, which * PAIRS + first + p))
    pos_block = lambda which: pl.BlockSpec((SEQ, PAIR), lambda p: (0, which * PAIRS + first + p))
    token_block = pl.BlockSpec((MICRO * SEQ, PAIR), lambda p: (0, first + p))
    table_block = pl.BlockSpec((PAIR, SEQ), lambda p: (first + p, 0))
    token_shape = jax.ShapeDtypeStruct((MICRO * SEQ, D), bf16)
    table_shape = jax.ShapeDtypeStruct((D, SEQ), f32)
    square = lambda kind: [pltpu.VMEM((SEQ, SEQ), kind)] * 2
    wide = pltpu.VMEM((MICRO, PAIR, SEQ), bf16)
    tall = pltpu.VMEM((MICRO, SEQ, PAIR), bf16)
    return pl.pallas_call(
        functools.partial(attend_back_kernel, len(earlier)),
        grid=(count,),
        input_output_aliases={9 + i: i for i in range(len(earlier))},
        in_specs=[
            qkv_block(0), qkv_block(1), qkv_block(2), pos_block(0), pos_block(1),
            token_block, token_block,
            pl.BlockSpec((MICRO, 2, SEQ, SEQ), lambda p: (0, first + p, 0, 0)),
            pl.BlockSpec((MICRO, 2, SEQ, CHUNK), lambda p: (0, first + p, 0, 0)),
        ]
        + [pl.BlockSpec(memory_space=pl.ANY)] * len(earlier),
        out_specs=[token_block, token_block, token_block, table_block, table_block],
        out_shape=[token_shape, token_shape, token_shape, table_shape, table_shape],
        scratch_shapes=square(f32) + square(bf16) * 3
        + [pltpu.VMEM((SEQ, CHUNK), f32)] * 2
        + [wide, wide, wide, pltpu.VMEM((PAIR, SEQ), bf16), pltpu.VMEM((PAIR, SEQ), bf16)]
        + [tall, tall, wide, wide, wide],
        compiler_params=pltpu.CompilerParams(vmem_limit_bytes=56 * 2**20),
        cost_estimate=pl.CostEstimate(
            flops=count * 4 * 16 * 2 * SEQ * SEQ * PAIR, bytes_accessed=count * 4 * 2**20, transcendentals=0
        ),
        name="attend_back",
    )(qkv, qkv, qkv, pos, pos, grad_context, context_wide, probs, scale, *earlier)


def weigh_kernel(
    low_ref, x_ref, gq_ref, gk_ref, gv_ref, rel_ref, gpq_ref, gpk_ref, wq_ref, wk_ref,
    vec_ref, up_bias_ref,
    first_keep, first_send, second_keep, second_send, x_turned, rel_sum, rows_ref,
):
    step = pl.program_id(0)
    width = gq_ref.shape[1]
    count, rows = first_keep.shape[0], first_keep.shape[1]

    def put(keep, send, columns, value):
        value = value.astype(bf16).reshape(count, 2, rows, value.shape[1])
        lower, upper = value[:, 0], value[:, 1]
        is_upper = low_ref[0] == 1
        keep[:, :, columns] = jnp.where(is_upper, upper, lower)
        send[:, :, columns] = jnp.where(is_upper, lower, upper)

    def columns_at(start):
        return pl.ds(pl.multiple_of(start, width), width)

    @pl.when(step == 0)
    def begin():
        x_turned[...] = x_ref[...].T
        rel_sum[...] = jnp.zeros_like(rel_sum)
        rows_ref[...] = jnp.zeros_like(rows_ref)
        rows_ref[8:14, :] = vec_ref[...]
        rows_ref[14:18, :] = up_bias_ref[...]

    token_ones = jnp.ones((8, MICRO * SEQ), bf16)
    place_ones = jnp.ones((8, SEQ), bf16)
    row = lax.broadcasted_iota(jnp.int32, (8, width), 0)
    biases = jnp.zeros((8, width), f32)
    tables = ((gq_ref, gpq_ref, wq_ref), (gk_ref, gpk_ref, wk_ref))
    for which, (grad_ref, table_ref, weight_ref) in enumerate(tables):
        grad = grad_ref[...]
        table = table_ref[...].astype(bf16)
        total = dot_nn(x_turned[...], grad) + dot_nt(rel_ref[...], table)
        put(first_keep, first_send, columns_at(which * D + step * width), total)
        rel_sum[...] += dot_nn(weight_ref[...], table)
        bias = dot_nn(token_ones, grad) + dot_nt(place_ones, table)
        biases = jnp.where(row == which, bias, biases)
    grad = gv_ref[...]
    put(second_keep, second_send, columns_at(step * width), dot_nn(x_turned[...], grad))
    rows_ref[:8, columns_at(step * width)] = jnp.where(row == 2, dot_nn(token_ones, grad), biases)

    @pl.when(step == pl.num_programs(0) - 1)
    def end():
        put(second_keep, second_send, slice(D, D + SEQ), rel_sum[...])
        put(second_keep, second_send, slice(D + SEQ, D + SEQ + CHUNK), rows_ref[...].T)


def weigh(x, gq, gk, gv, gpq, gpk, first_pack, vectors):
    steps = 3
    width = D // steps
    whole = lambda shape: pl.BlockSpec(shape, lambda p, n: (0,) * len(shape))
    columns = lambda rows, skip=0: pl.BlockSpec((rows, width), lambda p, n: (0, skip // width + p))
    tokens = MICRO * SEQ
    size = lax.axis_size("wide")
    shapes = [(size // 2, D // size, cols) for cols in (2 * D, 2 * D, D + SEQ + CHUNK, D + SEQ + CHUNK)]
    return pl.pallas_call(
        weigh_kernel,
        grid_spec=pltpu.PrefetchScalarGridSpec(
            num_scalar_prefetch=1,
            grid=(steps,),
            in_specs=[
                whole((tokens, D)), columns(tokens), columns(tokens), columns(tokens),
                whole((D, SEQ)),
                pl.BlockSpec((width, SEQ), lambda p, n: (p, 0)),
                pl.BlockSpec((width, SEQ), lambda p, n: (p, 0)),
                columns(D, SEQ), columns(D, SEQ + D),
            ]
            + [whole((6, D)), whole((4, D))],
            out_specs=[whole(shape) for shape in shapes],
            scratch_shapes=[
                pltpu.VMEM((D, tokens), bf16), pltpu.VMEM((D, SEQ), f32), pltpu.VMEM((CHUNK, D), f32),
            ],
        ),
        out_shape=[jax.ShapeDtypeStruct(shape, bf16) for shape in shapes],
        compiler_params=pltpu.CompilerParams(vmem_limit_bytes=56 * 2**20),
        cost_estimate=pl.CostEstimate(
            flops=2 * D * D * (3 * tokens + 4 * SEQ), bytes_accessed=20 * 2**20, transcendentals=0
        ),
        name="weigh",
    )(my_bit(0).reshape(1), x, gq, gk, gv, first_pack, gpq, gpk, first_pack, first_pack, *vectors)


def feed_back_kernel(
    grad_ref, hidden_ref, slope_ref, down_ref, up_ref,
    grad_hidden_ref, grad_weight_ref, bias_ref, hidden_turned, grad_up,
):
    step = pl.program_id(0)

    @pl.when(step == 0)
    def begin():
        hidden_turned[...] = hidden_ref[...].T
        grad_hidden_ref[...] = jnp.zeros_like(grad_hidden_ref)

    for seq in range(MICRO):
        part = slice(seq * SEQ, (seq + 1) * SEQ)
        grad_act = dot_nt(grad_ref[part, :], down_ref[...])
        grad_up[part, :] = (grad_act * slope_ref[part, :].astype(f32)).astype(bf16)
    for seq in range(MICRO):
        part = slice(seq * SEQ, (seq + 1) * SEQ)
        grad_hidden_ref[part, :] += dot_nt(grad_up[part, :], up_ref[...])
    grad_weight_ref[...] = dot_nn(hidden_turned[...], grad_up[...]).astype(bf16)
    bias_ref[...] = dot_nn(jnp.ones((8, MICRO * SEQ), bf16), grad_up[...])


def feed_back(grad_feed, hidden_low, slope, down_full, second_pack):
    tokens = MICRO * SEQ
    blocks = slope.shape[1] // D
    whole = lambda shape: pl.BlockSpec(shape, lambda f: (0, 0))
    return pl.pallas_call(
        feed_back_kernel,
        grid=(blocks,),
        in_specs=[
            whole((tokens, D)), whole((tokens, D)),
            pl.BlockSpec((tokens, D), lambda f: (0, f)),
            pl.BlockSpec((D, D), lambda f: (f, 0)),
            pl.BlockSpec((D, D), lambda f: (0, 1 + f)),
        ],
        out_specs=[
            whole((tokens, D)),
            pl.BlockSpec((D, D), lambda f: (0, 1 + f)),
            pl.BlockSpec((8, D), lambda f: (0, f)),
        ],
        out_shape=[
            jax.ShapeDtypeStruct((tokens, D), f32),
            jax.ShapeDtypeStruct((D, (1 + blocks) * D), bf16),
            jax.ShapeDtypeStruct((8, blocks * D), f32),
        ],
        scratch_shapes=[pltpu.VMEM((D, tokens), bf16), pltpu.VMEM((tokens, D), bf16)],
        compiler_params=pltpu.CompilerParams(vmem_limit_bytes=56 * 2**20),
        cost_estimate=pl.CostEstimate(
            flops=6 * tokens * D * blocks * D, bytes_accessed=30 * 2**20, transcendentals=0
        ),
        name="feed_back",
    )(grad_feed, hidden_low, slope, down_full, second_pack)


def normalise(v):
    row_mean = jnp.mean(v, axis=-1, keepdims=True)
    centered = v - row_mean
    variance = jnp.mean(centered * centered, axis=-1, keepdims=True)
    rstd = lax.rsqrt(variance + norm_epsilon)
    return centered * rstd, rstd


def column_sums(values):
    return jnp.sum(values, axis=0)


def norm_back(normed, rstd, gain, grad):
    e = grad * gain
    grad_in = rstd * (
        e
        - jnp.mean(e, axis=-1, keepdims=True)
        - normed * jnp.mean(e * normed, axis=-1, keepdims=True)
    )
    return grad_in, column_sums(grad * normed), column_sums(grad)


def narrow_shifts(block, shift):
    size = lax.axis_size("narrow")
    return lax.ppermute(block, "narrow", [(i, (i + shift) % size) for i in range(size)])


def gather_rows(shard):
    size = lax.axis_size("narrow")
    me = lax.axis_index("narrow")
    rows, cols = shard.shape
    together = jnp.zeros((size * rows, cols), shard.dtype)
    for shift in range(size):
        block = narrow_shifts(shard, shift) if shift else shard
        owner = lax.rem(me - shift + size, size)
        together = lax.dynamic_update_slice(together, block, (owner * rows, 0))
    return lax.all_gather(together, "wide", axis=0, tiled=True)


def scatter_wide(full):
    return lax.psum_scatter(full, "wide", scatter_dimension=0, tiled=True)


def scatter_narrow_start(part):
    size = lax.axis_size("narrow")
    me = lax.axis_index("narrow")
    rows = part.shape[-2] // size
    pieces = []
    for shift in range(size):
        target = lax.rem(me + shift, size)
        block = lax.dynamic_slice_in_dim(part, target * rows, rows, part.ndim - 2)
        pieces.append(narrow_shifts(block, shift) if shift else block)
    return pieces


def scatter_narrow(part):
    return sum(piece.astype(f32) for piece in scatter_narrow_start(part))


def swap(block, bit):
    size = lax.axis_size("wide")
    return lax.ppermute(block, "wide", [(i, i ^ (1 << bit)) for i in range(size)])


def my_bit(bit):
    return lax.rem(lax.axis_index("wide") // (1 << bit), 2)


def wide_bits():
    return (lax.axis_size("wide") - 1).bit_length()


def split_bits(full):
    bits = wide_bits()
    return full.reshape((2,) * bits + (full.shape[0] >> bits, full.shape[1]))


def add_low(first, second):
    return (first.astype(f32) + second.astype(f32)).astype(bf16)


def two_halves(part, bit, left):
    axis, mine = left.index(bit), my_bit(bit)
    keep = lax.dynamic_index_in_dim(part, mine, axis, keepdims=False)
    send = lax.dynamic_index_in_dim(part, 1 - mine, axis, keepdims=False)
    left.remove(bit)
    return keep, send


def scatter_upper(part):
    size = lax.axis_size("wide")
    groups = [list(range(low, size, 2)) for low in range(2)]
    part = part.reshape(-1, part.shape[-1])
    return lax.psum_scatter(part, "wide", scatter_dimension=0, tiled=True, axis_index_groups=groups)


def halve(part, bit, left):
    keep, send = two_halves(part, bit, left)
    return add_low(keep, swap(send, bit))


def all_bits():
    return list(range(wide_bits()))[::-1]


def body(
    hidden_in, cotangent, seq_lengths,
    query_weight, query_bias, key_weight, key_bias, value_weight, value_bias,
    out_weight, out_bias, first_gain, first_shift, up_weight, up_bias,
    down_weight, down_bias, second_gain, second_shift, rel_table,
):
    tokens = MICRO * SEQ
    x = hidden_in.reshape(tokens, D)
    cot = cotangent.reshape(tokens, D).astype(f32)
    lengths = seq_lengths.reshape(MICRO)
    share = query_weight.shape[0]
    vectors = [
        query_bias, key_bias, value_bias, out_bias, first_gain, first_shift,
        down_bias, second_gain, second_shift,
    ]
    vectors += [up_bias[c * share : (c + 1) * share] for c in range(4)]
    places = lax.broadcasted_iota(jnp.int32, (VECTORS, share), 0)
    stacked = jnp.zeros((VECTORS, share), bf16)
    for place, vector in enumerate(vectors):
        stacked = jnp.where(places == place, vector[None, :], stacked)
    first_pack = gather_rows(
        jnp.concatenate(
            [rel_table.T, query_weight, key_weight, value_weight, stacked.T], axis=1
        )
    )
    second_pack = gather_rows(jnp.concatenate([out_weight, up_weight], axis=1))
    down_full = gather_rows(down_weight)
    qkv_weight = first_pack[:, SEQ : SEQ + 3 * D]
    rel_turned = first_pack[:, :SEQ]
    out_full = second_pack[:, :D]
    up_full = second_pack[:, D:]
    vector_rows = first_pack[:, SEQ + 3 * D :].T.astype(f32)
    qkv_bias = vector_rows[:3].reshape(3 * D)
    out_b, gain_1, shift_1, down_b, gain_2, shift_2 = (vector_rows[i] for i in range(3, 9))
    up_b = jnp.transpose(vector_rows[9:13].reshape(4, D // share, share), (1, 0, 2)).reshape(4 * D)

    qkv = (dot_nn(x, qkv_weight) + qkv_bias).astype(bf16)
    pos = (dot_tn(rel_turned, qkv_weight[:, : 2 * D]) + qkv_bias[: 2 * D]).astype(bf16)
    context, context_wide, probs, probs_scale = attend(lengths, qkv, pos)

    first_in = x.astype(f32) + dot_nn(context, out_full) + out_b
    normed_1, rstd_1 = normalise(first_in)
    hidden = normed_1 * gain_1 + shift_1
    hidden_low = hidden.astype(bf16)
    upward = dot_nn(hidden_low, up_full) + up_b
    cdf = 0.5 * (1.0 + lax.erf(upward * math.sqrt(0.5)))
    activated_low = (upward * cdf).astype(bf16)
    slope = (cdf + upward * jnp.exp(-0.5 * upward * upward) * (1 / math.sqrt(2 * math.pi))).astype(
        bf16
    )
    second_in = hidden + dot_nn(activated_low, down_full) + down_b
    normed_2, rstd_2 = normalise(second_in)
    hidden_out = (normed_2 * gain_2 + shift_2).astype(bf16)

    grad_second, grad_gain_2, grad_shift_2 = norm_back(normed_2, rstd_2, gain_2, cot)
    grad_feed = grad_second.astype(bf16)
    grad_down_bias = column_sums(grad_feed.astype(f32))
    grad_down = dot_tn(activated_low, grad_feed).astype(bf16)
    grad_hidden, grad_second_pack, grad_up_bias = feed_back(
        grad_feed, hidden_low, slope, down_full, second_pack
    )
    grad_up_bias = grad_up_bias[0]
    grad_hidden = grad_second + grad_hidden
    grad_first, grad_gain_1, grad_shift_1 = norm_back(normed_1, rstd_1, gain_1, grad_hidden)
    grad_branch = grad_first.astype(bf16)
    grad_out_bias = column_sums(grad_branch.astype(f32))
    grad_out = dot_tn(context, grad_branch).astype(bf16)
    grad_context = dot_nt(grad_branch, out_full).astype(bf16)

    grad_second_pack = lax.dynamic_update_slice(grad_second_pack, grad_out, (0, 0))
    down_part = scatter_wide(grad_down)
    keep, send = two_halves(split_bits(grad_second_pack), 0, all_bits())
    came = swap(send, 0)
    grad_context, keep, send = lax.optimization_barrier((grad_context, keep, send))
    inputs = (qkv, pos, grad_context, context_wide, probs, probs_scale)
    early = list(attend_back(0, EARLY, (), *inputs))
    early[0], keep, came, down_part = lax.optimization_barrier((early[0], keep, came, down_part))
    second_part = scatter_upper(add_low(keep, came))
    down_pieces = scatter_narrow_start(down_part)
    gq, gk, gv, gpq, gpk = attend_back(EARLY, PAIRS - EARLY, early, *inputs)
    grad_up_bias = jnp.transpose(grad_up_bias.reshape(D // share, 4, share), (1, 0, 2))
    vector_grads = jnp.concatenate(
        [grad_out_bias, grad_gain_1, grad_shift_1, grad_down_bias, grad_gain_2, grad_shift_2]
    )
    vector_grads = (vector_grads.reshape(6, D), grad_up_bias.reshape(4, D))
    gq, down_pieces = lax.optimization_barrier((gq, down_pieces))
    down_sum = sum(piece.astype(f32) for piece in down_pieces)
    first_keep, first_send, second_keep, second_send = weigh(
        x, gq, gk, gv, gpq, gpk, first_pack, vector_grads
    )
    first_keep, second_part = lax.optimization_barrier((first_keep, second_part))
    second_pieces = scatter_narrow_start(second_part)
    upper = all_bits()[:-1]
    sides = lambda part: part.reshape((2,) * len(upper) + part.shape[1:])
    halves = [
        [sides(add_low(first_keep, swap(first_send, 0))), all_bits()[:-1], list(upper)],
        [sides(add_low(second_keep, swap(second_send, 0))), all_bits()[:-1], upper[::-1]],
    ]

    def halve_both():
        for entry in halves:
            entry[0] = halve(entry[0], entry[2].pop(0), entry[1])

    def together(*others):
        kept = lax.optimization_barrier((halves[0][0], halves[1][0]) + others)
        halves[0][0], halves[1][0] = kept[:2]
        return kept[2:]

    gq, gk, gv = together(gq, gk, gv)
    grad_inputs = grad_first + dot_nt(jnp.concatenate([gq, gk, gv], axis=1), qkv_weight)
    halve_both()
    grad_inputs, *second_pieces = together(grad_inputs, *second_pieces)
    second_sum = sum(piece.astype(f32) for piece in second_pieces)
    while halves[0][2]:
        halve_both()
    last_sum = scatter_narrow(jnp.concatenate([halves[0][0], halves[1][0]], axis=1))
    turned = last_sum[:, 3 * D :].T
    vec = lambda i: turned[SEQ + i]
    return (
        hidden_out.reshape(hidden_in.shape),
        grad_inputs.reshape(hidden_in.shape),
        last_sum[:, :D], vec(0),
        last_sum[:, D : 2 * D], vec(1),
        last_sum[:, 2 * D : 3 * D], vec(2),
        second_sum[:, :D], vec(8), vec(9), vec(10),
        second_sum[:, D:],
        turned[SEQ + 14 : SEQ + 18].reshape(4 * share),
        down_sum, vec(11), vec(12), vec(13),
        turned[:SEQ],
    )


def solution(mesh):
    tokens = P(None, AXES, None, None)
    rows = P(AXES, None)
    vector = P(AXES)
    weights = (
        rows, vector, rows, vector, rows, vector, rows, vector, vector, vector,
        rows, vector, rows, vector, vector, vector, P(None, AXES),
    )
    return jax.shard_map(
        body,
        mesh=mesh,
        in_specs=(tokens, tokens, P(None, AXES)) + weights,
        out_specs=(tokens, tokens) + weights,
        check_vma=False,
    )
```

```python
import functools
import math

import jax
import jax.numpy as jnp
from jax import lax
from jax.experimental import pallas as pl
from jax.experimental.pallas import tpu as pltpu
from jax.sharding import PartitionSpec as P

D = 768
HEADS = 12
HEAD = 64
SEQ = 512
MICRO = 2
PAIR = 2 * HEAD
PAIRS = HEADS // 2
CHUNK = 128
ROWS = 32
DELAYS = (0, 1)
LOG2E = 1.4426950408889634
VECTORS = 128
EARLY = 3
SCALE = 1.0 / math.sqrt(3 * HEAD)
AXES = ("wide", "narrow")
norm_epsilon = 1e-06
bf16 = jnp.bfloat16
f32 = jnp.float32


def dot_nt(left, right):
    return lax.dot_general(left, right, (((1,), (1,)), ((), ())), preferred_element_type=f32)


def dot_nn(left, right):
    return lax.dot_general(left, right, (((1,), (0,)), ((), ())), preferred_element_type=f32)


def dot_tn(left, right):
    return lax.dot_general(left, right, (((0,), (0,)), ((), ())), preferred_element_type=f32)


def reverse_rows(flip, block):
    half = SEQ // 2
    return jnp.concatenate(
        [dot_nn(flip, block[half:]).astype(bf16), dot_nn(flip, block[:half]).astype(bf16)], axis=0
    )


def flip_matrix():
    half = SEQ // 2
    rows = lax.broadcasted_iota(jnp.int32, (half, half), 0)
    cols = lax.broadcasted_iota(jnp.int32, (half, half), 1)
    return jnp.where(rows + cols == half - 1, 1.0, 0.0).astype(bf16)


def skew(rows, base):
    return pltpu.roll(rows, base % SEQ, 1, stride=1, stride_axis=0)


def lane_tiles(block):
    return [block[:, t * CHUNK : (t + 1) * CHUNK] for t in range(SEQ // CHUNK)]


def clip_edges(moved, table, c, below):
    tiles = lane_tiles(moved)
    left = jnp.broadcast_to(table[:, :1], (CHUNK, CHUNK))
    right = jnp.broadcast_to(table[:, SEQ - 1 :], (CHUNK, CHUNK))
    if c == 0:
        tiles[2], tiles[3] = jnp.where(below, tiles[2], right), right
    elif c == 1:
        tiles[3] = jnp.where(below, tiles[3], right)
    elif c == 2:
        tiles[0] = jnp.where(below, left, tiles[0])
    else:
        tiles[0], tiles[1] = left, jnp.where(below, left, tiles[1])
    return jnp.concatenate(tiles, axis=1)


def fold_edges(moved, c, below):
    tiles = lane_tiles(moved)
    part = (2, 3, 0, 1)[c]
    zero = jnp.zeros_like(tiles[part])
    upper = c < 2
    if upper:
        outside, tiles[part] = jnp.where(below, zero, tiles[part]), jnp.where(below, tiles[part], zero)
    else:
        outside, tiles[part] = jnp.where(below, tiles[part], zero), jnp.where(below, zero, tiles[part])
    outside = [outside]
    if c in (0, 3):
        whole = 3 if c == 0 else 0
        outside.append(tiles[whole])
        tiles[whole] = zero
    edge, lane = (0, 0) if upper else (3, CHUNK - 1)
    outside = jnp.concatenate(outside, axis=1)
    lanes = lax.broadcasted_iota(jnp.int32, (outside.shape[1], CHUNK), 1)
    to_lane = jnp.where(lanes == lane, 1.0, 0.0).astype(bf16)
    tiles[edge] = tiles[edge] + dot_nn(outside, to_lane).astype(bf16)
    return jnp.concatenate(tiles, axis=1)


def weave(first, second):
    waiting = {0: [], 1: []}

    def emit(which, piece):
        store = piece() if piece is not None else None
        if store is not None:
            waiting[which].append(store)
        keep = DELAYS[which] if piece is not None else 0
        while len(waiting[which]) > keep:
            waiting[which].pop(0)()

    total = max(len(first), len(second))
    done = [0, 0]
    for step in range(1, total + 1):
        for which, pieces in ((1, second), (0, first)):
            while done[which] * total < step * len(pieces):
                emit(which, pieces[done[which]])
                done[which] += 1
    for which in (1, 0):
        emit(which, None)


def storing(ref, where, value):
    def store():
        ref[where] = value

    return store


def attend_kernel(
    len_ref, q_ref, k_ref, v_ref, pq_ref, pk_ref, ctx_ref, wide_ref, probs_ref, scale_ref,
    kp_a, kp_b, qp_a, qp_b, raw_a, raw_b, back_a, back_b, low_a, low_b,
):
    kp, qp, raw, back, low = (kp_a, kp_b), (qp_a, qp_b), (raw_a, raw_b), (back_a, back_b), (low_a, low_b)
    flip = flip_matrix()
    half = SEQ // 2
    lane_pair = lax.broadcasted_iota(jnp.int32, (1, PAIR), 1)
    rows = lax.broadcasted_iota(jnp.int32, (CHUNK, CHUNK), 0)
    cols = lax.broadcasted_iota(jnp.int32, (CHUNK, CHUNK), 1)
    strictly_below, below = cols < rows, cols <= rows
    places = lax.broadcasted_iota(jnp.int32, (1, SEQ), 1)
    pq_all = pq_ref[...]
    pk_flipped = reverse_rows(flip, pk_ref[...])
    units = [(seq, head) for seq in range(MICRO) for head in range(2)]
    heads = [
        (lane_pair >= head * HEAD) & (lane_pair < (head + 1) * HEAD) for head in range(2)
    ]
    hidden_keys = [jnp.where(places < len_ref[seq], 0.0, -1e30) for seq in range(MICRO)]

    def products(u):
        seq, head = units[u]
        slot = u % 2
        tokens = slice(seq * SEQ, (seq + 1) * SEQ)
        pieces = []
        for part in (slice(0, half), slice(half, SEQ)):
            def key_places(part=part):
                k_all = k_ref[tokens, :]
                k_head = jnp.where(heads[head], k_all, jnp.zeros_like(k_all))
                return storing(kp[slot], (slice(None), part), dot_nt(k_head, pq_all[part]).astype(bf16))

            def query_places(part=part):
                q_all = q_ref[tokens, :]
                q_head = jnp.where(heads[head], q_all, jnp.zeros_like(q_all))
                return storing(qp[slot], (slice(None), part), dot_nt(q_head, pk_flipped[part]).astype(bf16))

            def content(part=part):
                q_all = q_ref[tokens, :]
                q_head = jnp.where(heads[head], q_all, jnp.zeros_like(q_all))
                keys = slice(seq * SEQ + part.start, seq * SEQ + part.stop)
                return storing(raw[slot], (slice(None), part), dot_nt(q_head, k_ref[keys, :]))

            pieces += [key_places, query_places, content]
        return pieces

    def softmax(u):
        seq, head = units[u]
        slot = u % 2
        pieces = []
        for c in range(SEQ // CHUNK):
            def turn(c=c):
                part = slice(c * CHUNK, (c + 1) * CHUNK)
                table = kp[slot][part, :]
                moved = clip_edges(skew(table, c * CHUNK + 256), table, c, strictly_below)
                return storing(back[slot], (slice(None), part), moved.T)

            pieces.append(turn)
        for c in range(SEQ // CHUNK):
            def shift(c=c):
                part = slice(c * CHUNK, (c + 1) * CHUNK)
                table = qp[slot][part, :]
                return storing(
                    qp[slot], (part, slice(None)),
                    clip_edges(skew(table, c * CHUNK - 255), table, c, below),
                )

            pieces.append(shift)
        pieces.append(None)

        def normal(here):
            scores = (
                raw[slot][here, :]
                + (qp[slot][here, :].astype(f32) + back[slot][here, :].astype(f32))
                + hidden_keys[seq]
            )
            row_max = jnp.max(scores, axis=1, keepdims=True)
            exp_scores = jnp.exp2((scores - row_max) * (SCALE * LOG2E))
            return storing(low[slot], (here, slice(None)), exp_scores.astype(bf16))

        for start in range(0, SEQ, ROWS):
            pieces.append(functools.partial(normal, slice(start, start + ROWS)))
        return pieces

    def results(u):
        seq, head = units[u]
        slot = u % 2
        tokens = slice(seq * SEQ, (seq + 1) * SEQ)

        def context():
            v_all = v_ref[tokens, :]
            both = dot_nn(low[slot][...], jnp.concatenate([v_all, jnp.ones_like(v_all)], axis=1))
            scale = 1.0 / both[:, PAIR:]
            scale_ref[seq, head] = scale
            ctx = both[:, :PAIR] * scale
            if head == 1:
                ctx = jnp.where(heads[head], ctx, wide_ref[tokens, :])
                ctx_ref[tokens, :] = ctx.astype(bf16)
            wide_ref[tokens, :] = ctx

        def left():
            probs_ref[seq, head, :, :half] = dot_nn(low[slot][:, half:], flip).astype(bf16)

        def right():
            probs_ref[seq, head, :, half:] = dot_nn(low[slot][:, :half], flip).astype(bf16)

        return [context, left, right]

    count = len(units)
    for step in range(count + 2):
        matrix = products(step) if step < count else []
        if step >= 2:
            matrix = results(step - 2) + matrix
        vector = softmax(step - 1) if 1 <= step <= count else []
        weave(matrix, vector)


def attend(lengths, qkv, pos):
    qkv_block = lambda which: pl.BlockSpec((MICRO * SEQ, PAIR), lambda p, n: (0, which * PAIRS + p))
    pos_block = lambda which: pl.BlockSpec((SEQ, PAIR), lambda p, n: (0, which * PAIRS + p))
    square = lambda kind: [pltpu.VMEM((SEQ, SEQ), kind)] * 2
    return pl.pallas_call(
        attend_kernel,
        grid_spec=pltpu.PrefetchScalarGridSpec(
            num_scalar_prefetch=1,
            grid=(PAIRS,),
            in_specs=[qkv_block(0), qkv_block(1), qkv_block(2), pos_block(0), pos_block(1)],
            out_specs=[
                pl.BlockSpec((MICRO * SEQ, PAIR), lambda p, n: (0, p)),
                pl.BlockSpec((MICRO * SEQ, PAIR), lambda p, n: (0, p)),
                pl.BlockSpec((MICRO, 2, SEQ, SEQ), lambda p, n: (0, p, 0, 0)),
                pl.BlockSpec((MICRO, 2, SEQ, CHUNK), lambda p, n: (0, p, 0, 0)),
            ],
            scratch_shapes=square(bf16) + square(bf16) + square(f32) + square(bf16) + square(bf16),
        ),
        out_shape=[
            jax.ShapeDtypeStruct((MICRO * SEQ, D), bf16),
            jax.ShapeDtypeStruct((MICRO * SEQ, D), f32),
            jax.ShapeDtypeStruct((MICRO, HEADS, SEQ, SEQ), bf16),
            jax.ShapeDtypeStruct((MICRO, HEADS, SEQ, CHUNK), f32),
        ],
        compiler_params=pltpu.CompilerParams(vmem_limit_bytes=40 * 2**20),
        cost_estimate=pl.CostEstimate(
            flops=24 * 8 * 2 * SEQ * SEQ * PAIR,
            bytes_accessed=20 * 2**20,
            transcendentals=24 * SEQ * SEQ,
        ),
        name="attend",
    )(lengths, qkv, qkv, qkv, pos, pos)


def attend_back_kernel(
    earlier, q_ref, k_ref, v_ref, pq_ref, pk_ref, gc_ref, ctx_ref, probs_ref, scale_ref, *refs
):
    (
    gq_ref, gk_ref, gv_ref, gpq_ref, gpk_ref,
    raw_a, raw_b, grad_a, grad_b, moved_a, moved_b, turned_a, turned_b,
    inner_a, inner_b, q_t, k_t, gc_t, pq_t, pk_t, k_rev, v_rev, gq_t, gk_t, gv_t,
    ) = refs[earlier:]
    raw, grad, moved, turned = (raw_a, raw_b), (grad_a, grad_b), (moved_a, moved_b), (turned_a, turned_b)
    inner = (inner_a, inner_b)
    flip = flip_matrix()
    half = SEQ // 2
    lane_pair = lax.broadcasted_iota(jnp.int32, (1, PAIR), 1)
    rows = lax.broadcasted_iota(jnp.int32, (CHUNK, CHUNK), 0)
    cols = lax.broadcasted_iota(jnp.int32, (CHUNK, CHUNK), 1)
    below = cols <= rows
    units = [(seq, head) for seq in range(MICRO) for head in range(2)]
    heads = [
        (lane_pair >= head * HEAD) & (lane_pair < (head + 1) * HEAD) for head in range(2)
    ]
    tokens = [slice(seq * SEQ, (seq + 1) * SEQ) for seq in range(MICRO)]
    pq_t[...] = pq_ref[...].T
    pk_t[...] = pk_ref[...].T

    def prepare(seq):
        v_rev[seq] = reverse_rows(flip, v_ref[tokens[seq], :])
        k_flipped = reverse_rows(flip, k_ref[tokens[seq], :])
        k_t[seq] = k_flipped.T
        q_t[seq] = q_ref[tokens[seq], :].T
        scale = jnp.where(heads[0], scale_ref[seq, 0], scale_ref[seq, 1])
        gc_t[seq] = (gc_ref[tokens[seq], :].astype(f32) * scale).astype(bf16).T

    def grads(u):
        seq, head = units[u]
        slot = u % 2
        pieces = []

        def start():
            if head == 0:
                prepare(seq)
            product = gc_ref[tokens[seq], :].astype(f32) * ctx_ref[tokens[seq], :]
            product = jnp.where(heads[head], product, 0.0)
            inner[slot][...] = jnp.broadcast_to(
                jnp.sum(product, axis=1, keepdims=True), (SEQ, CHUNK)
            )

        pieces.append(start)
        for part in (slice(0, half), slice(half, SEQ)):
            def values(part=part):
                gc_all = gc_ref[tokens[seq], :]
                gc_head = jnp.where(heads[head], gc_all, jnp.zeros_like(gc_all))
                return storing(raw[slot], (slice(None), part), dot_nt(gc_head, v_rev[seq, part, :]))

            pieces.append(values)
        pieces.append(None)
        for c in range(SEQ // CHUNK):
            for r in range(0, CHUNK, ROWS):
                def softmax(here=slice(c * CHUNK + r, c * CHUNK + r + ROWS)):
                    low, scale = inner[slot][here, :], scale_ref[seq, head, here, :]
                    tiles = [
                        (
                            probs_ref[seq, head, here, t : t + CHUNK].astype(f32)
                            * ((raw[slot][here, t : t + CHUNK] - low) * scale)
                        ).astype(bf16)
                        for t in range(0, SEQ, CHUNK)
                    ]
                    return storing(grad[slot], (here, slice(None)), jnp.concatenate(tiles, axis=1))

                pieces.append(softmax)
        pieces.append(None)

        def shift(c):
            part = slice(c * CHUNK, (c + 1) * CHUNK)
            table = fold_edges(skew(grad[slot][part, :], c * CHUNK - 255), c, below)
            return storing(moved[slot], (part, slice(None)), table)

        def turn(c):
            part = slice(c * CHUNK, (c + 1) * CHUNK)
            table = fold_edges(skew(grad[slot][:, part].T, c * CHUNK - 255), c, below)
            return storing(turned[slot], (part, slice(None)), table)

        for c in range(SEQ // CHUNK):
            pieces += [functools.partial(turn, c), functools.partial(shift, c)]
        return pieces

    def results(u):
        seq, head = units[u]
        slot = u % 2
        mine = slice(head * HEAD, (head + 1) * HEAD)

        def values():
            gv_t[seq, mine, :] = dot_nn(gc_t[seq, mine, :], probs_ref[seq, head]).astype(bf16)

        def keys():
            total = dot_nn(q_t[seq, mine, :], grad[slot][...])
            total = total + dot_nt(pq_t[mine, :], turned[slot][...])
            gk_t[seq, mine, :] = (total * SCALE).astype(bf16)

        def queries():
            total = dot_nt(k_t[seq, mine, :], grad[slot][...])
            total = total + dot_nt(pk_t[mine, :], moved[slot][...])
            gq_t[seq, mine, :] = (total * SCALE).astype(bf16)

        def key_places():
            total = dot_nn(q_t[seq, mine, :], moved[slot][...]) * SCALE
            gpk_ref[mine, :] = total if seq == 0 else gpk_ref[mine, :] + total

        def query_places():
            total = dot_nn(k_t[seq, mine, :], turned[slot][...]) * SCALE
            gpq_ref[mine, :] = total if seq == 0 else gpq_ref[mine, :] + total

        def finish():
            gq_ref[tokens[seq], :] = gq_t[seq].T
            for kept, out in ((gk_t, gk_ref), (gv_t, gv_ref)):
                out[tokens[seq], :] = jnp.concatenate(
                    [
                        dot_nn(kept[seq, :, half:], flip).astype(bf16),
                        dot_nn(kept[seq, :, :half], flip).astype(bf16),
                    ],
                    axis=1,
                ).T

        pieces = [values, keys, queries, key_places, query_places]
        return pieces + [finish] if head == 1 else pieces

    count = len(units)
    for step in range(count + 1):
        matrix = results(step - 1) if step >= 1 else []
        vector = grads(step) if step < count else []
        weave(matrix, vector)


def attend_back(first, count, earlier, qkv, pos, grad_context, context_wide, probs, scale):
    qkv_block = lambda which: pl.BlockSpec((MICRO * SEQ, PAIR), lambda p: (0, which * PAIRS + first + p))
    pos_block = lambda which: pl.BlockSpec((SEQ, PAIR), lambda p: (0, which * PAIRS + first + p))
    token_block = pl.BlockSpec((MICRO * SEQ, PAIR), lambda p: (0, first + p))
    table_block = pl.BlockSpec((PAIR, SEQ), lambda p: (first + p, 0))
    token_shape = jax.ShapeDtypeStruct((MICRO * SEQ, D), bf16)
    table_shape = jax.ShapeDtypeStruct((D, SEQ), f32)
    square = lambda kind: [pltpu.VMEM((SEQ, SEQ), kind)] * 2
    wide = pltpu.VMEM((MICRO, PAIR, SEQ), bf16)
    tall = pltpu.VMEM((MICRO, SEQ, PAIR), bf16)
    return pl.pallas_call(
        functools.partial(attend_back_kernel, len(earlier)),
        grid=(count,),
        input_output_aliases={9 + i: i for i in range(len(earlier))},
        in_specs=[
            qkv_block(0), qkv_block(1), qkv_block(2), pos_block(0), pos_block(1),
            token_block, token_block,
            pl.BlockSpec((MICRO, 2, SEQ, SEQ), lambda p: (0, first + p, 0, 0)),
            pl.BlockSpec((MICRO, 2, SEQ, CHUNK), lambda p: (0, first + p, 0, 0)),
        ]
        + [pl.BlockSpec(memory_space=pl.ANY)] * len(earlier),
        out_specs=[token_block, token_block, token_block, table_block, table_block],
        out_shape=[token_shape, token_shape, token_shape, table_shape, table_shape],
        scratch_shapes=square(f32) + square(bf16) * 3
        + [pltpu.VMEM((SEQ, CHUNK), f32)] * 2
        + [wide, wide, wide, pltpu.VMEM((PAIR, SEQ), bf16), pltpu.VMEM((PAIR, SEQ), bf16)]
        + [tall, tall, wide, wide, wide],
        compiler_params=pltpu.CompilerParams(vmem_limit_bytes=56 * 2**20),
        cost_estimate=pl.CostEstimate(
            flops=count * 4 * 16 * 2 * SEQ * SEQ * PAIR, bytes_accessed=count * 4 * 2**20, transcendentals=0
        ),
        name="attend_back",
    )(qkv, qkv, qkv, pos, pos, grad_context, context_wide, probs, scale, *earlier)


def weigh_kernel(
    low_ref, x_ref, gq_ref, gk_ref, gv_ref, rel_ref, gpq_ref, gpk_ref, wq_ref, wk_ref,
    vec_ref, up_bias_ref,
    first_keep, first_send, second_keep, second_send, x_turned, rel_sum, rows_ref,
):
    step = pl.program_id(0)
    width = gq_ref.shape[1]
    count, rows = first_keep.shape[0], first_keep.shape[1]

    def put(keep, send, columns, value):
        value = value.astype(bf16).reshape(count, 2, rows, value.shape[1])
        lower, upper = value[:, 0], value[:, 1]
        is_upper = low_ref[0] == 1
        keep[:, :, columns] = jnp.where(is_upper, upper, lower)
        send[:, :, columns] = jnp.where(is_upper, lower, upper)

    def columns_at(start):
        return pl.ds(pl.multiple_of(start, width), width)

    @pl.when(step == 0)
    def begin():
        x_turned[...] = x_ref[...].T
        rel_sum[...] = jnp.zeros_like(rel_sum)
        rows_ref[...] = jnp.zeros_like(rows_ref)
        rows_ref[8:14, :] = vec_ref[...]
        rows_ref[14:18, :] = up_bias_ref[...]

    token_ones = jnp.ones((8, MICRO * SEQ), bf16)
    place_ones = jnp.ones((8, SEQ), bf16)
    row = lax.broadcasted_iota(jnp.int32, (8, width), 0)
    biases = jnp.zeros((8, width), f32)
    tables = ((gq_ref, gpq_ref, wq_ref), (gk_ref, gpk_ref, wk_ref))
    for which, (grad_ref, table_ref, weight_ref) in enumerate(tables):
        grad = grad_ref[...]
        table = table_ref[...].astype(bf16)
        total = dot_nn(x_turned[...], grad) + dot_nt(rel_ref[...], table)
        put(first_keep, first_send, columns_at(which * D + step * width), total)
        rel_sum[...] += dot_nn(weight_ref[...], table)
        bias = dot_nn(token_ones, grad) + dot_nt(place_ones, table)
        biases = jnp.where(row == which, bias, biases)
    grad = gv_ref[...]
    put(second_keep, second_send, columns_at(step * width), dot_nn(x_turned[...], grad))
    rows_ref[:8, columns_at(step * width)] = jnp.where(row == 2, dot_nn(token_ones, grad), biases)

    @pl.when(step == pl.num_programs(0) - 1)
    def end():
        put(second_keep, second_send, slice(D, D + SEQ), rel_sum[...])
        put(second_keep, second_send, slice(D + SEQ, D + SEQ + CHUNK), rows_ref[...].T)


def weigh(x, gq, gk, gv, gpq, gpk, first_pack, vectors):
    steps = 3
    width = D // steps
    whole = lambda shape: pl.BlockSpec(shape, lambda p, n: (0,) * len(shape))
    columns = lambda rows, skip=0: pl.BlockSpec((rows, width), lambda p, n: (0, skip // width + p))
    tokens = MICRO * SEQ
    size = lax.axis_size("wide")
    shapes = [(size // 2, D // size, cols) for cols in (2 * D, 2 * D, D + SEQ + CHUNK, D + SEQ + CHUNK)]
    return pl.pallas_call(
        weigh_kernel,
        grid_spec=pltpu.PrefetchScalarGridSpec(
            num_scalar_prefetch=1,
            grid=(steps,),
            in_specs=[
                whole((tokens, D)), columns(tokens), columns(tokens), columns(tokens),
                whole((D, SEQ)),
                pl.BlockSpec((width, SEQ), lambda p, n: (p, 0)),
                pl.BlockSpec((width, SEQ), lambda p, n: (p, 0)),
                columns(D, SEQ), columns(D, SEQ + D),
            ]
            + [whole((6, D)), whole((4, D))],
            out_specs=[whole(shape) for shape in shapes],
            scratch_shapes=[
                pltpu.VMEM((D, tokens), bf16), pltpu.VMEM((D, SEQ), f32), pltpu.VMEM((CHUNK, D), f32),
            ],
        ),
        out_shape=[jax.ShapeDtypeStruct(shape, bf16) for shape in shapes],
        compiler_params=pltpu.CompilerParams(vmem_limit_bytes=56 * 2**20),
        cost_estimate=pl.CostEstimate(
            flops=2 * D * D * (3 * tokens + 4 * SEQ), bytes_accessed=20 * 2**20, transcendentals=0
        ),
        name="weigh",
    )(my_bit(0).reshape(1), x, gq, gk, gv, first_pack, gpq, gpk, first_pack, first_pack, *vectors)


def feed_back_kernel(
    grad_ref, hidden_ref, slope_ref, down_ref, up_ref,
    grad_hidden_ref, grad_weight_ref, bias_ref, hidden_turned, grad_up,
):
    step = pl.program_id(0)

    @pl.when(step == 0)
    def begin():
        hidden_turned[...] = hidden_ref[...].T
        grad_hidden_ref[...] = jnp.zeros_like(grad_hidden_ref)

    for seq in range(MICRO):
        part = slice(seq * SEQ, (seq + 1) * SEQ)
        grad_act = dot_nt(grad_ref[part, :], down_ref[...])
        grad_up[part, :] = (grad_act * slope_ref[part, :].astype(f32)).astype(bf16)
    for seq in range(MICRO):
        part = slice(seq * SEQ, (seq + 1) * SEQ)
        grad_hidden_ref[part, :] += dot_nt(grad_up[part, :], up_ref[...])
    grad_weight_ref[...] = dot_nn(hidden_turned[...], grad_up[...]).astype(bf16)
    bias_ref[...] = dot_nn(jnp.ones((8, MICRO * SEQ), bf16), grad_up[...])


def feed_back(grad_feed, hidden_low, slope, down_full, second_pack):
    tokens = MICRO * SEQ
    blocks = slope.shape[1] // D
    whole = lambda shape: pl.BlockSpec(shape, lambda f: (0, 0))
    return pl.pallas_call(
        feed_back_kernel,
        grid=(blocks,),
        in_specs=[
            whole((tokens, D)), whole((tokens, D)),
            pl.BlockSpec((tokens, D), lambda f: (0, f)),
            pl.BlockSpec((D, D), lambda f: (f, 0)),
            pl.BlockSpec((D, D), lambda f: (0, 1 + f)),
        ],
        out_specs=[
            whole((tokens, D)),
            pl.BlockSpec((D, D), lambda f: (0, 1 + f)),
            pl.BlockSpec((8, D), lambda f: (0, f)),
        ],
        out_shape=[
            jax.ShapeDtypeStruct((tokens, D), f32),
            jax.ShapeDtypeStruct((D, (1 + blocks) * D), bf16),
            jax.ShapeDtypeStruct((8, blocks * D), f32),
        ],
        scratch_shapes=[pltpu.VMEM((D, tokens), bf16), pltpu.VMEM((tokens, D), bf16)],
        compiler_params=pltpu.CompilerParams(vmem_limit_bytes=56 * 2**20),
        cost_estimate=pl.CostEstimate(
            flops=6 * tokens * D * blocks * D, bytes_accessed=30 * 2**20, transcendentals=0
        ),
        name="feed_back",
    )(grad_feed, hidden_low, slope, down_full, second_pack)


def normalise(v):
    row_mean = jnp.mean(v, axis=-1, keepdims=True)
    centered = v - row_mean
    variance = jnp.mean(centered * centered, axis=-1, keepdims=True)
    rstd = lax.rsqrt(variance + norm_epsilon)
    return centered * rstd, rstd


def column_sums(values):
    return jnp.sum(values, axis=0)


def norm_back(normed, rstd, gain, grad):
    e = grad * gain
    grad_in = rstd * (
        e
        - jnp.mean(e, axis=-1, keepdims=True)
        - normed * jnp.mean(e * normed, axis=-1, keepdims=True)
    )
    return grad_in, column_sums(grad * normed), column_sums(grad)


def far_first(size):
    return sorted(range(size), key=lambda shift: -min(shift, size - shift))


def narrow_shifts(block, shift):
    size = lax.axis_size("narrow")
    return lax.ppermute(block, "narrow", [(i, (i + shift) % size) for i in range(size)])


def gather_rows(shard):
    size = lax.axis_size("narrow")
    me = lax.axis_index("narrow")
    rows, cols = shard.shape
    together = jnp.zeros((size * rows, cols), shard.dtype)
    for shift in far_first(size):
        block = narrow_shifts(shard, shift) if shift else shard
        owner = lax.rem(me - shift + size, size)
        together = lax.dynamic_update_slice(together, block, (owner * rows, 0))
    return lax.all_gather(together, "wide", axis=0, tiled=True)


def scatter_wide(full):
    return lax.psum_scatter(full, "wide", scatter_dimension=0, tiled=True)


def scatter_narrow_start(part):
    size = lax.axis_size("narrow")
    me = lax.axis_index("narrow")
    rows = part.shape[-2] // size
    pieces = []
    for shift in far_first(size):
        target = lax.rem(me + shift, size)
        block = lax.dynamic_slice_in_dim(part, target * rows, rows, part.ndim - 2)
        pieces.append(narrow_shifts(block, shift) if shift else block)
    return pieces


def scatter_narrow(part):
    return sum(piece.astype(f32) for piece in scatter_narrow_start(part))


def swap(block, bit):
    size = lax.axis_size("wide")
    return lax.ppermute(block, "wide", [(i, i ^ (1 << bit)) for i in range(size)])


def my_bit(bit):
    return lax.rem(lax.axis_index("wide") // (1 << bit), 2)


def wide_bits():
    return (lax.axis_size("wide") - 1).bit_length()


def split_bits(full):
    bits = wide_bits()
    return full.reshape((2,) * bits + (full.shape[0] >> bits, full.shape[1]))


def add_low(first, second):
    return (first.astype(f32) + second.astype(f32)).astype(bf16)


def two_halves(part, bit, left):
    axis, mine = left.index(bit), my_bit(bit)
    keep = lax.dynamic_index_in_dim(part, mine, axis, keepdims=False)
    send = lax.dynamic_index_in_dim(part, 1 - mine, axis, keepdims=False)
    left.remove(bit)
    return keep, send


def scatter_upper(part):
    size = lax.axis_size("wide")
    groups = [list(range(low, size, 2)) for low in range(2)]
    part = part.reshape(-1, part.shape[-1])
    return lax.psum_scatter(part, "wide", scatter_dimension=0, tiled=True, axis_index_groups=groups)


def halve(part, bit, left):
    keep, send = two_halves(part, bit, left)
    return add_low(keep, swap(send, bit))


def all_bits():
    return list(range(wide_bits()))[::-1]


def body(
    hidden_in, cotangent, seq_lengths,
    query_weight, query_bias, key_weight, key_bias, value_weight, value_bias,
    out_weight, out_bias, first_gain, first_shift, up_weight, up_bias,
    down_weight, down_bias, second_gain, second_shift, rel_table,
):
    tokens = MICRO * SEQ
    x = hidden_in.reshape(tokens, D)
    cot = cotangent.reshape(tokens, D).astype(f32)
    lengths = seq_lengths.reshape(MICRO)
    share = query_weight.shape[0]
    vectors = [
        query_bias, key_bias, value_bias, out_bias, first_gain, first_shift,
        down_bias, second_gain, second_shift,
    ]
    vectors += [up_bias[c * share : (c + 1) * share] for c in range(4)]
    places = lax.broadcasted_iota(jnp.int32, (VECTORS, share), 0)
    stacked = jnp.zeros((VECTORS, share), bf16)
    for place, vector in enumerate(vectors):
        stacked = jnp.where(places == place, vector[None, :], stacked)
    first_pack = gather_rows(
        jnp.concatenate(
            [rel_table.T, query_weight, key_weight, value_weight, stacked.T], axis=1
        )
    )
    second_pack = gather_rows(jnp.concatenate([out_weight, up_weight], axis=1))
    down_full = gather_rows(down_weight)
    qkv_weight = first_pack[:, SEQ : SEQ + 3 * D]
    rel_turned = first_pack[:, :SEQ]
    out_full = second_pack[:, :D]
    up_full = second_pack[:, D:]
    vector_rows = first_pack[:, SEQ + 3 * D :].T.astype(f32)
    qkv_bias = vector_rows[:3].reshape(3 * D)
    out_b, gain_1, shift_1, down_b, gain_2, shift_2 = (vector_rows[i] for i in range(3, 9))
    up_b = jnp.transpose(vector_rows[9:13].reshape(4, D // share, share), (1, 0, 2)).reshape(4 * D)

    qkv = (dot_nn(x, qkv_weight) + qkv_bias).astype(bf16)
    pos = (dot_tn(rel_turned, qkv_weight[:, : 2 * D]) + qkv_bias[: 2 * D]).astype(bf16)
    context, context_wide, probs, probs_scale = attend(lengths, qkv, pos)

    first_in = x.astype(f32) + dot_nn(context, out_full) + out_b
    normed_1, rstd_1 = normalise(first_in)
    hidden = normed_1 * gain_1 + shift_1
    hidden_low = hidden.astype(bf16)
    upward = dot_nn(hidden_low, up_full) + up_b
    cdf = 0.5 * (1.0 + lax.erf(upward * math.sqrt(0.5)))
    activated_low = (upward * cdf).astype(bf16)
    slope = (cdf + upward * jnp.exp(-0.5 * upward * upward) * (1 / math.sqrt(2 * math.pi))).astype(
        bf16
    )
    second_in = hidden + dot_nn(activated_low, down_full) + down_b
    normed_2, rstd_2 = normalise(second_in)
    hidden_out = (normed_2 * gain_2 + shift_2).astype(bf16)

    grad_second, grad_gain_2, grad_shift_2 = norm_back(normed_2, rstd_2, gain_2, cot)
    grad_feed = grad_second.astype(bf16)
    grad_down_bias = column_sums(grad_feed.astype(f32))
    grad_down = dot_tn(activated_low, grad_feed).astype(bf16)
    grad_hidden, grad_second_pack, grad_up_bias = feed_back(
        grad_feed, hidden_low, slope, down_full, second_pack
    )
    grad_up_bias = grad_up_bias[0]
    grad_hidden = grad_second + grad_hidden
    grad_first, grad_gain_1, grad_shift_1 = norm_back(normed_1, rstd_1, gain_1, grad_hidden)
    grad_branch = grad_first.astype(bf16)
    grad_out_bias = column_sums(grad_branch.astype(f32))
    grad_out = dot_tn(context, grad_branch).astype(bf16)
    grad_context = dot_nt(grad_branch, out_full).astype(bf16)

    grad_second_pack = lax.dynamic_update_slice(grad_second_pack, grad_out, (0, 0))
    down_part = scatter_wide(grad_down)
    keep, send = two_halves(split_bits(grad_second_pack), 0, all_bits())
    came = swap(send, 0)
    grad_context, keep, send = lax.optimization_barrier((grad_context, keep, send))
    inputs = (qkv, pos, grad_context, context_wide, probs, probs_scale)
    early = list(attend_back(0, EARLY, (), *inputs))
    early[0], keep, came, down_part = lax.optimization_barrier((early[0], keep, came, down_part))
    second_part = scatter_upper(add_low(keep, came))
    down_pieces = scatter_narrow_start(down_part)
    gq, gk, gv, gpq, gpk = attend_back(EARLY, PAIRS - EARLY, early, *inputs)
    grad_up_bias = jnp.transpose(grad_up_bias.reshape(D // share, 4, share), (1, 0, 2))
    vector_grads = jnp.concatenate(
        [grad_out_bias, grad_gain_1, grad_shift_1, grad_down_bias, grad_gain_2, grad_shift_2]
    )
    vector_grads = (vector_grads.reshape(6, D), grad_up_bias.reshape(4, D))
    gq, down_pieces = lax.optimization_barrier((gq, down_pieces))
    down_sum = sum(piece.astype(f32) for piece in down_pieces)
    first_keep, first_send, second_keep, second_send = weigh(
        x, gq, gk, gv, gpq, gpk, first_pack, vector_grads
    )
    first_keep, second_part = lax.optimization_barrier((first_keep, second_part))
    second_pieces = scatter_narrow_start(second_part)
    upper = all_bits()[:-1]
    sides = lambda part: part.reshape((2,) * len(upper) + part.shape[1:])
    halves = [
        [sides(add_low(first_keep, swap(first_send, 0))), all_bits()[:-1], list(upper)],
        [sides(add_low(second_keep, swap(second_send, 0))), all_bits()[:-1], upper[::-1]],
    ]

    def halve_both():
        for entry in halves:
            entry[0] = halve(entry[0], entry[2].pop(0), entry[1])

    def together(*others):
        kept = lax.optimization_barrier((halves[0][0], halves[1][0]) + others)
        halves[0][0], halves[1][0] = kept[:2]
        return kept[2:]

    gq, gk, gv = together(gq, gk, gv)
    grad_inputs = grad_first + dot_nt(jnp.concatenate([gq, gk, gv], axis=1), qkv_weight)
    halve_both()
    grad_inputs, *second_pieces = together(grad_inputs, *second_pieces)
    second_sum = sum(piece.astype(f32) for piece in second_pieces)
    while halves[0][2]:
        halve_both()
    last_sum = scatter_narrow(jnp.concatenate([halves[0][0], halves[1][0]], axis=1))
    turned = last_sum[:, 3 * D :].T
    vec = lambda i: turned[SEQ + i]
    return (
        hidden_out.reshape(hidden_in.shape),
        grad_inputs.reshape(hidden_in.shape),
        last_sum[:, :D], vec(0),
        last_sum[:, D : 2 * D], vec(1),
        last_sum[:, 2 * D : 3 * D], vec(2),
        second_sum[:, :D], vec(8), vec(9), vec(10),
        second_sum[:, D:],
        turned[SEQ + 14 : SEQ + 18].reshape(4 * share),
        down_sum, vec(11), vec(12), vec(13),
        turned[:SEQ],
    )


def solution(mesh):
    tokens = P(None, AXES, None, None)
    rows = P(AXES, None)
    vector = P(AXES)
    weights = (
        rows, vector, rows, vector, rows, vector, rows, vector, vector, vector,
        rows, vector, rows, vector, vector, vector, P(None, AXES),
    )
    return jax.shard_map(
        body,
        mesh=mesh,
        in_specs=(tokens, tokens, P(None, AXES)) + weights,
        out_specs=(tokens, tokens) + weights,
        check_vma=False,
    )
```
